32 devices in a mesh: dp: 8 (over z, y), seq: 4 (over x, core).
Axes of the slice: x: 2, y: 2, z: 4, core: 2. Of those that a mesh axis runs over, the one named last changes fastest.
Arguments:
- queries: bfloat16 [4096, 2560], P(('dp', 'seq')), may hold values from -400 to 400
- key_states: bfloat16 [4096, 2560], P(('dp', 'seq')), may hold values from -400 to 400
- value_states: bfloat16 [4096, 2560], P(('dp', 'seq')), may hold values from -6 to 6
- query_tangent: bfloat16 [4096, 2560], P(('dp', 'seq')), may hold values from -6 to 6
- key_tangent: bfloat16 [4096, 2560], P(('dp', 'seq')), may hold values from -6 to 6
- value_tangent: bfloat16 [4096, 2560], P(('dp', 'seq')), may hold values from -6 to 6
- query_gain: float32 [2560], replicated, may hold values from 0.25 to 1.75
- key_gain: float32 [2560], replicated, may hold values from 0.25 to 1.75
- out_weight: bfloat16 [2560, 5120], P('seq', 'dp'), may hold values from -0.125 to 0.125
Outputs:
- projected: bfloat16 [4096, 5120], P(('dp', 'seq'))
- projected_tangent: bfloat16 [4096, 5120], P(('dp', 'seq'))
The draws below stay inside these ranges and needn't reach their ends.
All inputs are finite; a program needn't handle non-finite values.
Results may differ from the reference program's by a relative error of at most 0.012.
The reference program's roundings to bfloat16 on the way count: a program that leaves them out, or rounds other values in their place, can miss the bound.
Values may be sent and summed in bfloat16 or wider, within the bound.
No kernel may reach another device: no remote copies, remote signals or barrier semaphores. Data moves between devices by JAX's collectives and lax.ppermute only.
A program may use at most 128 MiB of HBM per device.

```python
import math
import jax
import jax.numpy as jnp
from jax import lax

D = 5120
HEADS = 20
HDIM = 128
LEN = 512
CLIPS = 8
TOKENS = 4096
HW = 2560


def scaled_field(key):
    first, second, third = jax.random.split(key, 3)
    values = jnp.clip(jax.random.normal(first, (TOKENS, HW), jnp.float32), -4.0, 4.0)
    row_scale = jnp.exp(jax.random.uniform(second, (TOKENS, 1), jnp.float32) * math.log(10.0))
    column_scale = jnp.exp(jax.random.uniform(third, (1, HW), jnp.float32) * math.log(10.0))
    return values * row_scale * column_scale


def draw_queries(key, part):
    values = scaled_field(jax.random.fold_in(key, 1))
    return values.astype(jnp.bfloat16)


def draw_key_states(key, part):
    values = scaled_field(jax.random.fold_in(key, 2))
    return values.astype(jnp.bfloat16)


def levels(rng, shape, cuts, least, top_value):
    loudness, own = 1.0, jax.random.fold_in(rng, 6)
    for axis_at, blocks in cuts:
        heights = jnp.exp(jax.random.uniform(jax.random.fold_in(own, axis_at), (blocks,), jnp.float32, least / len(cuts), top_value / len(cuts)))
        loudness = loudness * jnp.repeat(heights, shape[axis_at] // blocks).reshape([-1 if axis == axis_at else 1 for axis in range(len(shape))])
    return loudness


def noise(stream_key, shape, deviation, limit, cuts=(), held_as=jnp.bfloat16):
    loudness = levels(stream_key, shape, cuts, -0.22, 0.18) if cuts else 1.0
    entries = jax.random.normal(stream_key, shape, jnp.float32) * deviation * loudness
    return jnp.minimum(jnp.maximum(entries, -limit), limit).astype(held_as)


def setup_inputs(seed: int = 0) -> dict:
    streams_of = jax.random.split(jax.random.key(seed), 10)
    return {
        "queries": draw_queries(jax.random.fold_in(streams_of[9], 71), 0),
        "key_states": draw_key_states(jax.random.fold_in(streams_of[9], 71), 0),
        "value_states": noise(streams_of[2], (TOKENS, HW), 1.0, 6.0, ((0, 32),)),
        "query_tangent": noise(streams_of[3], (TOKENS, HW), 1.0, 6.0, ((0, 32),)),
        "key_tangent": noise(streams_of[4], (TOKENS, HW), 1.0, 6.0, ((0, 32),)),
        "value_tangent": noise(streams_of[5], (TOKENS, HW), 1.0, 6.0, ((0, 32),)),
        "query_gain": jnp.clip(1.0 + 0.15 * jax.random.normal(streams_of[6], (HW,), jnp.float32), 0.25, 1.75),
        "key_gain": jnp.clip(1.0 + 0.15 * jax.random.normal(streams_of[7], (HW,), jnp.float32), 0.25, 1.75),
        "out_weight": noise(streams_of[8], (HW, D), HW ** -0.5, 0.125, ((0, 4), (1, 8))),
    }


def rms_tangent(primal, tangent, gain):
    primal_f = primal.astype(jnp.float32)
    tangent_f = tangent.astype(jnp.float32)
    inverse = lax.rsqrt(lax.optimization_barrier(jnp.mean(primal_f * primal_f, axis=-1, keepdims=True)) + 1e-06)
    across = lax.optimization_barrier(jnp.mean(primal_f * tangent_f, axis=-1, keepdims=True))
    normed = (primal_f * inverse * gain).astype(jnp.bfloat16)
    normed_tangent = (gain * (tangent_f * inverse - primal_f * inverse ** 3 * across)).astype(jnp.bfloat16)
    return (normed, normed_tangent)

def widen(array):
    return array.astype(jnp.float32)

def attend(query_normed, query_dual, key_normed, key_dual, value_plain, value_dual):
    factor = HDIM ** (-0.5)
    scores = jnp.einsum('qhd,khd->hqk', widen(query_normed), widen(key_normed)) * factor
    dual_scores = (jnp.einsum('qhd,khd->hqk', widen(query_dual), widen(key_normed)) + jnp.einsum('qhd,khd->hqk', widen(query_normed), widen(key_dual))) * factor
    peak = lax.optimization_barrier(jnp.max(scores, axis=-1, keepdims=True))
    raised = jnp.exp(scores - peak)
    probs = raised / lax.optimization_barrier(jnp.sum(raised, axis=-1, keepdims=True))
    spread = probs * (dual_scores - lax.optimization_barrier(jnp.sum(probs * dual_scores, axis=-1, keepdims=True)))
    probs_low, spread_low = lax.optimization_barrier((probs.astype(jnp.bfloat16), spread.astype(jnp.bfloat16)))
    attn = jnp.einsum('hqk,khd->qhd', widen(probs_low), widen(value_plain)).astype(jnp.bfloat16)
    dual_attn = (jnp.einsum('hqk,khd->qhd', widen(probs_low), widen(value_dual)) + jnp.einsum('hqk,khd->qhd', widen(spread_low), widen(value_plain))).astype(jnp.bfloat16)
    return (attn, dual_attn)

def reference(queries, key_states, value_states, query_tangent, key_tangent, value_tangent, query_gain, key_gain, out_weight):
    query_normed, query_dual = rms_tangent(queries, query_tangent, query_gain)
    key_normed, key_dual = rms_tangent(key_states, key_tangent, key_gain)
    query_normed, query_dual, key_normed, key_dual = lax.optimization_barrier((query_normed, query_dual, key_normed, key_dual))

    def per_clip(pieces):
        shaped = [array.reshape(LEN, HEADS, HDIM) for array in pieces]
        attn, dual_attn = attend(shaped[0], shaped[1], shaped[2], shaped[3], shaped[4], shaped[5])
        plain_out = jnp.dot(attn.reshape(LEN, HEADS * HDIM), out_weight, preferred_element_type=jnp.float32).astype(jnp.bfloat16)
        dual_out = jnp.dot(dual_attn.reshape(LEN, HEADS * HDIM), out_weight, preferred_element_type=jnp.float32).astype(jnp.bfloat16)
        return (plain_out, dual_out)
    clips = tuple((array.reshape(CLIPS, LEN, HEADS * HDIM) for array in (query_normed, query_dual, key_normed, key_dual, value_states, value_tangent)))
    plain_all, dual_all = lax.map(per_clip, clips)
    return (plain_all.reshape(TOKENS, D), dual_all.reshape(TOKENS, D))
```

```python
import functools

import jax
import jax.numpy as jnp
from jax import lax
from jax.experimental import pallas as pl
from jax.experimental.pallas import tpu as pltpu
from jax.sharding import PartitionSpec as P

HEADS = 20
EPS = 1e-06
VMEM_BYTES = 48 * 1024 * 1024
ROW_STEP = 32

LOW = jnp.bfloat16
WIDE = jnp.float32


def params():
    return pltpu.CompilerParams(vmem_limit_bytes=VMEM_BYTES)


def rms_rows(primal, tangent, gain):
    primal_f = primal.astype(WIDE)
    tangent_f = tangent.astype(WIDE)
    inverse = lax.rsqrt(jnp.mean(primal_f * primal_f, axis=-1, keepdims=True) + EPS)
    across = jnp.mean(primal_f * tangent_f, axis=-1, keepdims=True)
    normed = primal_f * inverse * gain
    dual = gain * (tangent_f * inverse - primal_f * (inverse * inverse * inverse * across))
    return normed.astype(LOW), dual.astype(LOW)


def norm_kernel(primal_ref, tangent_ref, gain_ref, *out_refs):
    normed, dual = rms_rows(primal_ref[...], tangent_ref[...], gain_ref[...])
    width = out_refs[0].shape[-1]
    for at, out_ref in enumerate(out_refs):
        out_ref[0] = normed[:, at * width : (at + 1) * width]
        out_ref[1] = dual[:, at * width : (at + 1) * width]


def norm(primal, tangent, gain, pieces):
    rows, features = primal.shape
    step = min(rows, ROW_STEP)
    width = features // pieces
    row_block = pl.BlockSpec((step, features), lambda i: (i, 0))
    return pl.pallas_call(
        norm_kernel,
        grid=(rows // step,),
        in_specs=[row_block, row_block, pl.BlockSpec((1, features), lambda i: (0, 0))],
        out_specs=[pl.BlockSpec((2, step, width), lambda i: (0, i, 0))] * pieces,
        out_shape=[jax.ShapeDtypeStruct((2, rows, width), LOW)] * pieces,
        compiler_params=params(),
    )(primal, tangent, gain.reshape(1, features))


def attend_kernel(n_blocks, query_ref, *refs):
    key_refs = refs[:n_blocks]
    value_refs = refs[n_blocks : 2 * n_blocks]
    dual_value_refs = refs[2 * n_blocks : 3 * n_blocks]
    out_ref = refs[3 * n_blocks]
    query, query_dual = query_ref[0], query_ref[1]
    factor = query.shape[-1] ** (-0.5)
    key = jnp.concatenate([ref[0] for ref in key_refs], axis=0)
    key_dual = jnp.concatenate([ref[1] for ref in key_refs], axis=0)
    value = jnp.concatenate([ref[...] for ref in value_refs], axis=0)
    value_dual = jnp.concatenate([ref[...] for ref in dual_value_refs], axis=0)
    last = (((1,), (1,)), ((), ()))
    scores = lax.dot_general(query, key, last, preferred_element_type=WIDE) * factor
    dual_scores = (
        lax.dot_general(
            jnp.concatenate([query_dual, query], axis=1),
            jnp.concatenate([key, key_dual], axis=1),
            last,
            preferred_element_type=WIDE,
        )
        * factor
    )
    raised = jnp.exp(scores - jnp.max(scores, axis=-1, keepdims=True))
    probs = raised * (1.0 / jnp.sum(raised, axis=-1, keepdims=True))
    spread = probs * (dual_scores - jnp.sum(probs * dual_scores, axis=-1, keepdims=True))
    probs_low = probs.astype(LOW)
    spread_low = spread.astype(LOW)
    attn = jnp.dot(probs_low, value, preferred_element_type=WIDE)
    dual_attn = jnp.dot(probs_low, value_dual, preferred_element_type=WIDE) + jnp.dot(
        spread_low, value, preferred_element_type=WIDE
    )
    out_ref[0] = attn.astype(LOW)
    out_ref[1] = dual_attn.astype(LOW)


def attend(chunk, chunk_heads, query, keys, values, dual_values):
    n_blocks = len(keys)
    rows, features = query.shape[1:]
    hdim = features // HEADS
    first = chunk * chunk_heads
    whole = pl.BlockSpec((2, rows, hdim), lambda h: (0, 0, first + h))
    part = pl.BlockSpec((2, rows, hdim), lambda h: (0, 0, h))
    flat = pl.BlockSpec((rows, hdim), lambda h: (0, first + h))
    return pl.pallas_call(
        functools.partial(attend_kernel, n_blocks),
        grid=(chunk_heads,),
        in_specs=[whole] + [part] * n_blocks + [flat] * (2 * n_blocks),
        out_specs=part,
        out_shape=jax.ShapeDtypeStruct((2, rows, chunk_heads * hdim), LOW),
        compiler_params=params(),
    )(query, *keys, *values, *dual_values)


def project_kernel(depth_steps, where_ref, acts_ref, first_ref, second_ref, mine_ref, other_ref, acc_ref):
    at = pl.program_id(0)
    kinds, rows, width = acts_ref.shape[1:]
    acts = acts_ref[0].reshape(kinds * rows, width)

    @pl.when(at == 0)
    def _():
        acc_ref[...] = jnp.zeros_like(acc_ref)

    @pl.when(at < depth_steps // 2)
    def _():
        acc_ref[...] += jnp.dot(acts, first_ref[0], preferred_element_type=WIDE)

    @pl.when(at >= depth_steps // 2)
    def _():
        acc_ref[...] += jnp.dot(acts, second_ref[0], preferred_element_type=WIDE)

    @pl.when(at == depth_steps - 1)
    def _():
        total = acc_ref[...].astype(LOW)
        half = kinds // 2
        mine_ref[...] = total[: half * rows].reshape(mine_ref.shape)
        other_ref[...] = total[half * rows :].reshape(other_ref.shape)


def project(order, acts, first, second):
    chunks, kinds, rows, width = acts.shape
    half = chunks // 2
    n = first.shape[-1]
    out = jax.ShapeDtypeStruct((kinds // 2, rows, n), LOW)
    out_spec = pl.BlockSpec((kinds // 2, rows, n), lambda i, w: (0, 0, 0))
    return pl.pallas_call(
        functools.partial(project_kernel, chunks),
        grid_spec=pltpu.PrefetchScalarGridSpec(
            num_scalar_prefetch=1,
            grid=(chunks,),
            in_specs=[
                pl.BlockSpec((1, kinds, rows, width), lambda i, w: (w[i], 0, 0, 0)),
                pl.BlockSpec((1, width, n), lambda i, w: (jnp.minimum(i, half - 1), 0, 0)),
                pl.BlockSpec((1, width, n), lambda i, w: (jnp.maximum(i - half, 0), 0, 0)),
            ],
            out_specs=[out_spec, out_spec],
            scratch_shapes=[pltpu.VMEM((kinds * rows, n), WIDE)],
        ),
        out_shape=[out, out],
        compiler_params=params(),
    )(order, acts, first, second)


def place_kernel(n_pieces, where_ref, *refs):
    piece_refs = refs[:n_pieces]
    plain_ref, dual_ref = refs[n_pieces:]
    n = piece_refs[0].shape[-1]
    for at, piece_ref in enumerate(piece_refs):
        columns = pl.ds(pl.multiple_of(where_ref[at] * n, n), n)
        plain_ref[:, columns] = piece_ref[0]
        dual_ref[:, columns] = piece_ref[1]


def place(where, pieces):
    kinds, rows, n = pieces[0].shape
    width = n * len(pieces)
    if n % 128:
        out = jnp.zeros((kinds, rows, width), LOW)
        for at, piece in enumerate(pieces):
            out = lax.dynamic_update_slice(out, piece, (0, 0, where[at] * n))
        return out[0], out[1]
    out = jax.ShapeDtypeStruct((rows, width), LOW)
    return pl.pallas_call(
        functools.partial(place_kernel, len(pieces)),
        in_specs=[pl.BlockSpec(memory_space=pltpu.SMEM)]
        + [pl.BlockSpec(memory_space=pltpu.VMEM)] * len(pieces),
        out_specs=[pl.BlockSpec(memory_space=pltpu.VMEM)] * 2,
        out_shape=[out, out],
        compiler_params=params(),
    )(where, *pieces)


def body(
    n_dp,
    n_seq,
    queries,
    key_states,
    value_states,
    query_tangent,
    key_tangent,
    value_tangent,
    query_gain,
    key_gain,
    out_weight,
):
    dp = lax.axis_index("dp")
    seq = lax.axis_index("seq")
    n_ring = n_dp // 2
    chunk_heads = HEADS // n_seq

    def far(array):
        return lax.ppermute(array, "seq", [(i, i ^ 2) for i in range(n_seq)])

    def near(array):
        return lax.ppermute(array, "seq", [(i, i ^ 1) for i in range(n_seq)])

    def across(array):
        return lax.ppermute(array, "dp", [(i, i ^ 1) for i in range(n_dp)])

    def onward(array):
        return lax.ppermute(array, "dp", [(i, (i + 2) % n_dp) for i in range(n_dp)])

    def four(array):
        there = far(array)
        return [array, there, near(array), near(there)]

    rings = [jnp.stack([out_weight, far(out_weight)])]
    for _ in range(n_ring - 1):
        rings.append(onward(rings[-1]))
    sides = [near(ring) for ring in rings]

    values = four(value_states)
    dual_values = four(value_tangent)
    keys = [four(piece) for piece in norm(key_states, key_tangent, key_gain, n_seq)]
    (query,) = norm(queries, query_tangent, query_gain, 1)

    acts = []
    for chunk in range(n_seq):
        mine = attend(chunk, chunk_heads, query, keys[chunk], values, dual_values)
        acts.append(jnp.concatenate([mine, across(mine)], axis=0))
    acts = jnp.stack(acts)

    order = jnp.stack([seq, seq ^ 2, seq ^ 1, seq ^ 3])
    pieces, where = [], []
    for step in range(n_ring):
        mine, other = project(order, acts, rings[step], sides[step])
        pair = (dp // 2 - step) % n_ring
        pieces += [mine, across(other)]
        where += [2 * pair + dp % 2, 2 * pair + 1 - dp % 2]
    return place(jnp.stack(where).astype(jnp.int32), pieces)


def solution(mesh):
    rows = P(("dp", "seq"), None)
    return jax.shard_map(
        functools.partial(body, mesh.shape["dp"], mesh.shape["seq"]),
        mesh=mesh,
        in_specs=(rows,) * 6 + (P(), P(), P("seq", "dp")),
        out_specs=(rows, rows),
        check_vma=False,
    )
```

```python
import functools

import jax
import jax.numpy as jnp
from jax import lax
from jax.experimental import pallas as pl
from jax.experimental.pallas import tpu as pltpu
from jax.sharding import PartitionSpec as P

HEADS = 20
EPS = 1e-06
VMEM_BYTES = 48 * 1024 * 1024
ROW_STEP = 32

LOW = jnp.bfloat16
WIDE = jnp.float32


def params():
    return pltpu.CompilerParams(vmem_limit_bytes=VMEM_BYTES)


def rms_rows(primal, tangent, gain):
    primal_f = primal.astype(WIDE)
    tangent_f = tangent.astype(WIDE)
    inverse = lax.rsqrt(jnp.mean(primal_f * primal_f, axis=-1, keepdims=True) + EPS)
    across = jnp.mean(primal_f * tangent_f, axis=-1, keepdims=True)
    normed = primal_f * inverse * gain
    dual = gain * (tangent_f * inverse - primal_f * (inverse * inverse * inverse * across))
    return normed.astype(LOW), dual.astype(LOW)


def norm_kernel(primal_ref, tangent_ref, gain_ref, *out_refs):
    normed, dual = rms_rows(primal_ref[...], tangent_ref[...], gain_ref[...])
    width = out_refs[0].shape[-1]
    for at, out_ref in enumerate(out_refs):
        out_ref[0] = normed[:, at * width : (at + 1) * width]
        out_ref[1] = dual[:, at * width : (at + 1) * width]


def norm(primal, tangent, gain, pieces):
    rows, features = primal.shape
    step = min(rows, ROW_STEP)
    width = features // pieces
    row_block = pl.BlockSpec((step, features), lambda i: (i, 0))
    return pl.pallas_call(
        norm_kernel,
        grid=(rows // step,),
        in_specs=[row_block, row_block, pl.BlockSpec((1, features), lambda i: (0, 0))],
        out_specs=[pl.BlockSpec((2, step, width), lambda i: (0, i, 0))] * pieces,
        out_shape=[jax.ShapeDtypeStruct((2, rows, width), LOW)] * pieces,
        compiler_params=params(),
    )(primal, tangent, gain.reshape(1, features))


def attend_kernel(n_blocks, query_ref, *refs):
    key_refs = refs[:n_blocks]
    value_refs = refs[n_blocks : 2 * n_blocks]
    dual_value_refs = refs[2 * n_blocks : 3 * n_blocks]
    out_ref = refs[3 * n_blocks]
    query, query_dual = query_ref[0], query_ref[1]
    factor = query.shape[-1] ** (-0.5)
    key = jnp.concatenate([ref[0] for ref in key_refs], axis=0)
    key_dual = jnp.concatenate([ref[1] for ref in key_refs], axis=0)
    value = jnp.concatenate([ref[...] for ref in value_refs], axis=0)
    value_dual = jnp.concatenate([ref[...] for ref in dual_value_refs], axis=0)
    last = (((1,), (1,)), ((), ()))
    scores = lax.dot_general(query, key, last, preferred_element_type=WIDE) * factor
    dual_scores = (
        lax.dot_general(
            jnp.concatenate([query_dual, query], axis=1),
            jnp.concatenate([key, key_dual], axis=1),
            last,
            preferred_element_type=WIDE,
        )
        * factor
    )
    raised = jnp.exp(scores - jnp.max(scores, axis=-1, keepdims=True))
    probs = raised * (1.0 / jnp.sum(raised, axis=-1, keepdims=True))
    spread = probs * (dual_scores - jnp.sum(probs * dual_scores, axis=-1, keepdims=True))
    probs_low = probs.astype(LOW)
    spread_low = spread.astype(LOW)
    attn = jnp.dot(probs_low, value, preferred_element_type=WIDE)
    dual_attn = jnp.dot(probs_low, value_dual, preferred_element_type=WIDE) + jnp.dot(
        spread_low, value, preferred_element_type=WIDE
    )
    out_ref[0] = attn.astype(LOW)
    out_ref[1] = dual_attn.astype(LOW)


def attend(chunk, chunk_heads, query, keys, values, dual_values):
    n_blocks = len(keys)
    rows, features = query.shape[1:]
    hdim = features // HEADS
    first = chunk * chunk_heads
    whole = pl.BlockSpec((2, rows, hdim), lambda h: (0, 0, first + h))
    part = pl.BlockSpec((2, rows, hdim), lambda h: (0, 0, h))
    flat = pl.BlockSpec((rows, hdim), lambda h: (0, first + h))
    return pl.pallas_call(
        functools.partial(attend_kernel, n_blocks),
        grid=(chunk_heads,),
        in_specs=[whole] + [part] * n_blocks + [flat] * (2 * n_blocks),
        out_specs=part,
        out_shape=jax.ShapeDtypeStruct((2, rows, chunk_heads * hdim), LOW),
        compiler_params=params(),
    )(query, *keys, *values, *dual_values)


def project_kernel(span, order_ref, acts_ref, *refs):
    weight_refs, (mine_ref, other_ref) = refs[:-2], refs[-2:]
    kinds, rows, width = acts_ref.shape[1:]
    total = 0.0
    for at, weight_ref in enumerate(weight_refs):
        weight = weight_ref[:, span] if weight_ref.shape[1] > span.stop - span.start else weight_ref[...]
        acts = acts_ref[order_ref[at]].reshape(kinds * rows, width)
        total = total + jnp.dot(acts, weight, preferred_element_type=WIDE)
    half = kinds // 2
    low = total.astype(LOW)
    mine_ref[...] = low[: half * rows].reshape(mine_ref.shape)
    other_ref[...] = low[half * rows :].reshape(other_ref.shape)


def project(order, acts, span, *weights):
    chunks, kinds, rows, width = acts.shape
    out = jax.ShapeDtypeStruct((kinds // 2, rows, span.stop - span.start), LOW)
    vmem = pl.BlockSpec(memory_space=pltpu.VMEM)
    return pl.pallas_call(
        functools.partial(project_kernel, span),
        in_specs=[pl.BlockSpec(memory_space=pltpu.SMEM)] + [vmem] * (1 + len(weights)),
        out_specs=[vmem, vmem],
        out_shape=[out, out],
        compiler_params=params(),
    )(order, acts, *weights)


def place_kernel(n_parts, where_ref, *refs):
    part_refs = refs[:-2]
    plain_ref, dual_ref = refs[-2:]
    for first in range(0, len(part_refs), n_parts):
        group = part_refs[first : first + n_parts]
        n = sum(ref.shape[-1] for ref in group)
        start = where_ref[first // n_parts] * n
        for part_ref in group:
            columns = pl.ds(pl.multiple_of(start, 128), part_ref.shape[-1])
            plain_ref[:, columns] = part_ref[0]
            dual_ref[:, columns] = part_ref[1]
            start = start + part_ref.shape[-1]


def place(where, pieces):
    kinds, rows = pieces[0][0].shape[:2]
    n = sum(part.shape[-1] for part in pieces[0])
    width = n * len(pieces)
    if n % 128:
        out = jnp.zeros((kinds, rows, width), LOW)
        for at, piece in enumerate(pieces):
            piece = jnp.concatenate(piece, axis=-1)
            out = lax.dynamic_update_slice(out, piece, (0, 0, where[at] * n))
        return out[0], out[1]
    parts = [part for piece in pieces for part in piece]
    out = jax.ShapeDtypeStruct((rows, width), LOW)
    return pl.pallas_call(
        functools.partial(place_kernel, len(pieces[0])),
        in_specs=[pl.BlockSpec(memory_space=pltpu.SMEM)]
        + [pl.BlockSpec(memory_space=pltpu.VMEM)] * len(parts),
        out_specs=[pl.BlockSpec(memory_space=pltpu.VMEM)] * 2,
        out_shape=[out, out],
        compiler_params=params(),
    )(where, *parts)


def body(
    n_dp,
    n_seq,
    queries,
    key_states,
    value_states,
    query_tangent,
    key_tangent,
    value_tangent,
    query_gain,
    key_gain,
    out_weight,
):
    dp = lax.axis_index("dp")
    seq = lax.axis_index("seq")
    n_ring = n_dp // 2
    chunk_heads = HEADS // n_seq

    def far(array):
        return lax.ppermute(array, "seq", [(i, i ^ 2) for i in range(n_seq)])

    def near(array):
        return lax.ppermute(array, "seq", [(i, i ^ 1) for i in range(n_seq)])

    def across(array):
        return lax.ppermute(array, "dp", [(i, i ^ 1) for i in range(n_dp)])

    def onward(array):
        return lax.ppermute(array, "dp", [(i, (i + 2) % n_dp) for i in range(n_dp)])

    def four(array):
        there = far(array)
        return [array, there, near(array), near(there)]

    n_columns = out_weight.shape[1]
    tile = 128 if n_columns % 128 == 0 else 16
    cut = n_columns // tile * 3 // 5 * tile
    token = jnp.zeros((1,), jnp.int32)

    def after(array):
        return lax.optimization_barrier((array, token))[0]

    def wait(array):
        nonlocal token
        array, token = lax.optimization_barrier((array, token))
        return array

    value_far = far(value_states)
    dual_far = far(value_tangent)
    rows = [out_weight, onward(out_weight)]
    keys = norm(key_states, key_tangent, key_gain, n_seq)
    (query,) = norm(queries, query_tangent, query_gain, 1)
    value_near, dual_near = near(value_states), near(value_tangent)

    value_far = wait(value_far)
    keys_far = [far(after(keys[0]))]
    value_cross = near(value_far)
    rows[1] = wait(rows[1])
    rows.append(onward(after(rows[1])))
    dual_far = wait(dual_far)
    keys_far.append(far(after(keys[1])))
    dual_cross = near(dual_far)
    values = [value_states, value_far, value_near, value_cross]
    dual_values = [value_tangent, dual_far, dual_near, dual_cross]

    acts, swapped = [], []

    def attention(chunk):
        blocks = [keys[chunk], keys_far[chunk], near(keys[chunk]), near(keys_far[chunk])]
        acts.append(wait(attend(chunk, chunk_heads, query, blocks, values, dual_values)))
        swapped.append(across(acts[-1]))
        if chunk:
            swapped[chunk - 1] = wait(swapped[chunk - 1])

    keys_far[0] = wait(keys_far[0])
    keys_far.append(far(after(keys[2])))
    rows[2] = wait(rows[2])
    for step in range(3, n_ring):
        rows.append(onward(after(rows[step - 1])))
    attention(0)
    keys_far[1] = wait(keys_far[1])
    keys_far.append(far(after(keys[3])))
    attention(1)
    keys_far[2] = wait(keys_far[2])
    left = far(after(out_weight[:, :cut]))
    attention(2)
    rows[-1] = wait(rows[-1])
    keys_far[3] = wait(keys_far[3])
    rights = [far(after(out_weight[:, cut:]))]
    attention(3)
    left = wait(left)
    lefts = [left, onward(after(left))]
    rights.append(far(after(rows[1][:, cut:])))
    swapped[-1] = wait(swapped[-1])
    acts = jnp.stack([jnp.concatenate(pair, axis=0) for pair in zip(acts, swapped)])

    order = jnp.stack([seq, seq ^ 2, seq ^ 1, seq ^ 3])
    mine = [[None, None] for _ in range(n_ring)]
    other = [[None, None] for _ in range(n_ring)]
    sent = []

    def columns(step, part):
        span = slice(cut, n_columns) if part else slice(0, cut)
        beside = (rights if part else lefts)[step]
        blocks = [rows[step], beside, near(rows[step]), near(beside)]
        own, out = project(order, acts, span, *blocks)
        mine[step][part] = own
        other[step][part] = across(wait(out))
        sent.append((step, part))
        if len(sent) > 1:
            step, part = sent.pop(0)
            other[step][part] = wait(other[step][part])

    columns(0, 0)
    for step in range(1, n_ring):
        rights[step - 1] = wait(rights[step - 1])
        if step + 1 < n_ring:
            rights.append(far(after(rows[step + 1][:, cut:])))
        columns(step - 1, 1)
        lefts[step] = wait(lefts[step])
        if step + 1 < n_ring:
            lefts.append(onward(after(lefts[step])))
        columns(step, 0)
    rights[-1] = wait(rights[-1])
    columns(n_ring - 1, 1)

    pieces, where = [], []
    for step in range(n_ring):
        pair = (dp // 2 - step) % n_ring
        pieces += [mine[step], other[step]]
        where += [2 * pair + dp % 2, 2 * pair + 1 - dp % 2]
    return place(jnp.stack(where).astype(jnp.int32) + token, pieces)


def solution(mesh):
    rows = P(("dp", "seq"), None)
    return jax.shard_map(
        functools.partial(body, mesh.shape["dp"], mesh.shape["seq"]),
        mesh=mesh,
        in_specs=(rows,) * 6 + (P(), P(), P("seq", "dp")),
        out_specs=(rows, rows),
        check_vma=False,
    )
```

```python
import functools

import jax
import jax.numpy as jnp
from jax import lax
from jax.experimental import pallas as pl
from jax.experimental.pallas import tpu as pltpu
from jax.sharding import PartitionSpec as P

HEADS = 20
EPS = 1e-06
VMEM_BYTES = 48 * 1024 * 1024
ROW_STEP = 32

LOW = jnp.bfloat16
WIDE = jnp.float32


def params():
    return pltpu.CompilerParams(vmem_limit_bytes=VMEM_BYTES)


def vmem_specs(count):
    return [pl.BlockSpec(memory_space=pltpu.VMEM)] * count


def pack_kernel(n_seq, chunks, core_ref, *refs):
    query_ref, key_ref, value_ref, dquery_ref, dkey_ref, dvalue_ref, query_gain_ref, key_gain_ref = refs[:8]
    out_refs = refs[8:]
    n_chunks = len(chunks)
    group = query_ref.shape[-1] // n_seq

    def statistics(primal_ref, tangent_ref):
        primal = primal_ref[...].astype(WIDE)
        tangent = tangent_ref[...].astype(WIDE)
        inverse = lax.rsqrt(jnp.mean(primal * primal, axis=-1, keepdims=True) + EPS)
        across = jnp.mean(primal * tangent, axis=-1, keepdims=True)
        return inverse, inverse * inverse * inverse * across

    query_stats = statistics(query_ref, dquery_ref)
    key_stats = statistics(key_ref, dkey_ref)

    def normed(primal_ref, tangent_ref, gain_ref, stats, lanes):
        primal = primal_ref[:, lanes].astype(WIDE)
        tangent = tangent_ref[:, lanes].astype(WIDE)
        gain = gain_ref[:, lanes]
        inverse, slope = stats
        return (primal * inverse * gain).astype(LOW), (gain * (tangent * inverse - primal * slope)).astype(LOW)

    for side in range(2):
        core = core_ref[0] if side == 0 else 1 - core_ref[0]
        queries_ref, *keyed_refs = out_refs[side * (1 + n_chunks) : (side + 1) * (1 + n_chunks)]
        for at in range(n_seq // 2):
            lanes = pl.ds(pl.multiple_of((2 * at + core) * group, 128), group)
            here = slice(at * group, (at + 1) * group)
            plain, dual = normed(query_ref, dquery_ref, query_gain_ref, query_stats, lanes)
            queries_ref[0, :, here] = plain
            queries_ref[1, :, here] = dual
            four = normed(key_ref, dkey_ref, key_gain_ref, key_stats, lanes)
            four += (value_ref[:, lanes], dvalue_ref[:, lanes])
            start = 0
            for keyed_ref, width in zip(keyed_refs, chunks):
                low, high = max(start, here.start), min(start + width, here.stop)
                if low < high:
                    for which, part in enumerate(four):
                        keyed_ref[which, :, low - start : high - start] = part[:, low - here.start : high - here.start]
                start += width


def pack(core, n_seq, chunks, arrays, gains):
    rows, features = arrays[0].shape
    step = min(rows, ROW_STEP)
    row_block = pl.BlockSpec((step, features), lambda i, c: (i, 0))
    gain_block = pl.BlockSpec((1, features), lambda i, c: (0, 0))
    kinds = [(2, features // 2)] + [(4, width) for width in chunks]
    kinds = kinds + kinds
    return pl.pallas_call(
        functools.partial(pack_kernel, n_seq, chunks),
        grid_spec=pltpu.PrefetchScalarGridSpec(
            num_scalar_prefetch=1,
            grid=(rows // step,),
            in_specs=[row_block] * 6 + [gain_block] * 2,
            out_specs=[pl.BlockSpec((count, step, width), lambda i, c: (0, i, 0)) for count, width in kinds],
        ),
        out_shape=[jax.ShapeDtypeStruct((count, rows, width), LOW) for count, width in kinds],
        compiler_params=params(),
    )(core, *arrays, *[gain.reshape(1, features) for gain in gains])


def attend_kernel(n_queries, *refs):
    query_refs, keyed_refs, out_ref = refs[:n_queries], refs[n_queries:-1], refs[-1]

    def stack(which, some_refs):
        return jnp.concatenate([ref[which] for ref in some_refs], axis=0)

    query, query_dual = (stack(which, query_refs) for which in range(2))
    key, key_dual, value, value_dual = (stack(which, keyed_refs) for which in range(4))
    factor = query.shape[-1] ** (-0.5)
    last = (((1,), (1,)), ((), ()))
    scores = lax.dot_general(query, key, last, preferred_element_type=WIDE) * factor
    dual_scores = (
        lax.dot_general(
            jnp.concatenate([query_dual, query], axis=1),
            jnp.concatenate([key, key_dual], axis=1),
            last,
            preferred_element_type=WIDE,
        )
        * factor
    )
    raised = jnp.exp(scores - jnp.max(scores, axis=-1, keepdims=True))
    probs = raised * (1.0 / jnp.sum(raised, axis=-1, keepdims=True))
    spread = probs * (dual_scores - jnp.sum(probs * dual_scores, axis=-1, keepdims=True))
    probs_low = probs.astype(LOW)
    spread_low = spread.astype(LOW)
    out_ref[0] = jnp.dot(probs_low, value, preferred_element_type=WIDE).astype(LOW)
    out_ref[1] = (
        jnp.dot(probs_low, value_dual, preferred_element_type=WIDE)
        + jnp.dot(spread_low, value, preferred_element_type=WIDE)
    ).astype(LOW)


def attend(start, hdim, queries, keyed):
    rows = queries[0].shape[1]
    width = keyed[0].shape[2]
    first = start // hdim
    return pl.pallas_call(
        functools.partial(attend_kernel, len(queries)),
        grid=(width // hdim,),
        in_specs=[pl.BlockSpec((2, rows, hdim), lambda h: (0, 0, first + h))] * len(queries)
        + [pl.BlockSpec((4, rows, hdim), lambda h: (0, 0, h))] * len(keyed),
        out_specs=pl.BlockSpec((2, len(queries) * rows, hdim), lambda h: (0, 0, h)),
        out_shape=jax.ShapeDtypeStruct((2, len(queries) * rows, width), LOW),
        compiler_params=params(),
    )(*queries, *keyed)


def assemble_kernel(chunks, flip_ref, *refs):
    part_refs, out_ref = refs[:-1], refs[-1]
    groups, rows_all, group = out_ref.shape
    rows = rows_all // 8
    start = 0
    for at, width in enumerate(chunks):
        for side in range(2):
            part_ref = part_refs[2 * at + side]
            for kind in range(2):
                for core in range(2):
                    first = (4 * core + 2 * side + kind) * rows
                    for g in range(groups):
                        low, high = max(start, g * group), min(start + width, (g + 1) * group)
                        if low < high:
                            out_ref[g ^ flip_ref[0], first : first + rows, low - g * group : high - g * group] = (
                                part_ref[kind, core * rows : (core + 1) * rows, low - start : high - start]
                            )
        start += width


def assemble(flip, groups, chunks, pairs):
    rows = 4 * pairs[0][0].shape[1]
    return pl.pallas_call(
        functools.partial(assemble_kernel, chunks),
        in_specs=[pl.BlockSpec(memory_space=pltpu.SMEM)] + vmem_specs(2 * len(pairs)),
        out_specs=vmem_specs(1)[0],
        out_shape=jax.ShapeDtypeStruct((groups, rows, sum(chunks) // groups), LOW),
        compiler_params=params(),
    )(flip, *[part for pair in pairs for part in pair])


def project_kernel(acts_ref, *refs):
    weight_refs, (keep_ref, send_ref) = refs[:-2], refs[-2:]
    rows = keep_ref.shape[0]
    beside = jnp.concatenate([ref[...] for ref in weight_refs[1:]], axis=0)
    total = jnp.dot(acts_ref[0], weight_refs[0][...], preferred_element_type=WIDE)
    total = total + jnp.dot(acts_ref[1], beside, preferred_element_type=WIDE)
    keep_ref[...] = total[:rows]
    send_ref[...] = total[rows:].astype(LOW)


def project(acts, weights):
    rows, n = acts.shape[1] // 2, weights[0].shape[1]
    return pl.pallas_call(
        project_kernel,
        in_specs=vmem_specs(1 + len(weights)),
        out_specs=vmem_specs(2),
        out_shape=[jax.ShapeDtypeStruct((rows, n), WIDE), jax.ShapeDtypeStruct((rows, n), LOW)],
        compiler_params=params(),
    )(acts, *weights)


def close_kernel(keep_ref, got_ref, mine_ref, other_ref):
    total = (keep_ref[...] + got_ref[...].astype(WIDE)).astype(LOW)
    half = total.shape[0] // 2
    mine_ref[...] = total[:half].reshape(mine_ref.shape)
    other_ref[...] = total[half:].reshape(other_ref.shape)


def close(keep, got):
    rows, n = keep.shape
    out = jax.ShapeDtypeStruct((2, rows // 4, n), LOW)
    return pl.pallas_call(
        close_kernel,
        in_specs=vmem_specs(2),
        out_specs=vmem_specs(2),
        out_shape=[out, out],
        compiler_params=params(),
    )(keep, got)


def place_kernel(n_pieces, where_ref, *refs):
    piece_refs = refs[:n_pieces]
    plain_ref, dual_ref = refs[n_pieces:]
    n = piece_refs[0].shape[-1]
    for at, piece_ref in enumerate(piece_refs):
        columns = pl.ds(pl.multiple_of(where_ref[at] * n, n), n)
        plain_ref[:, columns] = piece_ref[0]
        dual_ref[:, columns] = piece_ref[1]


def place(where, pieces):
    kinds, rows, n = pieces[0].shape
    width = n * len(pieces)
    if n % 128:
        out = jnp.zeros((kinds, rows, width), LOW)
        for at, piece in enumerate(pieces):
            out = lax.dynamic_update_slice(out, piece, (0, 0, where[at] * n))
        return out[0], out[1]
    out = jax.ShapeDtypeStruct((rows, width), LOW)
    return pl.pallas_call(
        functools.partial(place_kernel, len(pieces)),
        in_specs=[pl.BlockSpec(memory_space=pltpu.SMEM)] + vmem_specs(len(pieces)),
        out_specs=vmem_specs(2),
        out_shape=[out, out],
        compiler_params=params(),
    )(where, *pieces)


def body(
    n_dp,
    n_seq,
    queries,
    key_states,
    value_states,
    query_tangent,
    key_tangent,
    value_tangent,
    query_gain,
    key_gain,
    out_weight,
):
    dp = lax.axis_index("dp")
    seq = lax.axis_index("seq")
    n_ring = n_dp // 2
    groups = n_seq // 2
    features = queries.shape[1]
    hdim = features // HEADS
    group_heads = HEADS // n_seq
    few = group_heads * 2 // 5
    chunks = [group_heads * hdim] * (groups - 1) + [(group_heads - few) * hdim, few * hdim]
    starts = [sum(chunks[:at]) for at in range(len(chunks))]
    token = jnp.zeros((1,), jnp.int32)

    def far(array):
        return lax.ppermute(array, "seq", [(i, i ^ 2) for i in range(n_seq)])

    def near(array):
        return lax.ppermute(array, "seq", [(i, i ^ 1) for i in range(n_seq)])

    def across(array):
        return lax.ppermute(array, "dp", [(i, i ^ 1) for i in range(n_dp)])

    def onward(array):
        return lax.ppermute(array, "dp", [(i, (i + 2) % n_dp) for i in range(n_dp)])

    def wait(array):
        nonlocal token
        array, token = lax.optimization_barrier((array, token))
        return array

    def turn(ring, step):
        ring[step] = wait(ring[step])
        if step + 1 < n_ring:
            ring.append(onward(ring[step]))

    depth = out_weight.shape[0]
    cuts = [depth * 3 // 10 // 16 * 16, depth * 6 // 10 // 16 * 16]
    rings = [out_weight, onward(out_weight)]
    early = [far(out_weight[: cuts[0]])]

    core = jnp.stack([seq % 2])
    arrays = (queries, key_states, value_states, query_tangent, key_tangent, value_tangent)
    packs = [wait(array) for array in pack(core, n_seq, chunks, arrays, (query_gain, key_gain))]
    half = len(packs) // 2
    query_own, *keyed_own = packs[:half]
    query_other, *keyed_other = packs[half:]
    keyed_near = [wait(near(keyed_other[0]))]
    turn(early, 0)
    keyed_near += [wait(near(array)) for array in keyed_other[1:]]
    queries_both = [query_own, wait(near(query_other))]
    keyed_far = [[far(own), far(other)] for own, other in zip(keyed_own, keyed_near)]
    late = [far(out_weight[cuts[0] : cuts[1]])]
    rest = [far(out_weight[cuts[1] :])]

    acts, swapped = [], []

    def attention(chunk):
        keyed = [keyed_own[chunk], keyed_near[chunk], *keyed_far[chunk]]
        acts.append(wait(attend(starts[chunk], hdim, queries_both, keyed)))
        swapped.append(across(acts[-1]))

    def keyed_wait(chunk, at):
        keyed_far[chunk][at] = wait(keyed_far[chunk][at])

    turn(rings, 1)
    keyed_wait(0, 0)
    turn(early, 1)
    keyed_wait(0, 1)
    turn(rings, 2)
    keyed_wait(1, 0)
    attention(0)
    turn(early, 2)
    keyed_wait(1, 1)
    keyed_wait(2, 0)
    attention(1)
    keyed_wait(2, 1)
    swapped[0] = wait(swapped[0])
    for step in range(3, n_ring):
        turn(rings, step)
        turn(early, step)
    attention(2)
    rest.append(far(rings[1][cuts[1] :]))
    turn(late, 0)
    swapped[1] = wait(swapped[1])
    rest[0] = wait(rest[0])
    swapped[2] = wait(swapped[2])
    acts = assemble(jnp.stack([seq // 2]), groups, chunks, list(zip(acts, swapped)))

    keeps, sends, mine, other = [], [], [], []

    def columns(step):
        blocks = [rings[step], early[step], late[step], rest[step]]
        keep, send = project(acts, blocks)
        keeps.append(keep)
        sends.append(near(wait(send)))

    def finish(step):
        own, out = close(keeps[step], wait(sends[step]))
        mine.append(own)
        other.append(across(wait(out)))

    for step in range(1, n_ring):
        turn(late, step)
        columns(step - 1)
        if step + 1 < n_ring:
            rest.append(far(rings[step + 1][cuts[1] :]))
        rest[step] = wait(rest[step])
        finish(step - 1)
        if step > 1:
            other[step - 2] = wait(other[step - 2])
    columns(n_ring - 1)
    finish(n_ring - 1)

    pieces, where = [], []
    for step in range(n_ring):
        pair = (dp // 2 - step) % n_ring
        pieces += [mine[step], other[step]]
        where += [2 * pair + dp % 2, 2 * pair + 1 - dp % 2]
    return place(jnp.stack(where).astype(jnp.int32) + token, pieces)


def solution(mesh):
    rows = P(("dp", "seq"), None)
    return jax.shard_map(
        functools.partial(body, mesh.shape["dp"], mesh.shape["seq"]),
        mesh=mesh,
        in_specs=(rows,) * 6 + (P(), P(), P("seq", "dp")),
        out_specs=(rows, rows),
        check_vma=False,
    )
```

```python
import functools

import jax
import jax.numpy as jnp
from jax import lax
from jax.experimental import pallas as pl
from jax.experimental.pallas import tpu as pltpu
from jax.sharding import PartitionSpec as P

HEADS = 20
EPS = 1e-06
VMEM_BYTES = 48 * 1024 * 1024
ROW_STEP = 32

LOW = jnp.bfloat16
WIDE = jnp.float32
LIGHT = pl.CostEstimate(flops=1, transcendentals=0, bytes_accessed=1)


def params():
    return pltpu.CompilerParams(vmem_limit_bytes=VMEM_BYTES)


def vmem_specs(count):
    return [pl.BlockSpec(memory_space=pltpu.VMEM)] * count


def pack_kernel(n_seq, chunks, core_ref, *refs):
    query_ref, key_ref, value_ref, dquery_ref, dkey_ref, dvalue_ref, query_gain_ref, key_gain_ref = refs[:8]
    out_refs = refs[8:]
    n_chunks = len(chunks)
    group = query_ref.shape[-1] // n_seq

    def statistics(primal_ref, tangent_ref):
        primal = primal_ref[...].astype(WIDE)
        tangent = tangent_ref[...].astype(WIDE)
        inverse = lax.rsqrt(jnp.mean(primal * primal, axis=-1, keepdims=True) + EPS)
        across = jnp.mean(primal * tangent, axis=-1, keepdims=True)
        return inverse, inverse * inverse * inverse * across

    query_stats = statistics(query_ref, dquery_ref)
    key_stats = statistics(key_ref, dkey_ref)

    def normed(primal_ref, tangent_ref, gain_ref, stats, lanes):
        primal = primal_ref[:, lanes].astype(WIDE)
        tangent = tangent_ref[:, lanes].astype(WIDE)
        gain = gain_ref[:, lanes]
        inverse, slope = stats
        return (primal * inverse * gain).astype(LOW), (gain * (tangent * inverse - primal * slope)).astype(LOW)

    for side in range(2):
        core = core_ref[0] if side == 0 else 1 - core_ref[0]
        queries_ref, *keyed_refs = out_refs[side * (1 + n_chunks) : (side + 1) * (1 + n_chunks)]
        for at in range(n_seq // 2):
            lanes = pl.ds(pl.multiple_of((2 * at + core) * group, 128), group)
            here = slice(at * group, (at + 1) * group)
            plain, dual = normed(query_ref, dquery_ref, query_gain_ref, query_stats, lanes)
            queries_ref[0, :, here] = plain
            queries_ref[1, :, here] = dual
            four = normed(key_ref, dkey_ref, key_gain_ref, key_stats, lanes)
            four += (value_ref[:, lanes], dvalue_ref[:, lanes])
            start = 0
            for keyed_ref, width in zip(keyed_refs, chunks):
                low, high = max(start, here.start), min(start + width, here.stop)
                if low < high:
                    for which, part in enumerate(four):
                        keyed_ref[which, :, low - start : high - start] = part[:, low - here.start : high - here.start]
                start += width


def pack(core, n_seq, chunks, arrays, gains):
    rows, features = arrays[0].shape
    step = min(rows, ROW_STEP)
    row_block = pl.BlockSpec((step, features), lambda i, c: (i, 0))
    gain_block = pl.BlockSpec((1, features), lambda i, c: (0, 0))
    kinds = [(2, features // 2)] + [(4, width) for width in chunks]
    kinds = kinds + kinds
    return pl.pallas_call(
        functools.partial(pack_kernel, n_seq, chunks),
        grid_spec=pltpu.PrefetchScalarGridSpec(
            num_scalar_prefetch=1,
            grid=(rows // step,),
            in_specs=[row_block] * 6 + [gain_block] * 2,
            out_specs=[pl.BlockSpec((count, step, width), lambda i, c: (0, i, 0)) for count, width in kinds],
        ),
        out_shape=[jax.ShapeDtypeStruct((count, rows, width), LOW) for count, width in kinds],
        compiler_params=params(),
        cost_estimate=LIGHT,
    )(core, *arrays, *[gain.reshape(1, features) for gain in gains])


def attend_kernel(n_queries, *refs):
    query_refs, keyed_refs, out_ref = refs[:n_queries], refs[n_queries:-1], refs[-1]

    def stack(which, some_refs):
        return jnp.concatenate([ref[which] for ref in some_refs], axis=0)

    query, query_dual = (stack(which, query_refs) for which in range(2))
    key, key_dual, value, value_dual = (stack(which, keyed_refs) for which in range(4))
    factor = query.shape[-1] ** (-0.5)
    last = (((1,), (1,)), ((), ()))
    scores = lax.dot_general(query, key, last, preferred_element_type=WIDE) * factor
    dual_scores = (
        lax.dot_general(
            jnp.concatenate([query_dual, query], axis=1),
            jnp.concatenate([key, key_dual], axis=1),
            last,
            preferred_element_type=WIDE,
        )
        * factor
    )
    raised = jnp.exp(scores - jnp.max(scores, axis=-1, keepdims=True))
    probs = raised * (1.0 / jnp.sum(raised, axis=-1, keepdims=True))
    spread = probs * (dual_scores - jnp.sum(probs * dual_scores, axis=-1, keepdims=True))
    probs_low = probs.astype(LOW)
    spread_low = spread.astype(LOW)
    out_ref[0] = jnp.dot(probs_low, value, preferred_element_type=WIDE).astype(LOW)
    out_ref[1] = (
        jnp.dot(probs_low, value_dual, preferred_element_type=WIDE)
        + jnp.dot(spread_low, value, preferred_element_type=WIDE)
    ).astype(LOW)


def attend(start, hdim, queries, keyed):
    rows = queries[0].shape[1]
    width = keyed[0].shape[2]
    first = start // hdim
    return pl.pallas_call(
        functools.partial(attend_kernel, len(queries)),
        grid=(width // hdim,),
        in_specs=[pl.BlockSpec((2, rows, hdim), lambda h: (0, 0, first + h))] * len(queries)
        + [pl.BlockSpec((4, rows, hdim), lambda h: (0, 0, h))] * len(keyed),
        out_specs=pl.BlockSpec((2, len(queries) * rows, hdim), lambda h: (0, 0, h)),
        out_shape=jax.ShapeDtypeStruct((2, len(queries) * rows, width), LOW),
        compiler_params=params(),
        cost_estimate=LIGHT,
    )(*queries, *keyed)


def assemble_kernel(chunks, flip_ref, *refs):
    part_refs, out_ref = refs[:-1], refs[-1]
    groups, rows_all, group = out_ref.shape
    rows = rows_all // 8
    start = 0
    for at, width in enumerate(chunks):
        for side in range(2):
            part_ref = part_refs[2 * at + side]
            for kind in range(2):
                for core in range(2):
                    first = (4 * core + 2 * side + kind) * rows
                    for g in range(groups):
                        low, high = max(start, g * group), min(start + width, (g + 1) * group)
                        if low < high:
                            out_ref[g ^ flip_ref[0], first : first + rows, low - g * group : high - g * group] = (
                                part_ref[kind, core * rows : (core + 1) * rows, low - start : high - start]
                            )
        start += width


def assemble(flip, groups, chunks, pairs):
    rows = 4 * pairs[0][0].shape[1]
    return pl.pallas_call(
        functools.partial(assemble_kernel, chunks),
        in_specs=[pl.BlockSpec(memory_space=pltpu.SMEM)] + vmem_specs(2 * len(pairs)),
        out_specs=vmem_specs(1)[0],
        out_shape=jax.ShapeDtypeStruct((groups, rows, sum(chunks) // groups), LOW),
        compiler_params=params(),
        cost_estimate=LIGHT,
    )(flip, *[part for pair in pairs for part in pair])


def project_kernel(pieces, acts_ref, *refs):
    weight_refs, (keep_ref, send_ref) = list(refs[:-2]), refs[-2:]
    rows = keep_ref.shape[0]
    total = 0.0
    for at, count in enumerate(pieces):
        weight = jnp.concatenate([weight_refs.pop(0)[...] for _ in range(count)], axis=0)
        total = total + jnp.dot(acts_ref[at], weight, preferred_element_type=WIDE)
    keep_ref[...] = total[:rows]
    send_ref[...] = total[rows:].astype(LOW)


def project(acts, blocks):
    weights = [piece for block in blocks for piece in block]
    rows, n = acts.shape[1] // 2, weights[0].shape[1]
    return pl.pallas_call(
        functools.partial(project_kernel, [len(block) for block in blocks]),
        in_specs=vmem_specs(1 + len(weights)),
        out_specs=vmem_specs(2),
        out_shape=[jax.ShapeDtypeStruct((rows, n), WIDE), jax.ShapeDtypeStruct((rows, n), LOW)],
        compiler_params=params(),
        cost_estimate=LIGHT,
    )(acts, *weights)


def close_kernel(keep_ref, got_ref, mine_ref, other_ref):
    total = (keep_ref[...] + got_ref[...].astype(WIDE)).astype(LOW)
    half = total.shape[0] // 2
    mine_ref[...] = total[:half].reshape(mine_ref.shape)
    other_ref[...] = total[half:].reshape(other_ref.shape)


def close(keep, got):
    rows, n = keep.shape
    out = jax.ShapeDtypeStruct((2, rows // 4, n), LOW)
    return pl.pallas_call(
        close_kernel,
        in_specs=vmem_specs(2),
        out_specs=vmem_specs(2),
        out_shape=[out, out],
        compiler_params=params(),
        cost_estimate=LIGHT,
    )(keep, got)


def place_kernel(n_pieces, where_ref, *refs):
    piece_refs = refs[:n_pieces]
    plain_ref, dual_ref = refs[n_pieces:]
    n = piece_refs[0].shape[-1]
    for at, piece_ref in enumerate(piece_refs):
        columns = pl.ds(pl.multiple_of(where_ref[at] * n, n), n)
        plain_ref[:, columns] = piece_ref[0]
        dual_ref[:, columns] = piece_ref[1]


def place(where, pieces):
    kinds, rows, n = pieces[0].shape
    width = n * len(pieces)
    if n % 128:
        out = jnp.zeros((kinds, rows, width), LOW)
        for at, piece in enumerate(pieces):
            out = lax.dynamic_update_slice(out, piece, (0, 0, where[at] * n))
        return out[0], out[1]
    out = jax.ShapeDtypeStruct((rows, width), LOW)
    return pl.pallas_call(
        functools.partial(place_kernel, len(pieces)),
        in_specs=[pl.BlockSpec(memory_space=pltpu.SMEM)] + vmem_specs(len(pieces)),
        out_specs=vmem_specs(2),
        out_shape=[out, out],
        compiler_params=params(),
        cost_estimate=LIGHT,
    )(where, *pieces)


def body(
    n_dp,
    n_seq,
    queries,
    key_states,
    value_states,
    query_tangent,
    key_tangent,
    value_tangent,
    query_gain,
    key_gain,
    out_weight,
):
    dp = lax.axis_index("dp")
    seq = lax.axis_index("seq")
    n_ring = n_dp // 2
    groups = n_seq // 2
    features = queries.shape[1]
    hdim = features // HEADS
    group_heads = HEADS // n_seq
    few = group_heads * 2 // 5
    chunks = [group_heads * hdim] * (groups - 1) + [(group_heads - few) * hdim, few * hdim]
    starts = [sum(chunks[:at]) for at in range(len(chunks))]
    token = jnp.zeros((1,), jnp.int32)

    def far(array):
        return lax.ppermute(array, "seq", [(i, i ^ 2) for i in range(n_seq)])

    def near(array):
        return lax.ppermute(array, "seq", [(i, i ^ 1) for i in range(n_seq)])

    def across(array):
        return lax.ppermute(array, "dp", [(i, i ^ 1) for i in range(n_dp)])

    def onward(array):
        return lax.ppermute(array, "dp", [(i, (i + 2) % n_dp) for i in range(n_dp)])

    def wait(array):
        nonlocal token
        array, token = lax.optimization_barrier((array, token))
        return array

    def after(array):
        return lax.optimization_barrier((array, token))[0]

    def turn(ring, step):
        ring[step] = wait(ring[step])
        if step + 1 < n_ring:
            ring.append(onward(ring[step]))

    depth = out_weight.shape[0]
    cuts = [depth * 3 // 10 // 16 * 16, depth * 6 // 10 // 16 * 16]
    early = [far(out_weight[: cuts[0]])]
    turn(early, 0)

    core = jnp.stack([seq % 2])
    arrays = (queries, key_states, value_states, query_tangent, key_tangent, value_tangent)
    packs = [wait(array) for array in pack(core, n_seq, chunks, arrays, (query_gain, key_gain))]
    half = len(packs) // 2
    query_own, *keyed_own = packs[:half]
    query_other, *keyed_other = packs[half:]
    tops, lows = [out_weight[: depth // 2]], [out_weight[depth // 2 :]]
    tops.append(onward(tops[0]))
    lows.append(onward(lows[0]))
    keyed_near = [wait(near(array)) for array in keyed_other]
    queries_both = [query_own, wait(near(query_other))]
    keyed_far = [[far(own), far(other)] for own, other in zip(keyed_own, keyed_near)]

    acts, swapped = [], []

    def attention(chunk):
        keyed = [keyed_own[chunk], keyed_near[chunk], *keyed_far[chunk]]
        acts.append(wait(attend(starts[chunk], hdim, queries_both, keyed)))
        swapped.append(across(acts[-1]))

    def keyed_wait(chunk, at):
        keyed_far[chunk][at] = wait(keyed_far[chunk][at])

    keyed_wait(0, 0)
    turn(early, 1)
    turn(tops, 1)
    turn(lows, 1)
    keyed_wait(0, 1)
    keyed_wait(1, 0)
    turn(early, 2)
    turn(tops, 2)
    attention(0)
    turn(lows, 2)
    keyed_wait(1, 1)
    late = [far(after(out_weight[cuts[0] : cuts[1]]))]
    keyed_wait(2, 0)
    rest = [far(after(out_weight[cuts[1] :]))]
    attention(1)
    keyed_wait(2, 1)
    swapped[0] = wait(swapped[0])
    turn(late, 0)
    attention(2)
    for step in range(3, n_ring):
        turn(early, step)
        turn(tops, step)
        turn(lows, step)
    rest.append(far(lows[1][cuts[1] - depth // 2 :]))
    swapped[1] = wait(swapped[1])
    rest[0] = wait(rest[0])
    swapped[2] = wait(swapped[2])
    acts = assemble(jnp.stack([seq // 2]), groups, chunks, list(zip(acts, swapped)))

    keeps, sends, mine, other = [], [], [], []

    def columns(step):
        blocks = [[tops[step], lows[step]], [early[step], late[step], rest[step]]]
        keep, send = project(acts, blocks)
        keeps.append(keep)
        sends.append(near(wait(send)))

    def finish(step):
        own, out = close(keeps[step], wait(sends[step]))
        mine.append(own)
        other.append(across(wait(out)))

    for step in range(1, n_ring):
        turn(late, step)
        if step + 1 < n_ring:
            rest.append(far(lows[step + 1][cuts[1] - depth // 2 :]))
        rest[step] = wait(rest[step])
        columns(step - 1)
        if step > 1:
            finish(step - 2)
        if step > 2:
            other[step - 3] = wait(other[step - 3])
    columns(n_ring - 1)
    finish(n_ring - 2)
    finish(n_ring - 1)

    pieces, where = [], []
    for step in range(n_ring):
        pair = (dp // 2 - step) % n_ring
        pieces += [mine[step], other[step]]
        where += [2 * pair + dp % 2, 2 * pair + 1 - dp % 2]
    return place(jnp.stack(where).astype(jnp.int32) + token, pieces)


def solution(mesh):
    rows = P(("dp", "seq"), None)
    return jax.shard_map(
        functools.partial(body, mesh.shape["dp"], mesh.shape["seq"]),
        mesh=mesh,
        in_specs=(rows,) * 6 + (P(), P(), P("seq", "dp")),
        out_specs=(rows, rows),
        check_vma=False,
    )
```

```python
import functools

import jax
import jax.numpy as jnp
from jax import lax
from jax.experimental import pallas as pl
from jax.experimental.pallas import tpu as pltpu
from jax.sharding import PartitionSpec as P

HEADS = 20
EPS = 1e-06
VMEM_BYTES = 48 * 1024 * 1024
ROW_STEP = 32

LOW = jnp.bfloat16
WIDE = jnp.float32
LIGHT = pl.CostEstimate(flops=1, transcendentals=0, bytes_accessed=1)


def params():
    return pltpu.CompilerParams(vmem_limit_bytes=VMEM_BYTES)


def vmem_specs(count):
    return [pl.BlockSpec(memory_space=pltpu.VMEM)] * count


def pack_kernel(n_seq, chunks, core_ref, *refs):
    query_ref, key_ref, value_ref, dquery_ref, dkey_ref, dvalue_ref, gains_ref = refs[:7]
    out_refs = refs[7:]
    n_chunks = len(chunks)
    group = query_ref.shape[-1] // n_seq

    def statistics(primal_ref, tangent_ref):
        primal = primal_ref[...].astype(WIDE)
        tangent = tangent_ref[...].astype(WIDE)
        inverse = lax.rsqrt(jnp.mean(primal * primal, axis=-1, keepdims=True) + EPS)
        across = jnp.mean(primal * tangent, axis=-1, keepdims=True)
        return inverse, inverse * inverse * inverse * across

    query_stats = statistics(query_ref, dquery_ref)
    key_stats = statistics(key_ref, dkey_ref)

    def normed(primal_ref, tangent_ref, which, stats, lanes):
        primal = primal_ref[:, lanes].astype(WIDE)
        tangent = tangent_ref[:, lanes].astype(WIDE)
        gain = gains_ref[which : which + 1, lanes]
        inverse, slope = stats
        return (primal * inverse * gain).astype(LOW), (gain * (tangent * inverse - primal * slope)).astype(LOW)

    for side in range(2):
        core = core_ref[0] if side == 0 else 1 - core_ref[0]
        queries_ref, *keyed_refs = out_refs[side * (1 + n_chunks) : (side + 1) * (1 + n_chunks)]
        for at in range(n_seq // 2):
            lanes = pl.ds(pl.multiple_of((2 * at + core) * group, 128), group)
            here = slice(at * group, (at + 1) * group)
            plain, dual = normed(query_ref, dquery_ref, 0, query_stats, lanes)
            queries_ref[0, :, here] = plain
            queries_ref[1, :, here] = dual
            four = normed(key_ref, dkey_ref, 1, key_stats, lanes)
            four += (value_ref[:, lanes], dvalue_ref[:, lanes])
            start = 0
            for keyed_ref, width in zip(keyed_refs, chunks):
                low, high = max(start, here.start), min(start + width, here.stop)
                if low < high:
                    for which, part in enumerate(four):
                        keyed_ref[which, :, low - start : high - start] = part[:, low - here.start : high - here.start]
                start += width


def pack(core, n_seq, chunks, arrays, gains):
    rows, features = arrays[0].shape
    step = min(rows, ROW_STEP)
    row_block = pl.BlockSpec((step, features), lambda i, c: (i, 0))
    gain_block = pl.BlockSpec((2, features), lambda i, c: (0, 0))
    kinds = [(2, features // 2)] + [(4, width) for width in chunks]
    kinds = kinds + kinds
    return pl.pallas_call(
        functools.partial(pack_kernel, n_seq, chunks),
        grid_spec=pltpu.PrefetchScalarGridSpec(
            num_scalar_prefetch=1,
            grid=(rows // step,),
            in_specs=[row_block] * 6 + [gain_block],
            out_specs=[pl.BlockSpec((count, step, width), lambda i, c: (0, i, 0)) for count, width in kinds],
        ),
        out_shape=[jax.ShapeDtypeStruct((count, rows, width), LOW) for count, width in kinds],
        compiler_params=params(),
        cost_estimate=LIGHT,
    )(core, *arrays, gains)


def attend_kernel(n_queries, *refs):
    query_refs, keyed_refs, out_ref = refs[:n_queries], refs[n_queries:-1], refs[-1]

    def stack(which, some_refs, kinds):
        parts = [ref[at] for ref in some_refs for at in range(which, ref.shape[0], kinds)]
        return jnp.concatenate(parts, axis=0)

    query, query_dual = (stack(which, query_refs, 2) for which in range(2))
    key, key_dual, value, value_dual = (stack(which, keyed_refs, 4) for which in range(4))
    factor = query.shape[-1] ** (-0.5)
    last = (((1,), (1,)), ((), ()))
    scores = lax.dot_general(query, key, last, preferred_element_type=WIDE) * factor
    dual_scores = (
        lax.dot_general(
            jnp.concatenate([query_dual, query], axis=1),
            jnp.concatenate([key, key_dual], axis=1),
            last,
            preferred_element_type=WIDE,
        )
        * factor
    )
    raised = jnp.exp(scores - jnp.max(scores, axis=-1, keepdims=True))
    probs = raised * (1.0 / jnp.sum(raised, axis=-1, keepdims=True))
    spread = probs * (dual_scores - jnp.sum(probs * dual_scores, axis=-1, keepdims=True))
    probs_low = probs.astype(LOW)
    spread_low = spread.astype(LOW)
    out_ref[0] = jnp.dot(probs_low, value, preferred_element_type=WIDE).astype(LOW)
    out_ref[1] = (
        jnp.dot(probs_low, value_dual, preferred_element_type=WIDE)
        + jnp.dot(spread_low, value, preferred_element_type=WIDE)
    ).astype(LOW)


def attend(start, hdim, queries, keyed):
    rows = queries[0].shape[1]
    width = keyed[0].shape[2]
    first = start // hdim
    return pl.pallas_call(
        functools.partial(attend_kernel, len(queries)),
        grid=(width // hdim,),
        in_specs=[pl.BlockSpec((2, rows, hdim), lambda h: (0, 0, first + h))] * len(queries)
        + [pl.BlockSpec((array.shape[0], rows, hdim), lambda h: (0, 0, h)) for array in keyed],
        out_specs=pl.BlockSpec((2, len(queries) * rows, hdim), lambda h: (0, 0, h)),
        out_shape=jax.ShapeDtypeStruct((2, len(queries) * rows, width), LOW),
        compiler_params=params(),
        cost_estimate=LIGHT,
    )(*queries, *keyed)


def assemble_kernel(chunks, flip_ref, *refs):
    part_refs, out_ref = refs[:-1], refs[-1]
    groups, rows_all, group = out_ref.shape
    rows = rows_all // 8
    start = 0
    for at, width in enumerate(chunks):
        for side in range(2):
            part_ref = part_refs[2 * at + side]
            for kind in range(2):
                for core in range(2):
                    first = (4 * core + 2 * side + kind) * rows
                    for g in range(groups):
                        low, high = max(start, g * group), min(start + width, (g + 1) * group)
                        if low < high:
                            out_ref[g ^ flip_ref[0], first : first + rows, low - g * group : high - g * group] = (
                                part_ref[kind, core * rows : (core + 1) * rows, low - start : high - start]
                            )
        start += width


def assemble(flip, groups, chunks, pairs):
    rows = 4 * pairs[0][0].shape[1]
    return pl.pallas_call(
        functools.partial(assemble_kernel, chunks),
        in_specs=[pl.BlockSpec(memory_space=pltpu.SMEM)] + vmem_specs(2 * len(pairs)),
        out_specs=vmem_specs(1)[0],
        out_shape=jax.ShapeDtypeStruct((groups, rows, sum(chunks) // groups), LOW),
        compiler_params=params(),
        cost_estimate=LIGHT,
    )(flip, *[part for pair in pairs for part in pair])


def project_kernel(spans, acts_ref, *refs):
    weight_refs = refs[:-4]
    keep_mine_ref, keep_other_ref, send_mine_ref, send_other_ref = refs[-4:]
    rows = keep_mine_ref.shape[0]
    total = 0.0
    for at, block in enumerate(spans):
        weight = jnp.concatenate([weight_refs[which][low:high] for which, low, high in block], axis=0)
        total = total + jnp.dot(acts_ref[at], weight, preferred_element_type=WIDE)
    keep_mine_ref[...] = total[:rows]
    keep_other_ref[...] = total[rows : 2 * rows]
    send_mine_ref[...] = total[2 * rows : 3 * rows].astype(LOW)
    send_other_ref[...] = total[3 * rows :].astype(LOW)


def project(acts, *blocks):
    weights, spans = [], []
    for block in blocks:
        spans.append([])
        for weight, low, high in block:
            if not any(weight is known for known in weights):
                weights.append(weight)
            which = [weight is known for known in weights].index(True)
            spans[-1].append((which, low, high))
    rows, n = acts.shape[1] // 4, weights[0].shape[1]
    return pl.pallas_call(
        functools.partial(project_kernel, spans),
        in_specs=vmem_specs(1 + len(weights)),
        out_specs=vmem_specs(4),
        out_shape=[jax.ShapeDtypeStruct((rows, n), WIDE)] * 2 + [jax.ShapeDtypeStruct((rows, n), LOW)] * 2,
        compiler_params=params(),
        cost_estimate=LIGHT,
    )(acts, *weights)


def close_kernel(keep_ref, got_ref, out_ref):
    out_ref[...] = (keep_ref[...] + got_ref[...].astype(WIDE)).astype(LOW)


def close(keep, got):
    return pl.pallas_call(
        close_kernel,
        in_specs=vmem_specs(2),
        out_specs=vmem_specs(1)[0],
        out_shape=jax.ShapeDtypeStruct(keep.shape, LOW),
        compiler_params=params(),
        cost_estimate=LIGHT,
    )(keep, got)


def place_kernel(n_steps, where_ref, *refs):
    keep_refs, got_refs, other_refs = refs[:n_steps], refs[n_steps : 2 * n_steps], refs[2 * n_steps : -2]
    plain_ref, dual_ref = refs[-2:]
    rows, n = plain_ref.shape[0], other_refs[0].shape[-1]
    for step in range(n_steps):
        mine, others = (pl.ds(pl.multiple_of(where_ref[2 * step + side] * n, n), n) for side in range(2))
        for kind, out_ref in enumerate((plain_ref, dual_ref)):
            here = slice(kind * rows, (kind + 1) * rows)
            out_ref[:, mine] = (keep_refs[step][here] + got_refs[step][here].astype(WIDE)).astype(LOW)
            out_ref[:, others] = other_refs[step][here]


def place(where, keeps, gots, others):
    rows, n = others[0].shape[0] // 2, others[0].shape[1]
    width = 2 * n * len(others)
    if n % 128:
        out = jnp.zeros((2 * rows, width), LOW)
        for step, (keep, got, other) in enumerate(zip(keeps, gots, others)):
            for side, piece in enumerate((close(keep, got), other)):
                out = lax.dynamic_update_slice(out, piece, (0, where[2 * step + side] * n))
        return out[:rows], out[rows:]
    out = jax.ShapeDtypeStruct((rows, width), LOW)
    return pl.pallas_call(
        functools.partial(place_kernel, len(others)),
        in_specs=[pl.BlockSpec(memory_space=pltpu.SMEM)] + vmem_specs(3 * len(others)),
        out_specs=vmem_specs(2),
        out_shape=[out, out],
        compiler_params=params(),
        cost_estimate=LIGHT,
    )(where, *keeps, *gots, *others)


def body(
    n_dp,
    n_seq,
    queries,
    key_states,
    value_states,
    query_tangent,
    key_tangent,
    value_tangent,
    query_gain,
    key_gain,
    out_weight,
):
    dp = lax.axis_index("dp")
    seq = lax.axis_index("seq")
    n_ring = n_dp // 2
    groups = n_seq // 2
    features = queries.shape[1]
    hdim = features // HEADS
    group_heads = HEADS // n_seq
    few = group_heads * 2 // 5
    chunks = [group_heads * hdim] * (groups - 1) + [(group_heads - few) * hdim, few * hdim]
    starts = [sum(chunks[:at]) for at in range(len(chunks))]
    token = jnp.zeros((1,), jnp.int32)

    def far(array):
        return lax.ppermute(array, "seq", [(i, i ^ 2) for i in range(n_seq)])

    def near(array):
        return lax.ppermute(array, "seq", [(i, i ^ 1) for i in range(n_seq)])

    def across(array):
        return lax.ppermute(array, "dp", [(i, i ^ 1) for i in range(n_dp)])

    def onward(array):
        return lax.ppermute(array, "dp", [(i, (i + 2) % n_dp) for i in range(n_dp)])

    def wait(array):
        nonlocal token
        array, token = lax.optimization_barrier((array, token))
        return array

    def after(array):
        return lax.optimization_barrier((array, token))[0]

    def turn(ring, step):
        ring[step] = wait(ring[step])
        if step + 1 < n_ring:
            ring.append(onward(ring[step]))

    depth = out_weight.shape[0]
    cut = depth * 3 // 5 // 16 * 16
    upper, lower = [out_weight[:cut]], [out_weight[cut:]]
    lower.append(onward(lower[0]))
    beside = [wait(far(upper[0]))]
    turn(lower, 1)

    core = jnp.stack([seq % 2])
    arrays = (queries, key_states, value_states, query_tangent, key_tangent, value_tangent)
    packs = [wait(array) for array in pack(core, n_seq, chunks, arrays, jnp.stack([query_gain, key_gain]))]
    half = len(packs) // 2
    query_own, *keyed_own = packs[:half]
    query_other, *keyed_other = packs[half:]
    keyed_near = [wait(near(array)) for array in keyed_other]
    queries_both = [query_own, wait(near(query_other))]
    keyed_far = [[far(keyed_own[0]), far(keyed_near[0])]]
    keyed_far += [[far(jnp.concatenate(pair))] for pair in zip(keyed_own[1:], keyed_near[1:])]
    upper.append(onward(upper[0]))
    beside.append(onward(beside[0]))
    turn(lower, 2)

    acts, swapped = [], []

    def attention(chunk):
        keyed_far[chunk][-1] = wait(keyed_far[chunk][-1])
        blocks = [keyed_own[chunk], keyed_near[chunk], *keyed_far[chunk]]
        acts.append(wait(attend(starts[chunk], hdim, queries_both, blocks)))
        swapped.append(across(acts[-1]))

    turn(upper, 1)
    keyed_far[0][0] = wait(keyed_far[0][0])
    turn(beside, 1)
    attention(0)
    for step in range(3, n_ring):
        turn(lower, step)
    later = [wait(jnp.concatenate(lower[step : step + 2])) for step in range(2, n_ring, 2)]
    turn(upper, 2)
    rest = [far(after(lower[0]))]
    attention(1)
    turn(beside, 2)
    swapped[0] = wait(swapped[0])
    swapped[1] = wait(swapped[1])
    attention(2)
    rest += [far(after(piece)) for piece in lower[1:2] + later]
    for step in range(3, n_ring):
        turn(upper, step)
    rest[0] = wait(rest[0])
    swapped[2] = wait(swapped[2])
    acts = wait(assemble(jnp.stack([seq // 2]), groups, chunks, list(zip(acts, swapped))))

    keeps, mine_sends, sends, mine_got, other = [], [], [], [], []

    def columns(step):
        own = [(upper[step], 0, cut), (lower[step], 0, depth - cut)]
        start = step % 2 * (depth - cut) if step > 1 else 0
        got = rest[step] if step < 2 else rest[1 + step // 2]
        theirs = [(beside[step], 0, cut), (got, start, start + depth - cut)]
        keep_mine, keep_other, send_mine, send_other = project(acts, own, theirs)
        keeps.append((keep_mine, keep_other))
        sends.append(near(wait(send_other)))
        mine_sends.append(send_mine)

    def finish(step):
        other.append(across(wait(close(keeps[step][1], wait(sends[step])))))
        mine_got.append(near(mine_sends[step]))

    columns(0)
    rest[1] = wait(rest[1])
    columns(1)
    finish(0)
    finish(1)
    for step in range(2, n_ring, 2):
        for ahead in range(max(step, 3), step + 2):
            turn(beside, ahead)
        rest[1 + step // 2] = wait(rest[1 + step // 2])
        columns(step)
        other[step - 2] = wait(other[step - 2])
        finish(step)
        columns(step + 1)
        other[step - 1] = wait(other[step - 1])
        mine_got[step - 2] = wait(mine_got[step - 2])
        mine_got[step - 1] = wait(mine_got[step - 1])
        finish(step + 1)

    where = []
    for step in range(n_ring):
        pair = (dp // 2 - step) % n_ring
        where += [2 * pair + dp % 2, 2 * pair + 1 - dp % 2]
    where = jnp.stack(where).astype(jnp.int32) + token
    return place(where, [keep for keep, _ in keeps], mine_got, other)


def solution(mesh):
    rows = P(("dp", "seq"), None)
    return jax.shard_map(
        functools.partial(body, mesh.shape["dp"], mesh.shape["seq"]),
        mesh=mesh,
        in_specs=(rows,) * 6 + (P(), P(), P("seq", "dp")),
        out_specs=(rows, rows),
        check_vma=False,
    )
```

```python
import functools

import jax
import jax.numpy as jnp
from jax import lax
from jax.experimental import pallas as pl
from jax.experimental.pallas import tpu as pltpu
from jax.sharding import PartitionSpec as P

HEADS = 20
EPS = 1e-06
VMEM_BYTES = 16 * 1024 * 1024
ROW_STEP = 32

LOW = jnp.bfloat16
WIDE = jnp.float32
LIGHT = pl.CostEstimate(flops=1, transcendentals=0, bytes_accessed=1)


def params():
    return pltpu.CompilerParams(vmem_limit_bytes=VMEM_BYTES)


def vmem_specs(count):
    return [pl.BlockSpec(memory_space=pltpu.VMEM)] * count


def pack_kernel(n_seq, chunks, core_ref, *refs):
    query_ref, key_ref, value_ref, dquery_ref, dkey_ref, dvalue_ref, gains_ref = refs[:7]
    out_refs = refs[7:]
    n_chunks = len(chunks)
    group = query_ref.shape[-1] // n_seq

    def statistics(primal_ref, tangent_ref):
        primal = primal_ref[...].astype(WIDE)
        tangent = tangent_ref[...].astype(WIDE)
        inverse = lax.rsqrt(jnp.mean(primal * primal, axis=-1, keepdims=True) + EPS)
        across = jnp.mean(primal * tangent, axis=-1, keepdims=True)
        return inverse, inverse * inverse * inverse * across

    query_stats = statistics(query_ref, dquery_ref)
    key_stats = statistics(key_ref, dkey_ref)

    def normed(primal_ref, tangent_ref, which, stats, lanes):
        primal = primal_ref[:, lanes].astype(WIDE)
        tangent = tangent_ref[:, lanes].astype(WIDE)
        gain = gains_ref[which : which + 1, lanes]
        inverse, slope = stats
        return (primal * inverse * gain).astype(LOW), (gain * (tangent * inverse - primal * slope)).astype(LOW)

    for side in range(2):
        core = core_ref[0] if side == 0 else 1 - core_ref[0]
        queries_ref, *keyed_refs = out_refs[side * (1 + n_chunks) : (side + 1) * (1 + n_chunks)]
        for at in range(n_seq // 2):
            lanes = pl.ds(pl.multiple_of((2 * at + core) * group, 128), group)
            here = slice(at * group, (at + 1) * group)
            plain, dual = normed(query_ref, dquery_ref, 0, query_stats, lanes)
            queries_ref[0, :, here] = plain
            queries_ref[1, :, here] = dual
            four = normed(key_ref, dkey_ref, 1, key_stats, lanes)
            four += (value_ref[:, lanes], dvalue_ref[:, lanes])
            start = 0
            for keyed_ref, width in zip(keyed_refs, chunks):
                low, high = max(start, here.start), min(start + width, here.stop)
                if low < high:
                    for which, part in enumerate(four):
                        keyed_ref[which, :, low - start : high - start] = part[:, low - here.start : high - here.start]
                start += width


def pack(core, n_seq, chunks, arrays, gains):
    rows, features = arrays[0].shape
    step = min(rows, ROW_STEP)
    row_block = pl.BlockSpec((step, features), lambda i, c: (i, 0))
    gain_block = pl.BlockSpec((2, features), lambda i, c: (0, 0))
    kinds = [(2, features // 2)] + [(4, width) for width in chunks]
    kinds = kinds + kinds
    return pl.pallas_call(
        functools.partial(pack_kernel, n_seq, chunks),
        grid_spec=pltpu.PrefetchScalarGridSpec(
            num_scalar_prefetch=1,
            grid=(rows // step,),
            in_specs=[row_block] * 6 + [gain_block],
            out_specs=[pl.BlockSpec((count, step, width), lambda i, c: (0, i, 0)) for count, width in kinds],
        ),
        out_shape=[jax.ShapeDtypeStruct((count, rows, width), LOW) for count, width in kinds],
        compiler_params=params(),
        cost_estimate=LIGHT,
    )(core, *arrays, gains)


def attend_kernel(n_queries, *refs):
    query_refs, keyed_refs, out_ref = refs[:n_queries], refs[n_queries:-1], refs[-1]

    def stack(which, some_refs, kinds):
        parts = [ref[at] for ref in some_refs for at in range(which, ref.shape[0], kinds)]
        return jnp.concatenate(parts, axis=0)

    query, query_dual = (stack(which, query_refs, 2) for which in range(2))
    key, key_dual, value, value_dual = (stack(which, keyed_refs, 4) for which in range(4))
    factor = query.shape[-1] ** (-0.5)
    last = (((1,), (1,)), ((), ()))
    scores = lax.dot_general(query, key, last, preferred_element_type=WIDE) * factor
    dual_scores = (
        lax.dot_general(
            jnp.concatenate([query_dual, query], axis=1),
            jnp.concatenate([key, key_dual], axis=1),
            last,
            preferred_element_type=WIDE,
        )
        * factor
    )
    raised = jnp.exp(scores - jnp.max(scores, axis=-1, keepdims=True))
    probs = raised * (1.0 / jnp.sum(raised, axis=-1, keepdims=True))
    spread = probs * (dual_scores - jnp.sum(probs * dual_scores, axis=-1, keepdims=True))
    probs_low = probs.astype(LOW)
    spread_low = spread.astype(LOW)
    out_ref[0] = jnp.dot(probs_low, value, preferred_element_type=WIDE).astype(LOW)
    out_ref[1] = (
        jnp.dot(probs_low, value_dual, preferred_element_type=WIDE)
        + jnp.dot(spread_low, value, preferred_element_type=WIDE)
    ).astype(LOW)


def attend(start, hdim, queries, keyed):
    rows = queries[0].shape[1]
    width = keyed[0].shape[2]
    first = start // hdim
    return pl.pallas_call(
        functools.partial(attend_kernel, len(queries)),
        grid=(width // hdim,),
        in_specs=[pl.BlockSpec((2, rows, hdim), lambda h: (0, 0, first + h))] * len(queries)
        + [pl.BlockSpec((array.shape[0], rows, hdim), lambda h: (0, 0, h)) for array in keyed],
        out_specs=pl.BlockSpec((2, len(queries) * rows, hdim), lambda h: (0, 0, h)),
        out_shape=jax.ShapeDtypeStruct((2, len(queries) * rows, width), LOW),
        compiler_params=params(),
        cost_estimate=LIGHT,
    )(*queries, *keyed)


def assemble_kernel(groups, chunks, flip_ref, *refs):
    part_refs, out_ref = refs[:-1], refs[-1]
    rows, group = out_ref.shape[0] // 8, out_ref.shape[1] // groups
    start = 0
    for at, width in enumerate(chunks):
        for g in range(groups):
            low, high = max(start, g * group), min(start + width, (g + 1) * group)
            if low >= high:
                continue
            to = pl.ds(pl.multiple_of((g ^ flip_ref[0]) * group + low - g * group, 128), high - low)
            for side in range(2):
                for kind in range(2):
                    for core in range(2):
                        first = (4 * core + 2 * side + kind) * rows
                        out_ref[first : first + rows, to] = part_refs[2 * at + side][
                            kind, core * rows : (core + 1) * rows, low - start : high - start
                        ]
        start += width


def assemble(flip, groups, chunks, pairs):
    rows = 4 * pairs[0][0].shape[1]
    return pl.pallas_call(
        functools.partial(assemble_kernel, groups, chunks),
        in_specs=[pl.BlockSpec(memory_space=pltpu.SMEM)] + vmem_specs(2 * len(pairs)),
        out_specs=vmem_specs(1)[0],
        out_shape=jax.ShapeDtypeStruct((rows, sum(chunks)), LOW),
        compiler_params=params(),
        cost_estimate=LIGHT,
    )(flip, *[part for pair in pairs for part in pair])


def project_kernel(spans, acts_ref, *refs):
    weight_refs = refs[:-4]
    keep_mine_ref, keep_other_ref, send_mine_ref, send_other_ref = refs[-4:]
    rows = keep_mine_ref.shape[0]
    weight = jnp.concatenate([ref[low:high] for ref, (low, high) in zip(weight_refs, spans)], axis=0)
    for at, out_ref in enumerate((keep_mine_ref, keep_other_ref, send_mine_ref, send_other_ref)):
        part = jnp.dot(acts_ref[at * rows : (at + 1) * rows], weight, preferred_element_type=WIDE)
        out_ref[...] = part.astype(out_ref.dtype)


def project(acts, pieces):
    weights = [weight for weight, _, _ in pieces]
    rows, n = acts.shape[0] // 4, weights[0].shape[1]
    return pl.pallas_call(
        functools.partial(project_kernel, [(low, high) for _, low, high in pieces]),
        in_specs=vmem_specs(1 + len(weights)),
        out_specs=vmem_specs(4),
        out_shape=[jax.ShapeDtypeStruct((rows, n), WIDE)] * 2 + [jax.ShapeDtypeStruct((rows, n), LOW)] * 2,
        compiler_params=params(),
        cost_estimate=LIGHT,
    )(acts, *weights)


def close_kernel(keep_ref, got_ref, out_ref):
    out_ref[...] = (keep_ref[...] + got_ref[...].astype(WIDE)).astype(LOW)


def close(keep, got):
    return pl.pallas_call(
        close_kernel,
        in_specs=vmem_specs(2),
        out_specs=vmem_specs(1)[0],
        out_shape=jax.ShapeDtypeStruct(keep.shape, LOW),
        compiler_params=params(),
        cost_estimate=LIGHT,
    )(keep, got)


def place_kernel(where_ref, keep_ref, got_ref, other_ref, *refs):
    plain_ref, dual_ref = refs[-2:]
    rows = plain_ref.shape[0]

    @pl.when(pl.program_id(0) == 0)
    def _():
        total = (keep_ref[...] + got_ref[...].astype(WIDE)).astype(LOW)
        plain_ref[...] = total[:rows]
        dual_ref[...] = total[rows:]

    @pl.when(pl.program_id(0) == 1)
    def _():
        plain_ref[...] = other_ref[:rows]
        dual_ref[...] = other_ref[rows:]


def place(outs, width, where, keep, got, other):
    rows, n = other.shape[0] // 2, other.shape[1]
    if n % 128:
        outs = outs or [jnp.zeros((rows, width), LOW)] * 2
        for side, piece in enumerate((close(keep, got), other)):
            parts = (piece[:rows], piece[rows:])
            outs = [lax.dynamic_update_slice(out, part, (0, where[side] * n)) for out, part in zip(outs, parts)]
        return outs
    full = pl.BlockSpec((2 * rows, n), lambda i, w: (0, 0))
    block = pl.BlockSpec((rows, n), lambda i, w: (0, w[i]))
    return pl.pallas_call(
        place_kernel,
        grid_spec=pltpu.PrefetchScalarGridSpec(
            num_scalar_prefetch=1,
            grid=(2,),
            in_specs=[full] * 3 + [pl.BlockSpec(memory_space=pl.ANY)] * len(outs),
            out_specs=[block] * 2,
        ),
        out_shape=[jax.ShapeDtypeStruct((rows, width), LOW)] * 2,
        input_output_aliases={4 + at: at for at in range(len(outs))},
        compiler_params=params(),
        cost_estimate=LIGHT,
    )(where, keep, got, other, *outs)


def body(
    n_dp,
    n_seq,
    queries,
    key_states,
    value_states,
    query_tangent,
    key_tangent,
    value_tangent,
    query_gain,
    key_gain,
    out_weight,
):
    dp = lax.axis_index("dp")
    seq = lax.axis_index("seq")
    n_ring = n_dp // 2
    groups = n_seq // 2
    features = queries.shape[1]
    hdim = features // HEADS
    group_heads = HEADS // n_seq
    few = group_heads * 2 // 5
    chunks = [group_heads * hdim] * (groups - 1) + [(group_heads - few) * hdim, few * hdim]
    starts = [sum(chunks[:at]) for at in range(len(chunks))]
    token = jnp.zeros((1,), jnp.int32)

    def far(array):
        return lax.ppermute(array, "seq", [(i, i ^ 2) for i in range(n_seq)])

    def near(array):
        return lax.ppermute(array, "seq", [(i, i ^ 1) for i in range(n_seq)])

    def across(array):
        return lax.ppermute(array, "dp", [(i, i ^ 1) for i in range(n_dp)])

    def onward(array):
        return lax.ppermute(array, "dp", [(i, (i + 2) % n_dp) for i in range(n_dp)])

    def wait(array):
        nonlocal token
        array, token = lax.optimization_barrier((array, token))
        return array

    def after(array):
        return lax.optimization_barrier((array, token))[0]

    def turn(ring, step):
        ring[step] = wait(ring[step])
        if step + 1 < n_ring:
            ring.append(onward(ring[step]))

    depth = out_weight.shape[0]
    cut = depth * 3 // 5 // 16 * 16
    upper, lower = [out_weight[:cut]], [out_weight[cut:]]
    lower.append(onward(lower[0]))
    upper.append(onward(upper[0]))
    beside = [wait(far(upper[0]))]
    beside.append(onward(beside[0]))
    turn(lower, 1)

    core = jnp.stack([seq % 2])
    arrays = (queries, key_states, value_states, query_tangent, key_tangent, value_tangent)
    packs = [wait(array) for array in pack(core, n_seq, chunks, arrays, jnp.stack([query_gain, key_gain]))]
    query_own, *keyed_own = packs[: 1 + len(chunks)]
    query_other, *keyed_other = packs[1 + len(chunks) :]
    there = wait(near(keyed_other[0]))
    keyed = [[keyed_own[0], there, far(keyed_own[0]), far(there)]]
    for own, other in zip(keyed_own[1:], keyed_other[1:]):
        there = wait(near(other))
        keyed.append([own, there, far(jnp.concatenate([own, there]))])
    queries_both = [query_own, wait(near(query_other))]
    turn(lower, 2)

    acts, swapped = [], []

    def attention(chunk):
        keyed[chunk][-1] = wait(keyed[chunk][-1])
        acts.append(wait(attend(starts[chunk], hdim, queries_both, keyed[chunk])))
        swapped.append(across(acts[-1]))

    turn(upper, 1)
    keyed[0][2] = wait(keyed[0][2])
    turn(beside, 1)
    attention(0)
    for step in range(3, n_ring):
        turn(lower, step)
    later = [wait(jnp.concatenate(lower[step : step + 2])) for step in range(2, n_ring, 2)]
    turn(upper, 2)
    rest = [far(after(lower[0]))]
    attention(1)
    swapped[0] = wait(swapped[0])
    swapped[1] = wait(swapped[1])
    attention(2)
    turn(beside, 2)
    rest += [far(after(piece)) for piece in lower[1:2] + later]
    for step in range(3, n_ring):
        turn(upper, step)
    rest[0] = wait(rest[0])
    swapped[2] = wait(swapped[2])
    acts = wait(assemble(jnp.stack([seq // 2]), groups, chunks, list(zip(acts, swapped))))

    keeps, mine_sends, sends, mine_got, other = [], [], [], [], []

    def columns(step):
        own = [(upper[step], 0, cut), (lower[step], 0, depth - cut)]
        start = step % 2 * (depth - cut) if step > 1 else 0
        got = rest[step] if step < 2 else rest[1 + step // 2]
        theirs = [(beside[step], 0, cut), (got, start, start + depth - cut)]
        keep_mine, keep_other, send_mine, send_other = project(acts, own + theirs)
        keeps.append((keep_mine, keep_other))
        sends.append(near(wait(send_other)))
        mine_sends.append(send_mine)

    def finish(step):
        other.append(across(wait(close(keeps[step][1], wait(sends[step])))))
        mine_got.append(near(mine_sends[step]))

    outs = []

    def put(step):
        pair = (dp // 2 - step) % n_ring
        where = jnp.stack([2 * pair + dp % 2, 2 * pair + 1 - dp % 2]).astype(jnp.int32) + token
        return place(outs, n_dp * out_weight.shape[1], where, keeps[step][0], wait(mine_got[step]), wait(other[step]))

    columns(0)
    rest[1] = wait(rest[1])
    columns(1)
    finish(0)
    finish(1)
    for step in range(2, n_ring, 2):
        for ahead in range(max(step, 3), step + 2):
            turn(beside, ahead)
        rest[1 + step // 2] = wait(rest[1 + step // 2])
        columns(step)
        outs = put(step - 2)
        finish(step)
        columns(step + 1)
        outs = put(step - 1)
        finish(step + 1)
    for step in range(n_ring - 2, n_ring):
        outs = put(step)
    return tuple(outs)


def solution(mesh):
    rows = P(("dp", "seq"), None)
    return jax.shard_map(
        functools.partial(body, mesh.shape["dp"], mesh.shape["seq"]),
        mesh=mesh,
        in_specs=(rows,) * 6 + (P(), P(), P("seq", "dp")),
        out_specs=(rows, rows),
        check_vma=False,
    )
```

```python
import functools

import jax
import jax.numpy as jnp
from jax import lax
from jax.experimental import pallas as pl
from jax.experimental.pallas import tpu as pltpu
from jax.sharding import PartitionSpec as P

HEADS = 20
EPS = 1e-06
VMEM_BYTES = 16 * 1024 * 1024
ROW_STEP = 32

LOW = jnp.bfloat16
WIDE = jnp.float32
LIGHT = pl.CostEstimate(flops=1, transcendentals=0, bytes_accessed=1)


def params():
    return pltpu.CompilerParams(vmem_limit_bytes=VMEM_BYTES)


def vmem_specs(count):
    return [pl.BlockSpec(memory_space=pltpu.VMEM)] * count


def pack_kernel(n_seq, chunks, core_ref, *refs):
    query_ref, key_ref, value_ref, dquery_ref, dkey_ref, dvalue_ref, gains_ref = refs[:7]
    out_refs = refs[7:]
    n_chunks = len(chunks)
    group = query_ref.shape[-1] // n_seq

    def statistics(primal_ref, tangent_ref):
        primal = primal_ref[...].astype(WIDE)
        tangent = tangent_ref[...].astype(WIDE)
        inverse = lax.rsqrt(jnp.mean(primal * primal, axis=-1, keepdims=True) + EPS)
        across = jnp.mean(primal * tangent, axis=-1, keepdims=True)
        return inverse, inverse * inverse * inverse * across

    query_stats = statistics(query_ref, dquery_ref)
    key_stats = statistics(key_ref, dkey_ref)

    def normed(primal_ref, tangent_ref, which, stats, lanes):
        primal = primal_ref[:, lanes].astype(WIDE)
        tangent = tangent_ref[:, lanes].astype(WIDE)
        gain = gains_ref[which : which + 1, lanes]
        inverse, slope = stats
        return (primal * inverse * gain).astype(LOW), (gain * (tangent * inverse - primal * slope)).astype(LOW)

    for side in range(2):
        core = core_ref[0] if side == 0 else 1 - core_ref[0]
        queries_ref, *keyed_refs = out_refs[side * (1 + n_chunks) : (side + 1) * (1 + n_chunks)]
        for at in range(n_seq // 2):
            lanes = pl.ds(pl.multiple_of((2 * at + core) * group, 128), group)
            here = slice(at * group, (at + 1) * group)
            plain, dual = normed(query_ref, dquery_ref, 0, query_stats, lanes)
            queries_ref[0, :, here] = plain
            queries_ref[1, :, here] = dual
            four = normed(key_ref, dkey_ref, 1, key_stats, lanes)
            four += (value_ref[:, lanes], dvalue_ref[:, lanes])
            start = 0
            for keyed_ref, width in zip(keyed_refs, chunks):
                low, high = max(start, here.start), min(start + width, here.stop)
                if low < high:
                    for which, part in enumerate(four):
                        keyed_ref[which, :, low - start : high - start] = part[:, low - here.start : high - here.start]
                start += width


def pack(core, n_seq, chunks, arrays, gains):
    rows, features = arrays[0].shape
    step = min(rows, ROW_STEP)
    row_block = pl.BlockSpec((step, features), lambda i, c: (i, 0))
    gain_block = pl.BlockSpec((2, features), lambda i, c: (0, 0))
    kinds = [(2, features // 2)] + [(4, width) for width in chunks]
    kinds = kinds + kinds
    return pl.pallas_call(
        functools.partial(pack_kernel, n_seq, chunks),
        grid_spec=pltpu.PrefetchScalarGridSpec(
            num_scalar_prefetch=1,
            grid=(rows // step,),
            in_specs=[row_block] * 6 + [gain_block],
            out_specs=[pl.BlockSpec((count, step, width), lambda i, c: (0, i, 0)) for count, width in kinds],
        ),
        out_shape=[jax.ShapeDtypeStruct((count, rows, width), LOW) for count, width in kinds],
        compiler_params=params(),
        cost_estimate=LIGHT,
    )(core, *arrays, gains)


def attend_kernel(n_queries, *refs):
    query_refs, keyed_refs, out_ref = refs[:n_queries], refs[n_queries:-1], refs[-1]

    def stack(which, some_refs, kinds):
        parts = [ref[at] for ref in some_refs for at in range(which, ref.shape[0], kinds)]
        return jnp.concatenate(parts, axis=0)

    query, query_dual = (stack(which, query_refs, 2) for which in range(2))
    key, key_dual, value, value_dual = (stack(which, keyed_refs, 4) for which in range(4))
    factor = query.shape[-1] ** (-0.5)
    last = (((1,), (1,)), ((), ()))
    scores = lax.dot_general(query, key, last, preferred_element_type=WIDE) * factor
    dual_scores = (
        lax.dot_general(
            jnp.concatenate([query_dual, query], axis=1),
            jnp.concatenate([key, key_dual], axis=1),
            last,
            preferred_element_type=WIDE,
        )
        * factor
    )
    raised = jnp.exp(scores - jnp.max(scores, axis=-1, keepdims=True))
    probs = raised * (1.0 / jnp.sum(raised, axis=-1, keepdims=True))
    spread = probs * (dual_scores - jnp.sum(probs * dual_scores, axis=-1, keepdims=True))
    probs_low = probs.astype(LOW)
    spread_low = spread.astype(LOW)
    out_ref[0] = jnp.dot(probs_low, value, preferred_element_type=WIDE).astype(LOW)
    out_ref[1] = (
        jnp.dot(probs_low, value_dual, preferred_element_type=WIDE)
        + jnp.dot(spread_low, value, preferred_element_type=WIDE)
    ).astype(LOW)


def attend(start, hdim, queries, keyed):
    rows = queries[0].shape[1]
    width = keyed[0].shape[2]
    first = start // hdim
    return pl.pallas_call(
        functools.partial(attend_kernel, len(queries)),
        grid=(width // hdim,),
        in_specs=[pl.BlockSpec((2, rows, hdim), lambda h: (0, 0, first + h))] * len(queries)
        + [pl.BlockSpec((array.shape[0], rows, hdim), lambda h: (0, 0, h)) for array in keyed],
        out_specs=pl.BlockSpec((2, len(queries) * rows, hdim), lambda h: (0, 0, h)),
        out_shape=jax.ShapeDtypeStruct((2, len(queries) * rows, width), LOW),
        compiler_params=params(),
        cost_estimate=LIGHT,
    )(*queries, *keyed)


def project_kernel(n_chunks, spans, flip_ref, *refs):
    sides = refs[:n_chunks], refs[n_chunks : 2 * n_chunks]
    weight_refs, out_refs, weight_ref = refs[2 * n_chunks : -6], refs[-6:-1], refs[-1]
    rows = out_refs[0].shape[0] // 2
    depth = weight_ref.shape[0] // 2
    at = 0
    for ref, (low, high) in zip(weight_refs, spans):
        block, inside = at // depth, at % depth
        first = pl.multiple_of((block ^ flip_ref[0]) * depth + inside, 16)
        weight_ref[pl.ds(first, high - low)] = ref[low:high]
        at += high - low
    weight = weight_ref[...]
    for side, parts in enumerate(sides):
        acts = jnp.concatenate([ref[...].reshape(4 * rows, ref.shape[-1]) for ref in parts], axis=1)
        total = jnp.dot(acts, weight, preferred_element_type=WIDE)
        for kind in range(2):
            first = 2 * kind * rows
            here = slice(kind * rows, (kind + 1) * rows)
            out_refs[side][here] = total[first : first + rows]
            low = total[first + rows : first + 2 * rows].astype(LOW)
            if side:
                out_refs[3 + kind][...] = low
            else:
                out_refs[2][here] = low


def project(flip, acts, pieces):
    mine, theirs = zip(*acts)
    weights = [weight for weight, _, _ in pieces]
    spans = [(low, high) for _, low, high in pieces]
    rows, n = mine[0].shape[1], weights[0].shape[1]
    depth = sum(high - low for low, high in spans)
    return pl.pallas_call(
        functools.partial(project_kernel, len(acts), spans),
        in_specs=[pl.BlockSpec(memory_space=pltpu.SMEM)] + vmem_specs(2 * len(acts) + len(weights)),
        out_specs=vmem_specs(5),
        out_shape=[jax.ShapeDtypeStruct((rows, n), WIDE)] * 2
        + [jax.ShapeDtypeStruct((rows, n), LOW)]
        + [jax.ShapeDtypeStruct((rows // 2, n), LOW)] * 2,
        scratch_shapes=[pltpu.VMEM((depth, n), LOW)],
        compiler_params=params(),
        cost_estimate=pl.CostEstimate(flops=8 * rows * depth * pl.cdiv(n, 256) * 256, transcendentals=0, bytes_accessed=1),
    )(flip, *mine, *theirs, *weights)


def close_kernel(keep_ref, *refs):
    got_refs, out_ref = refs[:-1], refs[-1]
    first = 0
    for got_ref in got_refs:
        here = slice(first, first + got_ref.shape[0])
        out_ref[here] = (keep_ref[here] + got_ref[...].astype(WIDE)).astype(LOW)
        first = here.stop


def close(keep, *gots):
    return pl.pallas_call(
        close_kernel,
        in_specs=vmem_specs(1 + len(gots)),
        out_specs=vmem_specs(1)[0],
        out_shape=jax.ShapeDtypeStruct(keep.shape, LOW),
        compiler_params=params(),
        cost_estimate=LIGHT,
    )(keep, *gots)


def place_kernel(where_ref, keep_ref, got_ref, other_ref, *refs):
    plain_ref, dual_ref = refs[-2:]
    rows = plain_ref.shape[0]

    @pl.when(pl.program_id(0) == 0)
    def _():
        total = (keep_ref[...] + got_ref[...].astype(WIDE)).astype(LOW)
        plain_ref[...] = total[:rows]
        dual_ref[...] = total[rows:]

    @pl.when(pl.program_id(0) == 1)
    def _():
        plain_ref[...] = other_ref[:rows]
        dual_ref[...] = other_ref[rows:]


def place(outs, width, where, keep, got, other):
    rows, n = other.shape[0] // 2, other.shape[1]
    if n % 128:
        outs = outs or [jnp.zeros((rows, width), LOW)] * 2
        for side, piece in enumerate((close(keep, got), other)):
            parts = (piece[:rows], piece[rows:])
            outs = [lax.dynamic_update_slice(out, part, (0, where[side] * n)) for out, part in zip(outs, parts)]
        return outs
    full = pl.BlockSpec((2 * rows, n), lambda i, w: (0, 0))
    block = pl.BlockSpec((rows, n), lambda i, w: (0, w[i]))
    return pl.pallas_call(
        place_kernel,
        grid_spec=pltpu.PrefetchScalarGridSpec(
            num_scalar_prefetch=1,
            grid=(2,),
            in_specs=[full] * 3 + [pl.BlockSpec(memory_space=pl.ANY)] * len(outs),
            out_specs=[block] * 2,
        ),
        out_shape=[jax.ShapeDtypeStruct((rows, width), LOW)] * 2,
        input_output_aliases={4 + at: at for at in range(len(outs))},
        compiler_params=params(),
        cost_estimate=LIGHT,
    )(where, keep, got, other, *outs)


def body(
    n_dp,
    n_seq,
    queries,
    key_states,
    value_states,
    query_tangent,
    key_tangent,
    value_tangent,
    query_gain,
    key_gain,
    out_weight,
):
    dp = lax.axis_index("dp")
    seq = lax.axis_index("seq")
    n_ring = n_dp // 2
    groups = n_seq // 2
    features = queries.shape[1]
    hdim = features // HEADS
    group_heads = HEADS // n_seq
    few = group_heads * 2 // 5
    chunks = [group_heads * hdim] * (groups - 1) + [(group_heads - few) * hdim, few * hdim]
    starts = [sum(chunks[:at]) for at in range(len(chunks))]
    token = jnp.zeros((1,), jnp.int32)

    def far(array):
        return lax.ppermute(array, "seq", [(i, i ^ 2) for i in range(n_seq)])

    def near(array):
        return lax.ppermute(array, "seq", [(i, i ^ 1) for i in range(n_seq)])

    def across(array):
        return lax.ppermute(array, "dp", [(i, i ^ 1) for i in range(n_dp)])

    def onward(array):
        return lax.ppermute(array, "dp", [(i, (i + 2) % n_dp) for i in range(n_dp)])

    def wait(array):
        nonlocal token
        array, token = lax.optimization_barrier((array, token))
        return array

    def after(array):
        return lax.optimization_barrier((array, token))[0]

    def turn(ring, step):
        ring[step] = wait(ring[step])
        if step + 1 < n_ring:
            ring.append(onward(ring[step]))

    depth = out_weight.shape[0]
    cut = depth * 3 // 5 // 16 * 16
    upper, lower = [out_weight[:cut]], [out_weight[cut:]]
    lower.append(onward(lower[0]))
    upper.append(onward(upper[0]))
    beside = [wait(far(upper[0]))]
    beside.append(onward(beside[0]))
    turn(lower, 1)

    core = jnp.stack([seq % 2])
    arrays = (queries, key_states, value_states, query_tangent, key_tangent, value_tangent)
    packs = [wait(array) for array in pack(core, n_seq, chunks, arrays, jnp.stack([query_gain, key_gain]))]
    query_own, *keyed_own = packs[: 1 + len(chunks)]
    query_other, *keyed_other = packs[1 + len(chunks) :]
    there = wait(near(keyed_other[0]))
    keyed = [[keyed_own[0], there, far(keyed_own[0]), far(there)]]
    turn(lower, 2)

    acts, swapped = [], []

    def attention(chunk):
        keyed[chunk][-1] = wait(keyed[chunk][-1])
        acts.append(wait(attend(starts[chunk], hdim, queries_both, keyed[chunk])))
        swapped.append(across(acts[-1]))

    turn(upper, 1)
    keyed[0][2] = wait(keyed[0][2])
    for own, other in zip(keyed_own[1:], keyed_other[1:]):
        there = wait(near(other))
        keyed.append([own, there, far(jnp.concatenate([own, there]))])
    queries_both = [query_own, wait(near(query_other))]
    turn(beside, 1)
    attention(0)
    for step in range(3, n_ring):
        turn(lower, step)
    later = [wait(jnp.concatenate(lower[step : step + 2])) for step in range(2, n_ring, 2)]
    turn(upper, 2)
    rest = [far(after(lower[0]))]
    attention(1)
    swapped[0] = wait(swapped[0])
    attention(2)
    swapped[1] = wait(swapped[1])
    turn(beside, 2)
    rest.append(far(after(lower[1])))
    for step in range(3, n_ring):
        turn(upper, step)
    rest[0] = wait(rest[0])
    swapped[2] = wait(swapped[2])
    rest += [far(after(piece)) for piece in later]
    acts = list(zip(acts, swapped))
    flip = jnp.stack([seq // 2])

    keeps, mine_sends, sends, mine_got, other = [], [], [], [], []

    def columns(step):
        own = [(upper[step], 0, cut), (lower[step], 0, depth - cut)]
        start = step % 2 * (depth - cut) if step > 1 else 0
        got = rest[step] if step < 2 else rest[1 + step // 2]
        theirs = [(beside[step], 0, cut), (got, start, start + depth - cut)]
        keep_mine, keep_other, send_mine, *send_other = project(flip, acts, own + theirs)
        keeps.append((keep_mine, keep_other))
        sends.append([near(wait(array)) for array in send_other])
        mine_sends.append(send_mine)

    def finish(step):
        other.append(across(wait(close(keeps[step][1], *[wait(array) for array in sends[step]]))))
        mine_got.append(near(mine_sends[step]))

    columns(0)
    finish(0)
    rest[1] = wait(rest[1])
    columns(1)
    finish(1)
    for step in range(2, n_ring, 2):
        other[step - 2] = wait(other[step - 2])
        rest[1 + step // 2] = wait(rest[1 + step // 2])
        for ahead in range(max(step, 3), step + 2):
            turn(beside, ahead)
        columns(step)
        finish(step)
        columns(step + 1)
        other[step - 1] = wait(other[step - 1])
        finish(step + 1)
    outs = []
    for step in range(n_ring):
        pair = (dp // 2 - step) % n_ring
        where = jnp.stack([2 * pair + dp % 2, 2 * pair + 1 - dp % 2]).astype(jnp.int32) + token
        mine_got[step] = wait(mine_got[step])
        if step + 2 >= n_ring:
            other[step] = wait(other[step])
        outs = place(outs, n_dp * out_weight.shape[1], where, keeps[step][0], mine_got[step], other[step])
    return tuple(outs)


def solution(mesh):
    rows = P(("dp", "seq"), None)
    return jax.shard_map(
        functools.partial(body, mesh.shape["dp"], mesh.shape["seq"]),
        mesh=mesh,
        in_specs=(rows,) * 6 + (P(), P(), P("seq", "dp")),
        out_specs=(rows, rows),
        check_vma=False,
    )
```

```python
import functools

import jax
import jax.numpy as jnp
from jax import lax
from jax.experimental import pallas as pl
from jax.experimental.pallas import tpu as pltpu
from jax.sharding import PartitionSpec as P

HEADS = 20
EPS = 1e-06
VMEM_BYTES = 16 * 1024 * 1024
ROW_STEP = 32

LOW = jnp.bfloat16
WIDE = jnp.float32
LIGHT = pl.CostEstimate(flops=1, transcendentals=0, bytes_accessed=1)


def params():
    return pltpu.CompilerParams(vmem_limit_bytes=VMEM_BYTES)


def vmem_specs(count):
    return [pl.BlockSpec(memory_space=pltpu.VMEM)] * count


def pack_kernel(n_seq, chunks, core_ref, *refs):
    query_ref, key_ref, value_ref, dquery_ref, dkey_ref, dvalue_ref, gains_ref = refs[:7]
    out_refs = refs[7:]
    n_chunks = len(chunks)
    group = query_ref.shape[-1] // n_seq

    def statistics(primal_ref, tangent_ref):
        primal = primal_ref[...].astype(WIDE)
        tangent = tangent_ref[...].astype(WIDE)
        inverse = lax.rsqrt(jnp.mean(primal * primal, axis=-1, keepdims=True) + EPS)
        across = jnp.mean(primal * tangent, axis=-1, keepdims=True)
        return inverse, inverse * inverse * inverse * across

    query_stats = statistics(query_ref, dquery_ref)
    key_stats = statistics(key_ref, dkey_ref)

    def normed(primal_ref, tangent_ref, which, stats, lanes):
        primal = primal_ref[:, lanes].astype(WIDE)
        tangent = tangent_ref[:, lanes].astype(WIDE)
        gain = gains_ref[which : which + 1, lanes]
        inverse, slope = stats
        return (primal * inverse * gain).astype(LOW), (gain * (tangent * inverse - primal * slope)).astype(LOW)

    for side in range(2):
        core = core_ref[0] if side == 0 else 1 - core_ref[0]
        queries_ref, *keyed_refs = out_refs[side * (1 + n_chunks) : (side + 1) * (1 + n_chunks)]
        for at in range(n_seq // 2):
            lanes = pl.ds(pl.multiple_of((2 * at + core) * group, 128), group)
            here = slice(at * group, (at + 1) * group)
            plain, dual = normed(query_ref, dquery_ref, 0, query_stats, lanes)
            queries_ref[0, :, here] = plain
            queries_ref[1, :, here] = dual
            four = normed(key_ref, dkey_ref, 1, key_stats, lanes)
            four += (value_ref[:, lanes], dvalue_ref[:, lanes])
            start = 0
            for keyed_ref, width in zip(keyed_refs, chunks):
                low, high = max(start, here.start), min(start + width, here.stop)
                if low < high:
                    for which, part in enumerate(four):
                        keyed_ref[which, :, low - start : high - start] = part[:, low - here.start : high - here.start]
                start += width


def pack(core, n_seq, chunks, arrays, gains):
    rows, features = arrays[0].shape
    step = min(rows, ROW_STEP)
    row_block = pl.BlockSpec((step, features), lambda i, c: (i, 0))
    gain_block = pl.BlockSpec((2, features), lambda i, c: (0, 0))
    kinds = [(2, features // 2)] + [(4, width) for width in chunks]
    kinds = kinds + kinds
    return pl.pallas_call(
        functools.partial(pack_kernel, n_seq, chunks),
        grid_spec=pltpu.PrefetchScalarGridSpec(
            num_scalar_prefetch=1,
            grid=(rows // step,),
            in_specs=[row_block] * 6 + [gain_block],
            out_specs=[pl.BlockSpec((count, step, width), lambda i, c: (0, i, 0)) for count, width in kinds],
        ),
        out_shape=[jax.ShapeDtypeStruct((count, rows, width), LOW) for count, width in kinds],
        compiler_params=params(),
        cost_estimate=LIGHT,
    )(core, *arrays, gains)


def attend_kernel(n_queries, *refs):
    query_refs, keyed_refs, out_ref = refs[:n_queries], refs[n_queries:-1], refs[-1]

    def stack(which, some_refs, kinds):
        parts = [ref[at] for ref in some_refs for at in range(which, ref.shape[0], kinds)]
        return jnp.concatenate(parts, axis=0)

    query, query_dual = (stack(which, query_refs, 2) for which in range(2))
    key, key_dual, value, value_dual = (stack(which, keyed_refs, 4) for which in range(4))
    factor = query.shape[-1] ** (-0.5)
    last = (((1,), (1,)), ((), ()))
    scores = lax.dot_general(query, key, last, preferred_element_type=WIDE) * factor
    dual_scores = (
        lax.dot_general(
            jnp.concatenate([query_dual, query], axis=1),
            jnp.concatenate([key, key_dual], axis=1),
            last,
            preferred_element_type=WIDE,
        )
        * factor
    )
    raised = jnp.exp(scores - jnp.max(scores, axis=-1, keepdims=True))
    probs = raised * (1.0 / jnp.sum(raised, axis=-1, keepdims=True))
    spread = probs * (dual_scores - jnp.sum(probs * dual_scores, axis=-1, keepdims=True))
    probs_low = probs.astype(LOW)
    spread_low = spread.astype(LOW)
    out_ref[0] = jnp.dot(probs_low, value, preferred_element_type=WIDE).astype(LOW)
    out_ref[1] = (
        jnp.dot(probs_low, value_dual, preferred_element_type=WIDE)
        + jnp.dot(spread_low, value, preferred_element_type=WIDE)
    ).astype(LOW)


def attend(start, hdim, queries, keyed):
    rows = queries[0].shape[1]
    width = keyed[0].shape[2]
    first = start // hdim
    return pl.pallas_call(
        functools.partial(attend_kernel, len(queries)),
        grid=(width // hdim,),
        in_specs=[pl.BlockSpec((2, rows, hdim), lambda h: (0, 0, first + h))] * len(queries)
        + [pl.BlockSpec((array.shape[0], rows, hdim), lambda h: (0, 0, h)) for array in keyed],
        out_specs=pl.BlockSpec((2, len(queries) * rows, hdim), lambda h: (0, 0, h)),
        out_shape=jax.ShapeDtypeStruct((2, len(queries) * rows, width), LOW),
        compiler_params=params(),
        cost_estimate=LIGHT,
    )(*queries, *keyed)


def project_kernel(n_chunks, spans, flip_ref, *refs):
    sides = refs[:n_chunks], refs[n_chunks : 2 * n_chunks]
    weight_refs = refs[2 * n_chunks : -7]
    keep_mine_ref, keep_other_ref, send_mine_ref, first_ref, second_ref, weight_ref, send_other_ref = refs[-7:]
    rows = first_ref.shape[0]
    depth = weight_ref.shape[0] // 2
    at = 0
    for ref, (low, high) in zip(weight_refs, spans):
        block, inside = at // depth, at % depth
        first = pl.multiple_of((block ^ flip_ref[0]) * depth + inside, 16)
        weight_ref[pl.ds(first, high - low)] = ref[low:high]
        at += high - low

    def one(kind, _):
        acts = [jnp.concatenate([ref[kind] for ref in parts], axis=1) for parts in sides]
        total = jnp.dot(jnp.concatenate(acts), weight_ref[...], preferred_element_type=WIDE)
        here = pl.ds(pl.multiple_of(kind * rows, rows), rows)
        keep_mine_ref[here] = total[:rows]
        send_mine_ref[here] = total[rows : 2 * rows].astype(LOW)
        keep_other_ref[here] = total[2 * rows : 3 * rows]
        send_other_ref[kind] = total[3 * rows :].astype(LOW)
        return 0

    lax.fori_loop(0, 2, one, 0)
    first_ref[...] = send_other_ref[0]
    second_ref[...] = send_other_ref[1]


def project(flip, acts, pieces):
    mine, theirs = zip(*acts)
    weights = [weight for weight, _, _ in pieces]
    spans = [(low, high) for _, low, high in pieces]
    rows, n = mine[0].shape[1], weights[0].shape[1]
    depth = sum(high - low for low, high in spans)
    return pl.pallas_call(
        functools.partial(project_kernel, len(acts), spans),
        in_specs=[pl.BlockSpec(memory_space=pltpu.SMEM)] + vmem_specs(2 * len(acts) + len(weights)),
        out_specs=vmem_specs(5),
        out_shape=[jax.ShapeDtypeStruct((rows, n), WIDE)] * 2
        + [jax.ShapeDtypeStruct((rows, n), LOW)]
        + [jax.ShapeDtypeStruct((rows // 2, n), LOW)] * 2,
        scratch_shapes=[pltpu.VMEM((depth, n), LOW), pltpu.VMEM((2, rows // 2, n), LOW)],
        compiler_params=params(),
        cost_estimate=pl.CostEstimate(flops=8 * rows * depth * pl.cdiv(n, 256) * 256, transcendentals=0, bytes_accessed=1),
    )(flip, *mine, *theirs, *weights)


def close_kernel(keep_ref, *refs):
    got_refs, out_ref = refs[:-1], refs[-1]
    first = 0
    for got_ref in got_refs:
        here = slice(first, first + got_ref.shape[0])
        out_ref[here] = (keep_ref[here] + got_ref[...].astype(WIDE)).astype(LOW)
        first = here.stop


def close(keep, *gots):
    return pl.pallas_call(
        close_kernel,
        in_specs=vmem_specs(1 + len(gots)),
        out_specs=vmem_specs(1)[0],
        out_shape=jax.ShapeDtypeStruct(keep.shape, LOW),
        compiler_params=params(),
        cost_estimate=LIGHT,
    )(keep, *gots)


def place_kernel(where_ref, keep_ref, got_ref, other_ref, *refs):
    plain_ref, dual_ref = refs[-2:]
    rows = plain_ref.shape[0]

    @pl.when(pl.program_id(0) == 0)
    def _():
        total = (keep_ref[...] + got_ref[...].astype(WIDE)).astype(LOW)
        plain_ref[...] = total[:rows]
        dual_ref[...] = total[rows:]

    @pl.when(pl.program_id(0) == 1)
    def _():
        plain_ref[...] = other_ref[:rows]
        dual_ref[...] = other_ref[rows:]


def place(outs, width, where, keep, got, other):
    rows, n = other.shape[0] // 2, other.shape[1]
    if n % 128:
        outs = outs or [jnp.zeros((rows, width), LOW)] * 2
        for side, piece in enumerate((close(keep, got), other)):
            parts = (piece[:rows], piece[rows:])
            outs = [lax.dynamic_update_slice(out, part, (0, where[side] * n)) for out, part in zip(outs, parts)]
        return outs
    full = pl.BlockSpec((2 * rows, n), lambda i, w: (0, 0))
    block = pl.BlockSpec((rows, n), lambda i, w: (0, w[i]))
    return pl.pallas_call(
        place_kernel,
        grid_spec=pltpu.PrefetchScalarGridSpec(
            num_scalar_prefetch=1,
            grid=(2,),
            in_specs=[full] * 3 + [pl.BlockSpec(memory_space=pl.ANY)] * len(outs),
            out_specs=[block] * 2,
        ),
        out_shape=[jax.ShapeDtypeStruct((rows, width), LOW)] * 2,
        input_output_aliases={4 + at: at for at in range(len(outs))},
        compiler_params=params(),
        cost_estimate=LIGHT,
    )(where, keep, got, other, *outs)


def body(
    n_dp,
    n_seq,
    queries,
    key_states,
    value_states,
    query_tangent,
    key_tangent,
    value_tangent,
    query_gain,
    key_gain,
    out_weight,
):
    dp = lax.axis_index("dp")
    seq = lax.axis_index("seq")
    n_ring = n_dp // 2
    groups = n_seq // 2
    features = queries.shape[1]
    hdim = features // HEADS
    group_heads = HEADS // n_seq
    few = group_heads * 2 // 5
    chunks = [group_heads * hdim] * (groups - 1) + [(group_heads - few) * hdim, few * hdim]
    starts = [sum(chunks[:at]) for at in range(len(chunks))]
    token = jnp.zeros((1,), jnp.int32)

    def far(array):
        return lax.ppermute(array, "seq", [(i, i ^ 2) for i in range(n_seq)])

    def near(array):
        return lax.ppermute(array, "seq", [(i, i ^ 1) for i in range(n_seq)])

    def across(array):
        return lax.ppermute(array, "dp", [(i, i ^ 1) for i in range(n_dp)])

    def onward(array):
        return lax.ppermute(array, "dp", [(i, (i + 2) % n_dp) for i in range(n_dp)])

    def wait(array):
        nonlocal token
        array, token = lax.optimization_barrier((array, token))
        return array

    def after(array):
        return lax.optimization_barrier((array, token))[0]

    def turn(ring, step):
        ring[step] = wait(ring[step])
        if step + 1 < n_ring:
            ring.append(onward(ring[step]))

    depth = out_weight.shape[0]
    cut = depth * 3 // 5 // 16 * 16
    upper, lower = [out_weight[:cut]], [out_weight[cut:]]
    lower.append(onward(lower[0]))
    upper.append(onward(upper[0]))
    beside = [wait(far(upper[0]))]
    beside.append(onward(beside[0]))
    turn(lower, 1)

    core = jnp.stack([seq % 2])
    arrays = (queries, key_states, value_states, query_tangent, key_tangent, value_tangent)
    packs = [wait(array) for array in pack(core, n_seq, chunks, arrays, jnp.stack([query_gain, key_gain]))]
    query_own, *keyed_own = packs[: 1 + len(chunks)]
    query_other, *keyed_other = packs[1 + len(chunks) :]
    there = wait(near(keyed_other[0]))
    keyed = [[keyed_own[0], there, far(keyed_own[0]), far(there)]]
    for own, other in zip(keyed_own[1:], keyed_other[1:]):
        there = wait(near(other))
        keyed.append([own, there, far(jnp.concatenate([own, there]))])
    queries_both = [query_own, wait(near(query_other))]
    turn(lower, 2)

    acts, swapped = [], []

    def attention(chunk):
        keyed[chunk][-1] = wait(keyed[chunk][-1])
        acts.append(wait(attend(starts[chunk], hdim, queries_both, keyed[chunk])))
        swapped.append(across(acts[-1]))

    turn(upper, 1)
    keyed[0][2] = wait(keyed[0][2])
    turn(beside, 1)
    attention(0)
    for step in range(3, n_ring):
        turn(lower, step)
    later = [wait(jnp.concatenate(lower[step : step + 2])) for step in range(2, n_ring, 2)]
    turn(upper, 2)
    rest = [far(after(lower[0]))]
    attention(1)
    swapped[0] = wait(swapped[0])
    swapped[1] = wait(swapped[1])
    attention(2)
    turn(beside, 2)
    rest.append(far(after(lower[1])))
    for step in range(3, n_ring):
        turn(upper, step)
    rest[0] = wait(rest[0])
    swapped[2] = wait(swapped[2])
    rest += [far(after(piece)) for piece in later]
    acts = list(zip(acts, swapped))
    flip = jnp.stack([seq // 2])

    keeps, mine_sends, sends, mine_got, other = [], [], [], [], []

    def columns(step):
        own = [(upper[step], 0, cut), (lower[step], 0, depth - cut)]
        start = step % 2 * (depth - cut) if step > 1 else 0
        got = rest[step] if step < 2 else rest[1 + step // 2]
        theirs = [(beside[step], 0, cut), (got, start, start + depth - cut)]
        keep_mine, keep_other, send_mine, *send_other = project(flip, acts, own + theirs)
        keeps.append((keep_mine, keep_other))
        sends.append([near(wait(array)) for array in send_other])
        mine_sends.append(send_mine)

    def finish(step):
        other.append(across(wait(close(keeps[step][1], *[wait(array) for array in sends[step]]))))
        mine_got.append(near(mine_sends[step]))

    columns(0)
    finish(0)
    rest[1] = wait(rest[1])
    columns(1)
    finish(1)
    for step in range(2, n_ring, 2):
        other[step - 2] = wait(other[step - 2])
        rest[1 + step // 2] = wait(rest[1 + step // 2])
        for ahead in range(max(step, 3), step + 2):
            turn(beside, ahead)
        columns(step)
        finish(step)
        columns(step + 1)
        other[step - 1] = wait(other[step - 1])
        finish(step + 1)
    outs = []
    for step in range(n_ring):
        pair = (dp // 2 - step) % n_ring
        where = jnp.stack([2 * pair + dp % 2, 2 * pair + 1 - dp % 2]).astype(jnp.int32) + token
        mine_got[step] = wait(mine_got[step])
        if step + 2 >= n_ring:
            other[step] = wait(other[step])
        outs = place(outs, n_dp * out_weight.shape[1], where, keeps[step][0], mine_got[step], other[step])
    return tuple(outs)


def solution(mesh):
    rows = P(("dp", "seq"), None)
    return jax.shard_map(
        functools.partial(body, mesh.shape["dp"], mesh.shape["seq"]),
        mesh=mesh,
        in_specs=(rows,) * 6 + (P(), P(), P("seq", "dp")),
        out_specs=(rows, rows),
        check_vma=False,
    )
```

```python
import functools

import jax
import jax.numpy as jnp
from jax import lax
from jax.experimental import pallas as pl
from jax.experimental.pallas import tpu as pltpu
from jax.sharding import PartitionSpec as P

HEADS = 20
EPS = 1e-06
VMEM_BYTES = 16 * 1024 * 1024
ROW_STEP = 32

LOW = jnp.bfloat16
WIDE = jnp.float32
LIGHT = pl.CostEstimate(flops=1, transcendentals=0, bytes_accessed=1)


def params():
    return pltpu.CompilerParams(vmem_limit_bytes=VMEM_BYTES)


def vmem_specs(count):
    return [pl.BlockSpec(memory_space=pltpu.VMEM)] * count


def pack_kernel(n_seq, chunks, core_ref, *refs):
    query_ref, key_ref, value_ref, dquery_ref, dkey_ref, dvalue_ref, gains_ref = refs[:7]
    out_refs = refs[7:]
    n_chunks = len(chunks)
    group = query_ref.shape[-1] // n_seq

    def statistics(primal_ref, tangent_ref):
        primal = primal_ref[...].astype(WIDE)
        tangent = tangent_ref[...].astype(WIDE)
        inverse = lax.rsqrt(jnp.mean(primal * primal, axis=-1, keepdims=True) + EPS)
        across = jnp.mean(primal * tangent, axis=-1, keepdims=True)
        return inverse, inverse * inverse * inverse * across

    query_stats = statistics(query_ref, dquery_ref)
    key_stats = statistics(key_ref, dkey_ref)

    def normed(primal_ref, tangent_ref, which, stats, lanes):
        primal = primal_ref[:, lanes].astype(WIDE)
        tangent = tangent_ref[:, lanes].astype(WIDE)
        gain = gains_ref[which : which + 1, lanes]
        inverse, slope = stats
        return (primal * inverse * gain).astype(LOW), (gain * (tangent * inverse - primal * slope)).astype(LOW)

    for side in range(2):
        core = core_ref[0] if side == 0 else 1 - core_ref[0]
        queries_ref, *keyed_refs = out_refs[side * (1 + n_chunks) : (side + 1) * (1 + n_chunks)]
        for at in range(n_seq // 2):
            lanes = pl.ds(pl.multiple_of((2 * at + core) * group, 128), group)
            here = slice(at * group, (at + 1) * group)
            plain, dual = normed(query_ref, dquery_ref, 0, query_stats, lanes)
            queries_ref[0, :, here] = plain
            queries_ref[1, :, here] = dual
            four = normed(key_ref, dkey_ref, 1, key_stats, lanes)
            four += (value_ref[:, lanes], dvalue_ref[:, lanes])
            start = 0
            for keyed_ref, width in zip(keyed_refs, chunks):
                low, high = max(start, here.start), min(start + width, here.stop)
                if low < high:
                    for which, part in enumerate(four):
                        keyed_ref[which, :, low - start : high - start] = part[:, low - here.start : high - here.start]
                start += width


def pack(core, n_seq, chunks, arrays, gains):
    rows, features = arrays[0].shape
    step = min(rows, ROW_STEP)
    row_block = pl.BlockSpec((step, features), lambda i, c: (i, 0))
    gain_block = pl.BlockSpec((2, features), lambda i, c: (0, 0))
    kinds = [(2, features // 2)] + [(4, width) for width in chunks]
    kinds = kinds + kinds
    return pl.pallas_call(
        functools.partial(pack_kernel, n_seq, chunks),
        grid_spec=pltpu.PrefetchScalarGridSpec(
            num_scalar_prefetch=1,
            grid=(rows // step,),
            in_specs=[row_block] * 6 + [gain_block],
            out_specs=[pl.BlockSpec((count, step, width), lambda i, c: (0, i, 0)) for count, width in kinds],
        ),
        out_shape=[jax.ShapeDtypeStruct((count, rows, width), LOW) for count, width in kinds],
        compiler_params=params(),
        cost_estimate=LIGHT,
    )(core, *arrays, gains)


def attend_kernel(n_queries, *refs):
    query_refs, keyed_refs, out_ref = refs[:n_queries], refs[n_queries:-1], refs[-1]

    def stack(which, some_refs, kinds):
        parts = [ref[at] for ref in some_refs for at in range(which, ref.shape[0], kinds)]
        return jnp.concatenate(parts, axis=0)

    query, query_dual = (stack(which, query_refs, 2) for which in range(2))
    key, key_dual, value, value_dual = (stack(which, keyed_refs, 4) for which in range(4))
    factor = query.shape[-1] ** (-0.5)
    last = (((1,), (1,)), ((), ()))
    scores = lax.dot_general(query, key, last, preferred_element_type=WIDE) * factor
    dual_scores = (
        lax.dot_general(
            jnp.concatenate([query_dual, query], axis=1),
            jnp.concatenate([key, key_dual], axis=1),
            last,
            preferred_element_type=WIDE,
        )
        * factor
    )
    raised = jnp.exp(scores - jnp.max(scores, axis=-1, keepdims=True))
    probs = raised * (1.0 / jnp.sum(raised, axis=-1, keepdims=True))
    spread = probs * (dual_scores - jnp.sum(probs * dual_scores, axis=-1, keepdims=True))
    probs_low = probs.astype(LOW)
    spread_low = spread.astype(LOW)
    out_ref[0] = jnp.dot(probs_low, value, preferred_element_type=WIDE).astype(LOW)
    out_ref[1] = (
        jnp.dot(probs_low, value_dual, preferred_element_type=WIDE)
        + jnp.dot(spread_low, value, preferred_element_type=WIDE)
    ).astype(LOW)


def attend(start, hdim, queries, keyed):
    rows = queries[0].shape[1]
    width = keyed[0].shape[2]
    first = start // hdim
    return pl.pallas_call(
        functools.partial(attend_kernel, len(queries)),
        grid=(width // hdim,),
        in_specs=[pl.BlockSpec((2, rows, hdim), lambda h: (0, 0, first + h))] * len(queries)
        + [pl.BlockSpec((array.shape[0], rows, hdim), lambda h: (0, 0, h)) for array in keyed],
        out_specs=pl.BlockSpec((2, len(queries) * rows, hdim), lambda h: (0, 0, h)),
        out_shape=jax.ShapeDtypeStruct((2, len(queries) * rows, width), LOW),
        compiler_params=params(),
        cost_estimate=LIGHT,
    )(*queries, *keyed)


def project_kernel(n_chunks, spans, flip_ref, *refs):
    sides = refs[:n_chunks], refs[n_chunks : 2 * n_chunks]
    weight_refs, out_refs, weight_ref = refs[2 * n_chunks : -6], refs[-6:-1], refs[-1]
    rows = out_refs[0].shape[0] // 2
    depth = weight_ref.shape[0] // 2
    at = 0
    for ref, (low, high) in zip(weight_refs, spans):
        block, inside = at // depth, at % depth
        first = pl.multiple_of((block ^ flip_ref[0]) * depth + inside, 16)
        weight_ref[pl.ds(first, high - low)] = ref[low:high]
        at += high - low
    weight = weight_ref[...]
    for side, parts in enumerate(sides):
        acts = jnp.concatenate([ref[...].reshape(4 * rows, ref.shape[-1]) for ref in parts], axis=1)
        total = jnp.dot(acts, weight, preferred_element_type=WIDE)
        for kind in range(2):
            first = 2 * kind * rows
            here = slice(kind * rows, (kind + 1) * rows)
            out_refs[side][here] = total[first : first + rows]
            low = total[first + rows : first + 2 * rows].astype(LOW)
            if side:
                out_refs[3 + kind][...] = low
            else:
                out_refs[2][here] = low


def project(flip, acts, pieces):
    mine, theirs = zip(*acts)
    weights = [weight for weight, _, _ in pieces]
    spans = [(low, high) for _, low, high in pieces]
    rows, n = mine[0].shape[1], weights[0].shape[1]
    depth = sum(high - low for low, high in spans)
    return pl.pallas_call(
        functools.partial(project_kernel, len(acts), spans),
        in_specs=[pl.BlockSpec(memory_space=pltpu.SMEM)] + vmem_specs(2 * len(acts) + len(weights)),
        out_specs=vmem_specs(5),
        out_shape=[jax.ShapeDtypeStruct((rows, n), WIDE)] * 2
        + [jax.ShapeDtypeStruct((rows, n), LOW)]
        + [jax.ShapeDtypeStruct((rows // 2, n), LOW)] * 2,
        scratch_shapes=[pltpu.VMEM((depth, n), LOW)],
        compiler_params=params(),
        cost_estimate=LIGHT,
    )(flip, *mine, *theirs, *weights)


def close_kernel(keep_ref, *refs):
    got_refs, out_ref = refs[:-1], refs[-1]
    first = 0
    for got_ref in got_refs:
        here = slice(first, first + got_ref.shape[0])
        out_ref[here] = (keep_ref[here] + got_ref[...].astype(WIDE)).astype(LOW)
        first = here.stop


def close(keep, *gots):
    return pl.pallas_call(
        close_kernel,
        in_specs=vmem_specs(1 + len(gots)),
        out_specs=vmem_specs(1)[0],
        out_shape=jax.ShapeDtypeStruct(keep.shape, LOW),
        compiler_params=params(),
        cost_estimate=LIGHT,
    )(keep, *gots)


def place_kernel(where_ref, keep_ref, got_ref, other_ref, *refs):
    plain_ref, dual_ref = refs[-2:]
    rows = plain_ref.shape[0]

    @pl.when(pl.program_id(0) == 0)
    def _():
        total = (keep_ref[...] + got_ref[...].astype(WIDE)).astype(LOW)
        plain_ref[...] = total[:rows]
        dual_ref[...] = total[rows:]

    @pl.when(pl.program_id(0) == 1)
    def _():
        plain_ref[...] = other_ref[:rows]
        dual_ref[...] = other_ref[rows:]


def place(outs, width, where, keep, got, other):
    rows, n = other.shape[0] // 2, other.shape[1]
    if n % 128:
        outs = outs or [jnp.zeros((rows, width), LOW)] * 2
        for side, piece in enumerate((close(keep, got), other)):
            parts = (piece[:rows], piece[rows:])
            outs = [lax.dynamic_update_slice(out, part, (0, where[side] * n)) for out, part in zip(outs, parts)]
        return outs
    full = pl.BlockSpec((2 * rows, n), lambda i, w: (0, 0))
    block = pl.BlockSpec((rows, n), lambda i, w: (0, w[i]))
    return pl.pallas_call(
        place_kernel,
        grid_spec=pltpu.PrefetchScalarGridSpec(
            num_scalar_prefetch=1,
            grid=(2,),
            in_specs=[full] * 3 + [pl.BlockSpec(memory_space=pl.ANY)] * len(outs),
            out_specs=[block] * 2,
        ),
        out_shape=[jax.ShapeDtypeStruct((rows, width), LOW)] * 2,
        input_output_aliases={4 + at: at for at in range(len(outs))},
        compiler_params=params(),
        cost_estimate=LIGHT,
    )(where, keep, got, other, *outs)


def body(
    n_dp,
    n_seq,
    queries,
    key_states,
    value_states,
    query_tangent,
    key_tangent,
    value_tangent,
    query_gain,
    key_gain,
    out_weight,
):
    dp = lax.axis_index("dp")
    seq = lax.axis_index("seq")
    n_ring = n_dp // 2
    groups = n_seq // 2
    features = queries.shape[1]
    hdim = features // HEADS
    group_heads = HEADS // n_seq
    few = group_heads * 2 // 5
    chunks = [group_heads * hdim] * (groups - 1) + [(group_heads - few) * hdim, few * hdim]
    starts = [sum(chunks[:at]) for at in range(len(chunks))]
    token = jnp.zeros((1,), jnp.int32)

    def far(array):
        return lax.ppermute(array, "seq", [(i, i ^ 2) for i in range(n_seq)])

    def near(array):
        return lax.ppermute(array, "seq", [(i, i ^ 1) for i in range(n_seq)])

    def across(array):
        return lax.ppermute(array, "dp", [(i, i ^ 1) for i in range(n_dp)])

    def onward(array):
        return lax.ppermute(array, "dp", [(i, (i + 2) % n_dp) for i in range(n_dp)])

    def wait(array):
        nonlocal token
        array, token = lax.optimization_barrier((array, token))
        return array

    def after(array):
        return lax.optimization_barrier((array, token))[0]

    def turn(ring, step):
        ring[step] = wait(ring[step])
        if step + 1 < n_ring:
            ring.append(onward(ring[step]))

    depth = out_weight.shape[0]
    cut = depth * 3 // 5 // 16 * 16
    upper, lower = [out_weight[:cut]], [out_weight[cut:]]
    lower.append(onward(lower[0]))
    upper.append(onward(upper[0]))
    beside = [wait(far(upper[0]))]
    beside.append(onward(beside[0]))
    turn(lower, 1)

    core = jnp.stack([seq % 2])
    arrays = (queries, key_states, value_states, query_tangent, key_tangent, value_tangent)
    packs = [wait(array) for array in pack(core, n_seq, chunks, arrays, jnp.stack([query_gain, key_gain]))]
    query_own, *keyed_own = packs[: 1 + len(chunks)]
    query_other, *keyed_other = packs[1 + len(chunks) :]
    there = wait(near(keyed_other[0]))
    keyed = [[keyed_own[0], there, far(keyed_own[0]), far(there)]]
    for own, other in zip(keyed_own[1:], keyed_other[1:]):
        there = wait(near(other))
        keyed.append([own, there, far(jnp.concatenate([own, there]))])
    queries_both = [query_own, wait(near(query_other))]
    turn(lower, 2)

    acts, swapped = [], []

    def attention(chunk):
        keyed[chunk][-1] = wait(keyed[chunk][-1])
        acts.append(wait(attend(starts[chunk], hdim, queries_both, keyed[chunk])))
        swapped.append(across(acts[-1]))

    turn(upper, 1)
    keyed[0][2] = wait(keyed[0][2])
    turn(beside, 1)
    attention(0)
    for step in range(3, n_ring):
        turn(lower, step)
    later = [wait(jnp.concatenate(lower[step : step + 2])) for step in range(2, n_ring, 2)]
    turn(upper, 2)
    rest = [far(after(lower[0]))]
    attention(1)
    swapped[0] = wait(swapped[0])
    attention(2)
    swapped[1] = wait(swapped[1])
    turn(beside, 2)
    rest += [far(after(piece)) for piece in lower[1:2] + later]
    rest[0] = wait(rest[0])
    swapped[2] = wait(swapped[2])
    acts = list(zip(acts, swapped))
    flip = jnp.stack([seq // 2])

    keeps, mine_sends, sends, mine_got, other = [], [], [], [], []

    def columns(step):
        own = [(upper[step], 0, cut), (lower[step], 0, depth - cut)]
        start = step % 2 * (depth - cut) if step > 1 else 0
        got = rest[step] if step < 2 else rest[1 + step // 2]
        theirs = [(beside[step], 0, cut), (got, start, start + depth - cut)]
        keep_mine, keep_other, send_mine, *send_other = project(flip, acts, own + theirs)
        keeps.append((keep_mine, keep_other))
        sends.append([near(wait(array)) for array in send_other])
        mine_sends.append(send_mine)

    def finish(step):
        other.append(across(wait(close(keeps[step][1], *[wait(array) for array in sends[step]]))))
        mine_got.append(near(mine_sends[step]))

    outs = []

    def put(step):
        pair = (dp // 2 - step) % n_ring
        where = jnp.stack([2 * pair + dp % 2, 2 * pair + 1 - dp % 2]).astype(jnp.int32) + token
        return place(outs, n_dp * out_weight.shape[1], where, keeps[step][0], wait(mine_got[step]), wait(other[step]))

    columns(0)
    for step in range(3, n_ring):
        turn(upper, step)
    rest[1] = wait(rest[1])
    finish(0)
    columns(1)
    finish(1)
    for step in range(2, n_ring, 2):
        other[step - 2] = wait(other[step - 2])
        rest[1 + step // 2] = wait(rest[1 + step // 2])
        for ahead in range(max(step, 3), step + 2):
            turn(beside, ahead)
        columns(step)
        finish(step)
        columns(step + 1)
        other[step - 1] = wait(other[step - 1])
        finish(step + 1)
    for step in range(n_ring):
        outs = put(step)
    return tuple(outs)


def solution(mesh):
    rows = P(("dp", "seq"), None)
    return jax.shard_map(
        functools.partial(body, mesh.shape["dp"], mesh.shape["seq"]),
        mesh=mesh,
        in_specs=(rows,) * 6 + (P(), P(), P("seq", "dp")),
        out_specs=(rows, rows),
        check_vma=False,
    )
```

```python
import functools

import jax
import jax.numpy as jnp
from jax import lax
from jax.experimental import pallas as pl
from jax.experimental.pallas import tpu as pltpu
from jax.sharding import PartitionSpec as P

HEADS = 20
EPS = 1e-06
VMEM_BYTES = 10 * 1024 * 1024
ROW_STEP = 32

LOW = jnp.bfloat16
WIDE = jnp.float32
LIGHT = pl.CostEstimate(flops=1, transcendentals=0, bytes_accessed=1)


def params():
    return pltpu.CompilerParams(vmem_limit_bytes=VMEM_BYTES)


def vmem_specs(count):
    return [pl.BlockSpec(memory_space=pltpu.VMEM)] * count


def pack_kernel(n_seq, chunks, core_ref, *refs):
    query_ref, key_ref, value_ref, dquery_ref, dkey_ref, dvalue_ref, gains_ref = refs[:7]
    out_refs = refs[7:]
    n_chunks = len(chunks)
    group = query_ref.shape[-1] // n_seq

    def statistics(primal_ref, tangent_ref):
        primal = primal_ref[...].astype(WIDE)
        tangent = tangent_ref[...].astype(WIDE)
        inverse = lax.rsqrt(jnp.mean(primal * primal, axis=-1, keepdims=True) + EPS)
        across = jnp.mean(primal * tangent, axis=-1, keepdims=True)
        return inverse, inverse * inverse * inverse * across

    query_stats = statistics(query_ref, dquery_ref)
    key_stats = statistics(key_ref, dkey_ref)

    def normed(primal_ref, tangent_ref, which, stats, lanes):
        primal = primal_ref[:, lanes].astype(WIDE)
        tangent = tangent_ref[:, lanes].astype(WIDE)
        gain = gains_ref[which : which + 1, lanes]
        inverse, slope = stats
        return (primal * inverse * gain).astype(LOW), (gain * (tangent * inverse - primal * slope)).astype(LOW)

    for side in range(2):
        core = core_ref[0] if side == 0 else 1 - core_ref[0]
        queries_ref, *keyed_refs = out_refs[side * (1 + n_chunks) : (side + 1) * (1 + n_chunks)]
        for at in range(n_seq // 2):
            lanes = pl.ds(pl.multiple_of((2 * at + core) * group, 128), group)
            here = slice(at * group, (at + 1) * group)
            plain, dual = normed(query_ref, dquery_ref, 0, query_stats, lanes)
            queries_ref[0, :, here] = plain
            queries_ref[1, :, here] = dual
            four = normed(key_ref, dkey_ref, 1, key_stats, lanes)
            four += (value_ref[:, lanes], dvalue_ref[:, lanes])
            start = 0
            for keyed_ref, width in zip(keyed_refs, chunks):
                low, high = max(start, here.start), min(start + width, here.stop)
                if low < high:
                    for which, part in enumerate(four):
                        keyed_ref[which, :, low - start : high - start] = part[:, low - here.start : high - here.start]
                start += width


def pack(core, n_seq, chunks, arrays, gains):
    rows, features = arrays[0].shape
    step = min(rows, ROW_STEP)
    row_block = pl.BlockSpec((step, features), lambda i, c: (i, 0))
    gain_block = pl.BlockSpec((2, features), lambda i, c: (0, 0))
    kinds = [(2, features // 2)] + [(4, width) for width in chunks]
    kinds = kinds + kinds
    return pl.pallas_call(
        functools.partial(pack_kernel, n_seq, chunks),
        grid_spec=pltpu.PrefetchScalarGridSpec(
            num_scalar_prefetch=1,
            grid=(rows // step,),
            in_specs=[row_block] * 6 + [gain_block],
            out_specs=[pl.BlockSpec((count, step, width), lambda i, c: (0, i, 0)) for count, width in kinds],
        ),
        out_shape=[jax.ShapeDtypeStruct((count, rows, width), LOW) for count, width in kinds],
        compiler_params=params(),
        cost_estimate=LIGHT,
    )(core, *arrays, gains)


def attend_kernel(n_queries, *refs):
    query_refs, keyed_refs, out_ref = refs[:n_queries], refs[n_queries:-1], refs[-1]

    def stack(which, some_refs, kinds):
        parts = [ref[at] for ref in some_refs for at in range(which, ref.shape[0], kinds)]
        return jnp.concatenate(parts, axis=0)

    query, query_dual = (stack(which, query_refs, 2) for which in range(2))
    key, key_dual, value, value_dual = (stack(which, keyed_refs, 4) for which in range(4))
    factor = query.shape[-1] ** (-0.5)
    last = (((1,), (1,)), ((), ()))
    scores = lax.dot_general(query, key, last, preferred_element_type=WIDE) * factor
    dual_scores = (
        lax.dot_general(
            jnp.concatenate([query_dual, query], axis=1),
            jnp.concatenate([key, key_dual], axis=1),
            last,
            preferred_element_type=WIDE,
        )
        * factor
    )
    raised = jnp.exp(scores - jnp.max(scores, axis=-1, keepdims=True))
    probs = raised * (1.0 / jnp.sum(raised, axis=-1, keepdims=True))
    spread = probs * (dual_scores - jnp.sum(probs * dual_scores, axis=-1, keepdims=True))
    probs_low = probs.astype(LOW)
    spread_low = spread.astype(LOW)
    out_ref[0] = jnp.dot(probs_low, value, preferred_element_type=WIDE).astype(LOW)
    out_ref[1] = (
        jnp.dot(probs_low, value_dual, preferred_element_type=WIDE)
        + jnp.dot(spread_low, value, preferred_element_type=WIDE)
    ).astype(LOW)


def attend(start, hdim, queries, keyed):
    rows = queries[0].shape[1]
    width = keyed[0].shape[2]
    first = start // hdim
    return pl.pallas_call(
        functools.partial(attend_kernel, len(queries)),
        grid=(width // hdim,),
        in_specs=[pl.BlockSpec((2, rows, hdim), lambda h: (0, 0, first + h))] * len(queries)
        + [pl.BlockSpec((array.shape[0], rows, hdim), lambda h: (0, 0, h)) for array in keyed],
        out_specs=pl.BlockSpec((2, len(queries) * rows, hdim), lambda h: (0, 0, h)),
        out_shape=jax.ShapeDtypeStruct((2, len(queries) * rows, width), LOW),
        compiler_params=params(),
        cost_estimate=LIGHT,
    )(*queries, *keyed)


def project_kernel(n_chunks, spans, flip_ref, *refs):
    sides = refs[:n_chunks], refs[n_chunks : 2 * n_chunks]
    weight_refs, out_refs, weight_ref = refs[2 * n_chunks : -6], refs[-6:-1], refs[-1]
    rows = out_refs[0].shape[0] // 2
    depth = weight_ref.shape[0] // 2
    at = 0
    for ref, (low, high) in zip(weight_refs, spans):
        block, inside = at // depth, at % depth
        first = pl.multiple_of((block ^ flip_ref[0]) * depth + inside, 16)
        weight_ref[pl.ds(first, high - low)] = ref[low:high]
        at += high - low
    weight = weight_ref[...]
    for side, parts in enumerate(sides):
        acts = jnp.concatenate([ref[...].reshape(4 * rows, ref.shape[-1]) for ref in parts], axis=1)
        total = jnp.dot(acts, weight, preferred_element_type=WIDE)
        for kind in range(2):
            first = 2 * kind * rows
            here = slice(kind * rows, (kind + 1) * rows)
            out_refs[side][here] = total[first : first + rows]
            low = total[first + rows : first + 2 * rows].astype(LOW)
            if side:
                out_refs[3 + kind][...] = low
            else:
                out_refs[2][here] = low


def project(flip, acts, pieces):
    mine, theirs = zip(*acts)
    weights = [weight for weight, _, _ in pieces]
    spans = [(low, high) for _, low, high in pieces]
    rows, n = mine[0].shape[1], weights[0].shape[1]
    depth = sum(high - low for low, high in spans)
    return pl.pallas_call(
        functools.partial(project_kernel, len(acts), spans),
        in_specs=[pl.BlockSpec(memory_space=pltpu.SMEM)] + vmem_specs(2 * len(acts) + len(weights)),
        out_specs=vmem_specs(5),
        out_shape=[jax.ShapeDtypeStruct((rows, n), WIDE)] * 2
        + [jax.ShapeDtypeStruct((rows, n), LOW)]
        + [jax.ShapeDtypeStruct((rows // 2, n), LOW)] * 2,
        scratch_shapes=[pltpu.VMEM((depth, n), LOW)],
        compiler_params=params(),
        cost_estimate=LIGHT,
    )(flip, *mine, *theirs, *weights)


def close_kernel(keep_ref, *refs):
    got_refs, out_ref = refs[:-1], refs[-1]
    first = 0
    for got_ref in got_refs:
        here = slice(first, first + got_ref.shape[0])
        out_ref[here] = (keep_ref[here] + got_ref[...].astype(WIDE)).astype(LOW)
        first = here.stop


def close(keep, *gots):
    return pl.pallas_call(
        close_kernel,
        in_specs=vmem_specs(1 + len(gots)),
        out_specs=vmem_specs(1)[0],
        out_shape=jax.ShapeDtypeStruct(keep.shape, LOW),
        compiler_params=params(),
        cost_estimate=LIGHT,
    )(keep, *gots)


def place_kernel(where_ref, keep_ref, got_ref, other_ref, *refs):
    plain_ref, dual_ref = refs[-2:]
    rows = plain_ref.shape[0]

    @pl.when(pl.program_id(0) == 0)
    def _():
        total = (keep_ref[...] + got_ref[...].astype(WIDE)).astype(LOW)
        plain_ref[...] = total[:rows]
        dual_ref[...] = total[rows:]

    @pl.when(pl.program_id(0) == 1)
    def _():
        plain_ref[...] = other_ref[:rows]
        dual_ref[...] = other_ref[rows:]


def place(outs, width, where, keep, got, other):
    rows, n = other.shape[0] // 2, other.shape[1]
    if n % 128:
        outs = outs or [jnp.zeros((rows, width), LOW)] * 2
        for side, piece in enumerate((close(keep, got), other)):
            parts = (piece[:rows], piece[rows:])
            outs = [lax.dynamic_update_slice(out, part, (0, where[side] * n)) for out, part in zip(outs, parts)]
        return outs
    full = pl.BlockSpec((2 * rows, n), lambda i, w: (0, 0))
    block = pl.BlockSpec((rows, n), lambda i, w: (0, w[i]))
    return pl.pallas_call(
        place_kernel,
        grid_spec=pltpu.PrefetchScalarGridSpec(
            num_scalar_prefetch=1,
            grid=(2,),
            in_specs=[full] * 3 + [pl.BlockSpec(memory_space=pl.ANY)] * len(outs),
            out_specs=[block] * 2,
        ),
        out_shape=[jax.ShapeDtypeStruct((rows, width), LOW)] * 2,
        input_output_aliases={4 + at: at for at in range(len(outs))},
        compiler_params=params(),
        cost_estimate=LIGHT,
    )(where, keep, got, other, *outs)


def body(
    n_dp,
    n_seq,
    queries,
    key_states,
    value_states,
    query_tangent,
    key_tangent,
    value_tangent,
    query_gain,
    key_gain,
    out_weight,
):
    dp = lax.axis_index("dp")
    seq = lax.axis_index("seq")
    n_ring = n_dp // 2
    groups = n_seq // 2
    features = queries.shape[1]
    hdim = features // HEADS
    group_heads = HEADS // n_seq
    few = group_heads * 2 // 5
    chunks = [group_heads * hdim] * (groups - 1) + [(group_heads - few) * hdim, few * hdim]
    starts = [sum(chunks[:at]) for at in range(len(chunks))]
    token = jnp.zeros((1,), jnp.int32)

    def far(array):
        return lax.ppermute(array, "seq", [(i, i ^ 2) for i in range(n_seq)])

    def near(array):
        return lax.ppermute(array, "seq", [(i, i ^ 1) for i in range(n_seq)])

    def across(array):
        return lax.ppermute(array, "dp", [(i, i ^ 1) for i in range(n_dp)])

    def onward(array):
        return lax.ppermute(array, "dp", [(i, (i + 2) % n_dp) for i in range(n_dp)])

    def wait(array):
        nonlocal token
        array, token = lax.optimization_barrier((array, token))
        return array

    def after(array):
        return lax.optimization_barrier((array, token))[0]

    def turn(ring, step):
        ring[step] = wait(ring[step])
        if step + 1 < n_ring:
            ring.append(onward(ring[step]))

    depth = out_weight.shape[0]
    cut = depth * 3 // 5 // 16 * 16
    upper, lower = [out_weight[:cut]], [out_weight[cut:]]
    lower.append(onward(lower[0]))
    upper.append(onward(upper[0]))
    beside = [wait(far(upper[0]))]
    beside.append(onward(beside[0]))
    turn(lower, 1)

    core = jnp.stack([seq % 2])
    arrays = (queries, key_states, value_states, query_tangent, key_tangent, value_tangent)
    packs = [wait(array) for array in pack(core, n_seq, chunks, arrays, jnp.stack([query_gain, key_gain]))]
    query_own, *keyed_own = packs[: 1 + len(chunks)]
    query_other, *keyed_other = packs[1 + len(chunks) :]
    there = wait(near(keyed_other[0]))
    keyed = [[keyed_own[0], there, far(keyed_own[0]), far(there)]]
    for own, other in zip(keyed_own[1:], keyed_other[1:]):
        there = wait(near(other))
        keyed.append([own, there, far(jnp.concatenate([own, there]))])
    queries_both = [query_own, wait(near(query_other))]
    turn(lower, 2)

    acts, swapped = [], []

    def attention(chunk):
        keyed[chunk][-1] = wait(keyed[chunk][-1])
        acts.append(wait(attend(starts[chunk], hdim, queries_both, keyed[chunk])))
        swapped.append(across(acts[-1]))

    turn(upper, 1)
    keyed[0][2] = wait(keyed[0][2])
    turn(beside, 1)
    attention(0)
    for step in range(3, n_ring):
        turn(lower, step)
    later = [wait(jnp.concatenate(lower[step : step + 2])) for step in range(2, n_ring, 2)]
    turn(upper, 2)
    rest = [far(after(lower[0]))]
    attention(1)
    swapped[0] = wait(swapped[0])
    attention(2)
    swapped[1] = wait(swapped[1])
    turn(beside, 2)
    rest += [far(after(piece)) for piece in lower[1:2] + later]
    rest[0] = wait(rest[0])
    swapped[2] = wait(swapped[2])
    acts = list(zip(acts, swapped))
    flip = jnp.stack([seq // 2])

    keeps, mine_sends, sends, mine_got, other = [], [], [], [], []

    def columns(step):
        own = [(upper[step], 0, cut), (lower[step], 0, depth - cut)]
        start = step % 2 * (depth - cut) if step > 1 else 0
        got = rest[step] if step < 2 else rest[1 + step // 2]
        theirs = [(beside[step], 0, cut), (got, start, start + depth - cut)]
        keep_mine, keep_other, send_mine, *send_other = project(after(flip), acts, own + theirs)
        keeps.append((keep_mine, keep_other))
        sends.append([near(wait(array)) for array in send_other])
        mine_sends.append(send_mine)

    def finish(step):
        other.append(across(wait(close(keeps[step][1], *[wait(array) for array in sends[step]]))))
        mine_got.append(near(mine_sends[step]))

    outs = []

    def put(step):
        pair = (dp // 2 - step) % n_ring
        where = jnp.stack([2 * pair + dp % 2, 2 * pair + 1 - dp % 2]).astype(jnp.int32) + token
        return place(outs, n_dp * out_weight.shape[1], where, keeps[step][0], wait(mine_got[step]), wait(other[step]))

    columns(0)
    for step in range(3, n_ring):
        turn(upper, step)
    rest[1] = wait(rest[1])
    finish(0)
    columns(1)
    finish(1)
    for step in range(2, n_ring, 2):
        other[step - 2] = wait(other[step - 2])
        rest[1 + step // 2] = wait(rest[1 + step // 2])
        if step > 2:
            turn(beside, step)
        columns(step)
        finish(step)
        turn(beside, step + 1)
        columns(step + 1)
        other[step - 1] = wait(other[step - 1])
        finish(step + 1)
    other[-2] = wait(other[-2])
    for step in range(n_ring):
        outs = put(step)
    return tuple(outs)


def solution(mesh):
    rows = P(("dp", "seq"), None)
    return jax.shard_map(
        functools.partial(body, mesh.shape["dp"], mesh.shape["seq"]),
        mesh=mesh,
        in_specs=(rows,) * 6 + (P(), P(), P("seq", "dp")),
        out_specs=(rows, rows),
        check_vma=False,
    )
```

```python
import functools

import jax
import jax.numpy as jnp
from jax import lax
from jax.experimental import pallas as pl
from jax.experimental.pallas import tpu as pltpu
from jax.sharding import PartitionSpec as P

HEADS = 20
EPS = 1e-06
VMEM_BYTES = 10 * 1024 * 1024
ROW_STEP = 32

LOW = jnp.bfloat16
WIDE = jnp.float32
LIGHT = pl.CostEstimate(flops=1, transcendentals=0, bytes_accessed=1)


def params():
    return pltpu.CompilerParams(vmem_limit_bytes=VMEM_BYTES)


def vmem_specs(count):
    return [pl.BlockSpec(memory_space=pltpu.VMEM)] * count


def pack_kernel(n_seq, chunks, core_ref, *refs):
    query_ref, key_ref, value_ref, dquery_ref, dkey_ref, dvalue_ref, gains_ref = refs[:7]
    out_refs = refs[7:]
    n_chunks = len(chunks)
    group = query_ref.shape[-1] // n_seq

    def statistics(primal_ref, tangent_ref):
        primal = primal_ref[...].astype(WIDE)
        tangent = tangent_ref[...].astype(WIDE)
        inverse = lax.rsqrt(jnp.mean(primal * primal, axis=-1, keepdims=True) + EPS)
        across = jnp.mean(primal * tangent, axis=-1, keepdims=True)
        return inverse, inverse * inverse * inverse * across

    query_stats = statistics(query_ref, dquery_ref)
    key_stats = statistics(key_ref, dkey_ref)

    def normed(primal_ref, tangent_ref, which, stats, lanes):
        primal = primal_ref[:, lanes].astype(WIDE)
        tangent = tangent_ref[:, lanes].astype(WIDE)
        gain = gains_ref[which : which + 1, lanes]
        inverse, slope = stats
        return (primal * inverse * gain).astype(LOW), (gain * (tangent * inverse - primal * slope)).astype(LOW)

    for side in range(2):
        core = core_ref[0] if side == 0 else 1 - core_ref[0]
        queries_ref, *keyed_refs = out_refs[side * (1 + n_chunks) : (side + 1) * (1 + n_chunks)]
        for at in range(n_seq // 2):
            lanes = pl.ds(pl.multiple_of((2 * at + core) * group, 128), group)
            here = slice(at * group, (at + 1) * group)
            plain, dual = normed(query_ref, dquery_ref, 0, query_stats, lanes)
            queries_ref[0, :, here] = plain
            queries_ref[1, :, here] = dual
            four = normed(key_ref, dkey_ref, 1, key_stats, lanes)
            four += (value_ref[:, lanes], dvalue_ref[:, lanes])
            start = 0
            for keyed_ref, width in zip(keyed_refs, chunks):
                low, high = max(start, here.start), min(start + width, here.stop)
                if low < high:
                    for which, part in enumerate(four):
                        keyed_ref[which, :, low - start : high - start] = part[:, low - here.start : high - here.start]
                start += width


def pack(core, n_seq, chunks, arrays, gains):
    rows, features = arrays[0].shape
    step = min(rows, ROW_STEP)
    row_block = pl.BlockSpec((step, features), lambda i, c: (i, 0))
    gain_block = pl.BlockSpec((2, features), lambda i, c: (0, 0))
    kinds = [(2, features // 2)] + [(4, width) for width in chunks]
    kinds = kinds + kinds
    return pl.pallas_call(
        functools.partial(pack_kernel, n_seq, chunks),
        grid_spec=pltpu.PrefetchScalarGridSpec(
            num_scalar_prefetch=1,
            grid=(rows // step,),
            in_specs=[row_block] * 6 + [gain_block],
            out_specs=[pl.BlockSpec((count, step, width), lambda i, c: (0, i, 0)) for count, width in kinds],
        ),
        out_shape=[jax.ShapeDtypeStruct((count, rows, width), LOW) for count, width in kinds],
        compiler_params=params(),
        cost_estimate=LIGHT,
    )(core, *arrays, gains)


def attend_kernel(n_queries, *refs):
    query_refs, keyed_refs, out_ref = refs[:n_queries], refs[n_queries:-1], refs[-1]

    def stack(which, some_refs, kinds):
        parts = [ref[at] for ref in some_refs for at in range(which, ref.shape[0], kinds)]
        return jnp.concatenate(parts, axis=0)

    query, query_dual = (stack(which, query_refs, 2) for which in range(2))
    key, key_dual, value, value_dual = (stack(which, keyed_refs, 4) for which in range(4))
    factor = query.shape[-1] ** (-0.5)
    last = (((1,), (1,)), ((), ()))
    scores = lax.dot_general(query, key, last, preferred_element_type=WIDE) * factor
    dual_scores = (
        lax.dot_general(
            jnp.concatenate([query_dual, query], axis=1),
            jnp.concatenate([key, key_dual], axis=1),
            last,
            preferred_element_type=WIDE,
        )
        * factor
    )
    raised = jnp.exp(scores - jnp.max(scores, axis=-1, keepdims=True))
    probs = raised * (1.0 / jnp.sum(raised, axis=-1, keepdims=True))
    spread = probs * (dual_scores - jnp.sum(probs * dual_scores, axis=-1, keepdims=True))
    probs_low = probs.astype(LOW)
    spread_low = spread.astype(LOW)
    out_ref[0] = jnp.dot(probs_low, value, preferred_element_type=WIDE).astype(LOW)
    out_ref[1] = (
        jnp.dot(probs_low, value_dual, preferred_element_type=WIDE)
        + jnp.dot(spread_low, value, preferred_element_type=WIDE)
    ).astype(LOW)


def attend(start, hdim, queries, keyed):
    rows = queries[0].shape[1]
    width = keyed[0].shape[2]
    first = start // hdim
    return pl.pallas_call(
        functools.partial(attend_kernel, len(queries)),
        grid=(width // hdim,),
        in_specs=[pl.BlockSpec((2, rows, hdim), lambda h: (0, 0, first + h))] * len(queries)
        + [pl.BlockSpec((array.shape[0], rows, hdim), lambda h: (0, 0, h)) for array in keyed],
        out_specs=pl.BlockSpec((2, len(queries) * rows, hdim), lambda h: (0, 0, h)),
        out_shape=jax.ShapeDtypeStruct((2, len(queries) * rows, width), LOW),
        compiler_params=params(),
        cost_estimate=LIGHT,
    )(*queries, *keyed)


def project_kernel(n_chunks, spans, flip_ref, *refs):
    sides = refs[:n_chunks], refs[n_chunks : 2 * n_chunks]
    weight_refs = refs[2 * n_chunks : -10]
    keep_mine_ref, keep_other_ref, send_mine_ref, first_ref, second_ref = refs[-10:-5]
    weight_ref, keep_ref, send_ref, in_sems, out_sems = refs[-5:]
    rows = first_ref.shape[0]
    depth = weight_ref.shape[0] // 2
    loads = []
    at = 0
    for ref, (low, high) in zip(weight_refs, spans):
        block, inside = at // depth, at % depth
        first = pl.multiple_of((block ^ flip_ref[0]) * depth + inside, 16)
        to = weight_ref.at[pl.ds(first, high - low)]
        loads.append(pltpu.make_async_copy(ref.at[pl.ds(low, high - low)], to, in_sems.at[len(loads)]))
        loads[-1].start()
        at += high - low

    def gather(parts):
        return jnp.concatenate([ref[...].reshape(4 * rows, ref.shape[-1]) for ref in parts], axis=1)

    acts = gather(sides[0])
    for load in loads:
        load.wait()
    total = jnp.dot(acts, weight_ref[...], preferred_element_type=WIDE)
    for kind in range(2):
        here = slice(kind * rows, (kind + 1) * rows)
        keep_ref[here] = total[2 * kind * rows : (2 * kind + 1) * rows]
        send_ref[here] = total[(2 * kind + 1) * rows : (2 * kind + 2) * rows].astype(LOW)
    stores = [
        pltpu.make_async_copy(keep_ref, keep_mine_ref, out_sems.at[0]),
        pltpu.make_async_copy(send_ref, send_mine_ref, out_sems.at[1]),
    ]
    for store in stores:
        store.start()
    total = jnp.dot(gather(sides[1]), weight_ref[...], preferred_element_type=WIDE)
    for kind, out_ref in enumerate((first_ref, second_ref)):
        keep_other_ref[kind * rows : (kind + 1) * rows] = total[2 * kind * rows : (2 * kind + 1) * rows]
        out_ref[...] = total[(2 * kind + 1) * rows : (2 * kind + 2) * rows].astype(LOW)
    for store in stores:
        store.wait()


def project(flip, acts, pieces):
    mine, theirs = zip(*acts)
    weights = [weight for weight, _, _ in pieces]
    spans = [(low, high) for _, low, high in pieces]
    rows, n = mine[0].shape[1], weights[0].shape[1]
    depth = sum(high - low for low, high in spans)
    wide, low, part = (rows, n), (rows, n), (rows // 2, n)
    hbm = pl.BlockSpec(memory_space=pltpu.HBM)
    vmem = pl.BlockSpec(memory_space=pltpu.VMEM)
    return pl.pallas_call(
        functools.partial(project_kernel, len(acts), spans),
        in_specs=[pl.BlockSpec(memory_space=pltpu.SMEM)] + [vmem] * (2 * len(acts)) + [hbm] * len(weights),
        out_specs=[hbm, vmem, hbm, vmem, vmem],
        out_shape=[
            jax.ShapeDtypeStruct(wide, WIDE),
            jax.ShapeDtypeStruct(wide, WIDE),
            jax.ShapeDtypeStruct(low, LOW),
            jax.ShapeDtypeStruct(part, LOW),
            jax.ShapeDtypeStruct(part, LOW),
        ],
        scratch_shapes=[
            pltpu.VMEM((depth, n), LOW),
            pltpu.VMEM(wide, WIDE),
            pltpu.VMEM(low, LOW),
            pltpu.SemaphoreType.DMA((len(weights),)),
            pltpu.SemaphoreType.DMA((2,)),
        ],
        compiler_params=params(),
        cost_estimate=LIGHT,
    )(flip, *mine, *theirs, *weights)


def close_kernel(keep_ref, *refs):
    got_refs, out_ref = refs[:-1], refs[-1]
    first = 0
    for got_ref in got_refs:
        here = slice(first, first + got_ref.shape[0])
        out_ref[here] = (keep_ref[here] + got_ref[...].astype(WIDE)).astype(LOW)
        first = here.stop


def close(keep, *gots):
    return pl.pallas_call(
        close_kernel,
        in_specs=vmem_specs(1 + len(gots)),
        out_specs=vmem_specs(1)[0],
        out_shape=jax.ShapeDtypeStruct(keep.shape, LOW),
        compiler_params=params(),
        cost_estimate=LIGHT,
    )(keep, *gots)


def place_kernel(where_ref, keep_ref, got_ref, other_ref, *refs):
    plain_ref, dual_ref = refs[-2:]
    rows = plain_ref.shape[0]

    @pl.when(pl.program_id(0) == 0)
    def _():
        total = (keep_ref[...] + got_ref[...].astype(WIDE)).astype(LOW)
        plain_ref[...] = total[:rows]
        dual_ref[...] = total[rows:]

    @pl.when(pl.program_id(0) == 1)
    def _():
        plain_ref[...] = other_ref[:rows]
        dual_ref[...] = other_ref[rows:]


def place(outs, width, where, keep, got, other):
    rows, n = other.shape[0] // 2, other.shape[1]
    if n % 128:
        outs = outs or [jnp.zeros((rows, width), LOW)] * 2
        for side, piece in enumerate((close(keep, got), other)):
            parts = (piece[:rows], piece[rows:])
            outs = [lax.dynamic_update_slice(out, part, (0, where[side] * n)) for out, part in zip(outs, parts)]
        return outs
    full = pl.BlockSpec((2 * rows, n), lambda i, w: (0, 0))
    block = pl.BlockSpec((rows, n), lambda i, w: (0, w[i]))
    return pl.pallas_call(
        place_kernel,
        grid_spec=pltpu.PrefetchScalarGridSpec(
            num_scalar_prefetch=1,
            grid=(2,),
            in_specs=[full] * 3 + [pl.BlockSpec(memory_space=pl.ANY)] * len(outs),
            out_specs=[block] * 2,
        ),
        out_shape=[jax.ShapeDtypeStruct((rows, width), LOW)] * 2,
        input_output_aliases={4 + at: at for at in range(len(outs))},
        compiler_params=params(),
        cost_estimate=LIGHT,
    )(where, keep, got, other, *outs)


def body(
    n_dp,
    n_seq,
    queries,
    key_states,
    value_states,
    query_tangent,
    key_tangent,
    value_tangent,
    query_gain,
    key_gain,
    out_weight,
):
    dp = lax.axis_index("dp")
    seq = lax.axis_index("seq")
    n_ring = n_dp // 2
    groups = n_seq // 2
    features = queries.shape[1]
    hdim = features // HEADS
    group_heads = HEADS // n_seq
    few = group_heads * 2 // 5
    chunks = [group_heads * hdim] * (groups - 1) + [(group_heads - few) * hdim, few * hdim]
    starts = [sum(chunks[:at]) for at in range(len(chunks))]
    token = jnp.zeros((1,), jnp.int32)

    def far(array):
        return lax.ppermute(array, "seq", [(i, i ^ 2) for i in range(n_seq)])

    def near(array):
        return lax.ppermute(array, "seq", [(i, i ^ 1) for i in range(n_seq)])

    def across(array):
        return lax.ppermute(array, "dp", [(i, i ^ 1) for i in range(n_dp)])

    def onward(array):
        return lax.ppermute(array, "dp", [(i, (i + 2) % n_dp) for i in range(n_dp)])

    def wait(array):
        nonlocal token
        array, token = lax.optimization_barrier((array, token))
        return array

    def after(array):
        return lax.optimization_barrier((array, token))[0]

    def turn(ring, step):
        ring[step] = wait(ring[step])
        if step + 1 < n_ring:
            ring.append(onward(ring[step]))

    depth = out_weight.shape[0]
    cut = depth * 3 // 5 // 16 * 16
    upper, lower = [out_weight[:cut]], [out_weight[cut:]]
    lower.append(onward(lower[0]))
    upper.append(onward(upper[0]))
    beside = [wait(far(upper[0]))]
    beside.append(onward(beside[0]))
    turn(lower, 1)

    core = jnp.stack([seq % 2])
    arrays = (queries, key_states, value_states, query_tangent, key_tangent, value_tangent)
    packs = [wait(array) for array in pack(core, n_seq, chunks, arrays, jnp.stack([query_gain, key_gain]))]
    query_own, *keyed_own = packs[: 1 + len(chunks)]
    query_other, *keyed_other = packs[1 + len(chunks) :]
    there = wait(near(keyed_other[0]))
    keyed = [[keyed_own[0], there, far(keyed_own[0]), far(there)]]
    for own, other in zip(keyed_own[1:], keyed_other[1:]):
        there = wait(near(other))
        keyed.append([own, there, far(jnp.concatenate([own, there]))])
    queries_both = [query_own, wait(near(query_other))]
    turn(lower, 2)

    acts, swapped = [], []

    def attention(chunk):
        keyed[chunk][-1] = wait(keyed[chunk][-1])
        acts.append(wait(attend(starts[chunk], hdim, queries_both, keyed[chunk])))
        swapped.append(across(acts[-1]))

    turn(upper, 1)
    keyed[0][2] = wait(keyed[0][2])
    turn(beside, 1)
    attention(0)
    for step in range(3, n_ring):
        turn(lower, step)
    later = [wait(jnp.concatenate(lower[step : step + 2])) for step in range(2, n_ring, 2)]
    turn(upper, 2)
    rest = [far(after(lower[0]))]
    attention(1)
    swapped[0] = wait(swapped[0])
    attention(2)
    swapped[1] = wait(swapped[1])
    turn(beside, 2)
    rest += [far(after(piece)) for piece in lower[1:2] + later]
    rest[0] = wait(rest[0])
    swapped[2] = wait(swapped[2])
    acts = list(zip(acts, swapped))
    flip = jnp.stack([seq // 2])

    keeps, mine_sends, sends, mine_got, other = [], [], [], [], []

    def columns(step):
        own = [(upper[step], 0, cut), (lower[step], 0, depth - cut)]
        start = step % 2 * (depth - cut) if step > 1 else 0
        got = rest[step] if step < 2 else rest[1 + step // 2]
        theirs = [(beside[step], 0, cut), (got, start, start + depth - cut)]
        keep_mine, keep_other, send_mine, *send_other = project(after(flip), acts, own + theirs)
        keeps.append((keep_mine, keep_other))
        sends.append([near(wait(array)) for array in send_other])
        mine_sends.append(send_mine)

    def finish(step):
        other.append(across(wait(close(keeps[step][1], *[wait(array) for array in sends[step]]))))
        mine_got.append(near(mine_sends[step]))

    outs = []

    def put(step):
        pair = (dp // 2 - step) % n_ring
        where = jnp.stack([2 * pair + dp % 2, 2 * pair + 1 - dp % 2]).astype(jnp.int32) + token
        return place(outs, n_dp * out_weight.shape[1], where, keeps[step][0], wait(mine_got[step]), wait(other[step]))

    columns(0)
    for step in range(3, n_ring):
        turn(upper, step)
    rest[1] = wait(rest[1])
    finish(0)
    columns(1)
    finish(1)
    for step in range(2, n_ring, 2):
        other[step - 2] = wait(other[step - 2])
        rest[1 + step // 2] = wait(rest[1 + step // 2])
        for ahead in range(max(step, 3), step + 2):
            turn(beside, ahead)
        columns(step)
        finish(step)
        columns(step + 1)
        other[step - 1] = wait(other[step - 1])
        finish(step + 1)
    other[-2] = wait(other[-2])
    for step in range(n_ring):
        outs = put(step)
    return tuple(outs)


def solution(mesh):
    rows = P(("dp", "seq"), None)
    return jax.shard_map(
        functools.partial(body, mesh.shape["dp"], mesh.shape["seq"]),
        mesh=mesh,
        in_specs=(rows,) * 6 + (P(), P(), P("seq", "dp")),
        out_specs=(rows, rows),
        check_vma=False,
    )
```

```python
import functools

import jax
import jax.numpy as jnp
from jax import lax
from jax.experimental import pallas as pl
from jax.experimental.pallas import tpu as pltpu
from jax.sharding import PartitionSpec as P

HEADS = 20
EPS = 1e-06
VMEM_BYTES = 10 * 1024 * 1024
ROW_STEP = 32

LOW = jnp.bfloat16
WIDE = jnp.float32
LIGHT = pl.CostEstimate(flops=1, transcendentals=0, bytes_accessed=1)


def params():
    return pltpu.CompilerParams(vmem_limit_bytes=VMEM_BYTES)


def vmem_specs(count):
    return [pl.BlockSpec(memory_space=pltpu.VMEM)] * count


def pack_kernel(n_seq, chunks, core_ref, *refs):
    query_ref, key_ref, value_ref, dquery_ref, dkey_ref, dvalue_ref, gains_ref = refs[:7]
    out_refs = refs[7:]
    n_chunks = len(chunks)
    group = query_ref.shape[-1] // n_seq

    def statistics(primal_ref, tangent_ref):
        primal = primal_ref[...].astype(WIDE)
        tangent = tangent_ref[...].astype(WIDE)
        inverse = lax.rsqrt(jnp.mean(primal * primal, axis=-1, keepdims=True) + EPS)
        across = jnp.mean(primal * tangent, axis=-1, keepdims=True)
        return inverse, inverse * inverse * inverse * across

    query_stats = statistics(query_ref, dquery_ref)
    key_stats = statistics(key_ref, dkey_ref)

    def normed(primal_ref, tangent_ref, which, stats, lanes):
        primal = primal_ref[:, lanes].astype(WIDE)
        tangent = tangent_ref[:, lanes].astype(WIDE)
        gain = gains_ref[which : which + 1, lanes]
        inverse, slope = stats
        return (primal * inverse * gain).astype(LOW), (gain * (tangent * inverse - primal * slope)).astype(LOW)

    for side in range(2):
        core = core_ref[0] if side == 0 else 1 - core_ref[0]
        queries_ref, *keyed_refs = out_refs[side * (1 + n_chunks) : (side + 1) * (1 + n_chunks)]
        for at in range(n_seq // 2):
            lanes = pl.ds(pl.multiple_of((2 * at + core) * group, 128), group)
            here = slice(at * group, (at + 1) * group)
            plain, dual = normed(query_ref, dquery_ref, 0, query_stats, lanes)
            queries_ref[0, :, here] = plain
            queries_ref[1, :, here] = dual
            four = normed(key_ref, dkey_ref, 1, key_stats, lanes)
            four += (value_ref[:, lanes], dvalue_ref[:, lanes])
            start = 0
            for keyed_ref, width in zip(keyed_refs, chunks):
                low, high = max(start, here.start), min(start + width, here.stop)
                if low < high:
                    for which, part in enumerate(four):
                        keyed_ref[which, :, low - start : high - start] = part[:, low - here.start : high - here.start]
                start += width


def pack(core, n_seq, chunks, arrays, gains):
    rows, features = arrays[0].shape
    step = min(rows, ROW_STEP)
    row_block = pl.BlockSpec((step, features), lambda i, c: (i, 0))
    gain_block = pl.BlockSpec((2, features), lambda i, c: (0, 0))
    kinds = [(2, features // 2)] + [(4, width) for width in chunks]
    kinds = kinds + kinds
    return pl.pallas_call(
        functools.partial(pack_kernel, n_seq, chunks),
        grid_spec=pltpu.PrefetchScalarGridSpec(
            num_scalar_prefetch=1,
            grid=(rows // step,),
            in_specs=[row_block] * 6 + [gain_block],
            out_specs=[pl.BlockSpec((count, step, width), lambda i, c: (0, i, 0)) for count, width in kinds],
        ),
        out_shape=[jax.ShapeDtypeStruct((count, rows, width), LOW) for count, width in kinds],
        compiler_params=params(),
        cost_estimate=LIGHT,
    )(core, *arrays, gains)


def attend_kernel(n_queries, *refs):
    query_refs, keyed_refs, out_ref = refs[:n_queries], refs[n_queries:-1], refs[-1]

    def stack(which, some_refs, kinds):
        parts = [ref[at] for ref in some_refs for at in range(which, ref.shape[0], kinds)]
        return jnp.concatenate(parts, axis=0)

    query, query_dual = (stack(which, query_refs, 2) for which in range(2))
    key, key_dual, value, value_dual = (stack(which, keyed_refs, 4) for which in range(4))
    factor = query.shape[-1] ** (-0.5)
    last = (((1,), (1,)), ((), ()))
    scores = lax.dot_general(query, key, last, preferred_element_type=WIDE) * factor
    dual_scores = (
        lax.dot_general(
            jnp.concatenate([query_dual, query], axis=1),
            jnp.concatenate([key, key_dual], axis=1),
            last,
            preferred_element_type=WIDE,
        )
        * factor
    )
    raised = jnp.exp(scores - jnp.max(scores, axis=-1, keepdims=True))
    probs = raised * (1.0 / jnp.sum(raised, axis=-1, keepdims=True))
    spread = probs * (dual_scores - jnp.sum(probs * dual_scores, axis=-1, keepdims=True))
    probs_low = probs.astype(LOW)
    spread_low = spread.astype(LOW)
    out_ref[0] = jnp.dot(probs_low, value, preferred_element_type=WIDE).astype(LOW)
    out_ref[1] = (
        jnp.dot(probs_low, value_dual, preferred_element_type=WIDE)
        + jnp.dot(spread_low, value, preferred_element_type=WIDE)
    ).astype(LOW)


def attend(start, hdim, queries, keyed):
    rows = queries[0].shape[1]
    width = keyed[0].shape[2]
    first = start // hdim
    return pl.pallas_call(
        functools.partial(attend_kernel, len(queries)),
        grid=(width // hdim,),
        in_specs=[pl.BlockSpec((2, rows, hdim), lambda h: (0, 0, first + h))] * len(queries)
        + [pl.BlockSpec((array.shape[0], rows, hdim), lambda h: (0, 0, h)) for array in keyed],
        out_specs=pl.BlockSpec((2, len(queries) * rows, hdim), lambda h: (0, 0, h)),
        out_shape=jax.ShapeDtypeStruct((2, len(queries) * rows, width), LOW),
        compiler_params=params(),
        cost_estimate=LIGHT,
    )(*queries, *keyed)


def project_kernel(n_parts, spans, flip_ref, *refs):
    part_refs, weight_refs = refs[:n_parts], refs[n_parts : n_parts + len(spans)]
    keep_ref, *send_refs, weight_ref = refs[n_parts + len(spans) :]
    rows = keep_ref.shape[0] // 2
    depth = weight_ref.shape[0] // 2
    at = 0
    for ref, (low, high) in zip(weight_refs, spans):
        block, inside = at // depth, at % depth
        first = pl.multiple_of((block ^ flip_ref[0]) * depth + inside, 16)
        weight_ref[pl.ds(first, high - low)] = ref[low:high]
        at += high - low
    acts = jnp.concatenate([ref[...].reshape(4 * rows, ref.shape[-1]) for ref in part_refs], axis=1)
    total = jnp.dot(acts, weight_ref[...], preferred_element_type=WIDE)
    for kind in range(2):
        here = slice(kind * rows, (kind + 1) * rows)
        first = 2 * kind * rows
        keep_ref[here] = total[first : first + rows]
        send_refs[kind][...] = total[first + rows : first + 2 * rows].astype(LOW)


def project(flip, acts, pieces):
    weights = [weight for weight, _, _ in pieces]
    spans = [(low, high) for _, low, high in pieces]
    rows, n = acts[0].shape[1], weights[0].shape[1]
    depth = sum(high - low for low, high in spans)
    return pl.pallas_call(
        functools.partial(project_kernel, len(acts), spans),
        in_specs=[pl.BlockSpec(memory_space=pltpu.SMEM)] + vmem_specs(len(acts) + len(weights)),
        out_specs=vmem_specs(3),
        out_shape=[jax.ShapeDtypeStruct((rows, n), WIDE)] + [jax.ShapeDtypeStruct((rows // 2, n), LOW)] * 2,
        scratch_shapes=[pltpu.VMEM((depth, n), LOW)],
        compiler_params=params(),
        cost_estimate=LIGHT,
    )(flip, *acts, *weights)


def close_kernel(keep_ref, *refs):
    got_refs, out_ref = refs[:-1], refs[-1]
    first = 0
    for got_ref in got_refs:
        here = slice(first, first + got_ref.shape[0])
        out_ref[here] = (keep_ref[here] + got_ref[...].astype(WIDE)).astype(LOW)
        first = here.stop


def close(keep, *gots):
    return pl.pallas_call(
        close_kernel,
        in_specs=vmem_specs(1 + len(gots)),
        out_specs=vmem_specs(1)[0],
        out_shape=jax.ShapeDtypeStruct(keep.shape, LOW),
        compiler_params=params(),
        cost_estimate=LIGHT,
    )(keep, *gots)


def place_kernel(where_ref, keep_ref, got_ref, dual_got_ref, other_ref, *refs):
    plain_ref, dual_ref = refs[-2:]
    rows = plain_ref.shape[0]

    @pl.when(pl.program_id(0) == 0)
    def _():
        plain_ref[...] = (keep_ref[:rows] + got_ref[...].astype(WIDE)).astype(LOW)
        dual_ref[...] = (keep_ref[rows:] + dual_got_ref[...].astype(WIDE)).astype(LOW)

    @pl.when(pl.program_id(0) == 1)
    def _():
        plain_ref[...] = other_ref[:rows]
        dual_ref[...] = other_ref[rows:]


def place(outs, width, where, keep, gots, other):
    rows, n = other.shape[0] // 2, other.shape[1]
    if n % 128:
        outs = outs or [jnp.zeros((rows, width), LOW)] * 2
        for side, piece in enumerate((close(keep, *gots), other)):
            parts = (piece[:rows], piece[rows:])
            outs = [lax.dynamic_update_slice(out, part, (0, where[side] * n)) for out, part in zip(outs, parts)]
        return outs
    full, half = (pl.BlockSpec((count * rows, n), lambda i, w: (0, 0)) for count in (2, 1))
    block = pl.BlockSpec((rows, n), lambda i, w: (0, w[i]))
    return pl.pallas_call(
        place_kernel,
        grid_spec=pltpu.PrefetchScalarGridSpec(
            num_scalar_prefetch=1,
            grid=(2,),
            in_specs=[full, half, half, full] + [pl.BlockSpec(memory_space=pl.ANY)] * len(outs),
            out_specs=[block] * 2,
        ),
        out_shape=[jax.ShapeDtypeStruct((rows, width), LOW)] * 2,
        input_output_aliases={5 + at: at for at in range(len(outs))},
        compiler_params=params(),
        cost_estimate=LIGHT,
    )(where, keep, *gots, other, *outs)


def body(
    n_dp,
    n_seq,
    queries,
    key_states,
    value_states,
    query_tangent,
    key_tangent,
    value_tangent,
    query_gain,
    key_gain,
    out_weight,
):
    dp = lax.axis_index("dp")
    seq = lax.axis_index("seq")
    n_ring = n_dp // 2
    groups = n_seq // 2
    features = queries.shape[1]
    hdim = features // HEADS
    group_heads = HEADS // n_seq
    few = group_heads * 2 // 5
    chunks = [group_heads * hdim] * (groups - 1) + [(group_heads - few) * hdim, few * hdim]
    starts = [sum(chunks[:at]) for at in range(len(chunks))]
    token = jnp.zeros((1,), jnp.int32)

    def far(array):
        return lax.ppermute(array, "seq", [(i, i ^ 2) for i in range(n_seq)])

    def near(array):
        return lax.ppermute(array, "seq", [(i, i ^ 1) for i in range(n_seq)])

    def across(array):
        return lax.ppermute(array, "dp", [(i, i ^ 1) for i in range(n_dp)])

    def onward(array):
        return lax.ppermute(array, "dp", [(i, (i + 2) % n_dp) for i in range(n_dp)])

    def wait(array):
        nonlocal token
        array, token = lax.optimization_barrier((array, token))
        return array

    def after(array):
        return lax.optimization_barrier((array, token))[0]

    def turn(ring, step):
        ring[step] = wait(ring[step])
        if step + 1 < n_ring:
            ring.append(onward(ring[step]))

    depth = out_weight.shape[0]
    cut = depth * 3 // 5 // 16 * 16
    upper, lower = [out_weight[:cut]], [out_weight[cut:]]
    lower.append(onward(lower[0]))
    upper.append(onward(upper[0]))
    beside = [wait(far(upper[0]))]
    beside.append(onward(beside[0]))
    turn(lower, 1)

    core = jnp.stack([seq % 2])
    arrays = (queries, key_states, value_states, query_tangent, key_tangent, value_tangent)
    packs = [wait(array) for array in pack(core, n_seq, chunks, arrays, jnp.stack([query_gain, key_gain]))]
    query_own, *keyed_own = packs[: 1 + len(chunks)]
    query_other, *keyed_other = packs[1 + len(chunks) :]
    there = wait(near(keyed_other[0]))
    keyed = [[keyed_own[0], there, far(keyed_own[0]), far(there)]]
    for own, other in zip(keyed_own[1:], keyed_other[1:]):
        there = wait(near(other))
        keyed.append([own, there, far(jnp.concatenate([own, there]))])
    queries_both = [query_own, wait(near(query_other))]
    turn(lower, 2)

    acts, swapped = [], []

    def attention(chunk):
        keyed[chunk][-1] = wait(keyed[chunk][-1])
        acts.append(wait(attend(starts[chunk], hdim, queries_both, keyed[chunk])))
        swapped.append(across(acts[-1]))

    turn(upper, 1)
    keyed[0][2] = wait(keyed[0][2])
    turn(beside, 1)
    attention(0)
    for step in range(3, n_ring):
        turn(lower, step)
    later = [wait(jnp.concatenate(lower[step : step + 2])) for step in range(2, n_ring, 2)]
    turn(upper, 2)
    rest = [far(after(lower[0]))]
    attention(1)
    swapped[0] = wait(swapped[0])
    attention(2)
    swapped[1] = wait(swapped[1])
    turn(beside, 2)
    rest += [far(after(piece)) for piece in lower[1:2] + later]
    rest[0] = wait(rest[0])
    swapped[2] = wait(swapped[2])
    acts = list(zip(acts, swapped))
    flip = jnp.stack([seq // 2])

    kept, got, other = {}, {}, []

    def columns(step, side):
        own = [(upper[step], 0, cut), (lower[step], 0, depth - cut)]
        start = step % 2 * (depth - cut) if step > 1 else 0
        part = rest[step] if step < 2 else rest[1 + step // 2]
        theirs = [(beside[step], 0, cut), (part, start, start + depth - cut)]
        keep, *send = project(after(flip), [pair[side] for pair in acts], own + theirs)
        kept[step, side] = keep
        got[step, side] = [near(wait(array)) for array in send]

    def send(step):
        columns(step, 1)
        other.append(across(wait(close(kept[step, 1], *[wait(array) for array in got[step, 1]]))))

    def stay(step):
        columns(step, 0)

    outs = []

    def put(step):
        pair = (dp // 2 - step) % n_ring
        where = jnp.stack([2 * pair + dp % 2, 2 * pair + 1 - dp % 2]).astype(jnp.int32) + token
        gots = [wait(array) for array in got[step, 0]]
        return place(outs, n_dp * out_weight.shape[1], where, kept[step, 0], gots, wait(other[step]))

    send(0)
    for step in range(3, n_ring):
        turn(upper, step)
    rest[1] = wait(rest[1])
    send(1)
    for step in range(2, n_ring, 2):
        stay(step - 2)
        other[step - 2] = wait(other[step - 2])
        rest[1 + step // 2] = wait(rest[1 + step // 2])
        if step > 2:
            turn(beside, step)
        send(step)
        stay(step - 1)
        turn(beside, step + 1)
        other[step - 1] = wait(other[step - 1])
        send(step + 1)
    other[-2] = wait(other[-2])
    stay(n_ring - 2)
    stay(n_ring - 1)
    for step in range(n_ring):
        outs = put(step)
    return tuple(outs)


def solution(mesh):
    rows = P(("dp", "seq"), None)
    return jax.shard_map(
        functools.partial(body, mesh.shape["dp"], mesh.shape["seq"]),
        mesh=mesh,
        in_specs=(rows,) * 6 + (P(), P(), P("seq", "dp")),
        out_specs=(rows, rows),
        check_vma=False,
    )
```

```python
import functools

import jax
import jax.numpy as jnp
from jax import lax
from jax.experimental import pallas as pl
from jax.experimental.pallas import tpu as pltpu
from jax.sharding import PartitionSpec as P

HEADS = 20
EPS = 1e-06
VMEM_BYTES = 10 * 1024 * 1024
ROW_STEP = 32

LOW = jnp.bfloat16
WIDE = jnp.float32
LIGHT = pl.CostEstimate(flops=1, transcendentals=0, bytes_accessed=1)


def params():
    return pltpu.CompilerParams(vmem_limit_bytes=VMEM_BYTES)


def vmem_specs(count):
    return [pl.BlockSpec(memory_space=pltpu.VMEM)] * count


def pack_kernel(n_seq, chunks, core_ref, *refs):
    query_ref, key_ref, value_ref, dquery_ref, dkey_ref, dvalue_ref, gains_ref = refs[:7]
    out_refs = refs[7:]
    n_chunks = len(chunks)
    group = query_ref.shape[-1] // n_seq

    def statistics(primal_ref, tangent_ref):
        primal = primal_ref[...].astype(WIDE)
        tangent = tangent_ref[...].astype(WIDE)
        inverse = lax.rsqrt(jnp.mean(primal * primal, axis=-1, keepdims=True) + EPS)
        across = jnp.mean(primal * tangent, axis=-1, keepdims=True)
        return inverse, inverse * inverse * inverse * across

    query_stats = statistics(query_ref, dquery_ref)
    key_stats = statistics(key_ref, dkey_ref)

    def normed(primal_ref, tangent_ref, which, stats, lanes):
        primal = primal_ref[:, lanes].astype(WIDE)
        tangent = tangent_ref[:, lanes].astype(WIDE)
        gain = gains_ref[which : which + 1, lanes]
        inverse, slope = stats
        return (primal * inverse * gain).astype(LOW), (gain * (tangent * inverse - primal * slope)).astype(LOW)

    for side in range(2):
        core = core_ref[0] if side == 0 else 1 - core_ref[0]
        queries_ref, *keyed_refs = out_refs[side * (1 + n_chunks) : (side + 1) * (1 + n_chunks)]
        for at in range(n_seq // 2):
            lanes = pl.ds(pl.multiple_of((2 * at + core) * group, 128), group)
            here = slice(at * group, (at + 1) * group)
            plain, dual = normed(query_ref, dquery_ref, 0, query_stats, lanes)
            queries_ref[0, :, here] = plain
            queries_ref[1, :, here] = dual
            four = normed(key_ref, dkey_ref, 1, key_stats, lanes)
            four += (value_ref[:, lanes], dvalue_ref[:, lanes])
            start = 0
            for keyed_ref, width in zip(keyed_refs, chunks):
                low, high = max(start, here.start), min(start + width, here.stop)
                if low < high:
                    for which, part in enumerate(four):
                        keyed_ref[which, :, low - start : high - start] = part[:, low - here.start : high - here.start]
                start += width


def pack(core, n_seq, chunks, arrays, gains):
    rows, features = arrays[0].shape
    step = min(rows, ROW_STEP)
    row_block = pl.BlockSpec((step, features), lambda i, c: (i, 0))
    gain_block = pl.BlockSpec((2, features), lambda i, c: (0, 0))
    kinds = [(2, features // 2)] + [(4, width) for width in chunks]
    kinds = kinds + kinds
    return pl.pallas_call(
        functools.partial(pack_kernel, n_seq, chunks),
        grid_spec=pltpu.PrefetchScalarGridSpec(
            num_scalar_prefetch=1,
            grid=(rows // step,),
            in_specs=[row_block] * 6 + [gain_block],
            out_specs=[pl.BlockSpec((count, step, width), lambda i, c: (0, i, 0)) for count, width in kinds],
        ),
        out_shape=[jax.ShapeDtypeStruct((count, rows, width), LOW) for count, width in kinds],
        compiler_params=params(),
        cost_estimate=LIGHT,
    )(core, *arrays, gains)


def attend_kernel(n_queries, *refs):
    query_refs, keyed_refs, out_ref = refs[:n_queries], refs[n_queries:-1], refs[-1]

    def stack(which, some_refs, kinds):
        parts = [ref[at] for ref in some_refs for at in range(which, ref.shape[0], kinds)]
        return jnp.concatenate(parts, axis=0)

    query, query_dual = (stack(which, query_refs, 2) for which in range(2))
    key, key_dual, value, value_dual = (stack(which, keyed_refs, 4) for which in range(4))
    factor = query.shape[-1] ** (-0.5)
    last = (((1,), (1,)), ((), ()))
    scores = lax.dot_general(query, key, last, preferred_element_type=WIDE) * factor
    dual_scores = (
        lax.dot_general(
            jnp.concatenate([query_dual, query], axis=1),
            jnp.concatenate([key, key_dual], axis=1),
            last,
            preferred_element_type=WIDE,
        )
        * factor
    )
    raised = jnp.exp(scores - jnp.max(scores, axis=-1, keepdims=True))
    probs = raised * (1.0 / jnp.sum(raised, axis=-1, keepdims=True))
    spread = probs * (dual_scores - jnp.sum(probs * dual_scores, axis=-1, keepdims=True))
    probs_low = probs.astype(LOW)
    spread_low = spread.astype(LOW)
    out_ref[0] = jnp.dot(probs_low, value, preferred_element_type=WIDE).astype(LOW)
    out_ref[1] = (
        jnp.dot(probs_low, value_dual, preferred_element_type=WIDE)
        + jnp.dot(spread_low, value, preferred_element_type=WIDE)
    ).astype(LOW)


def attend(start, hdim, queries, keyed):
    rows = queries[0].shape[1]
    width = keyed[0].shape[2]
    first = start // hdim
    return pl.pallas_call(
        functools.partial(attend_kernel, len(queries)),
        grid=(width // hdim,),
        in_specs=[pl.BlockSpec((2, rows, hdim), lambda h: (0, 0, first + h))] * len(queries)
        + [pl.BlockSpec((array.shape[0], rows, hdim), lambda h: (0, 0, h)) for array in keyed],
        out_specs=pl.BlockSpec((2, len(queries) * rows, hdim), lambda h: (0, 0, h)),
        out_shape=jax.ShapeDtypeStruct((2, len(queries) * rows, width), LOW),
        compiler_params=params(),
        cost_estimate=LIGHT,
    )(*queries, *keyed)


def project_kernel(n_chunks, spans, flip_ref, *refs):
    sides = refs[:n_chunks], refs[n_chunks : 2 * n_chunks]
    weight_refs, out_refs, weight_ref = refs[2 * n_chunks : -6], refs[-6:-1], refs[-1]
    rows = out_refs[0].shape[0] // 2
    depth = weight_ref.shape[0] // 2
    at = 0
    for ref, (low, high) in zip(weight_refs, spans):
        block, inside = at // depth, at % depth
        first = pl.multiple_of((block ^ flip_ref[0]) * depth + inside, 16)
        weight_ref[pl.ds(first, high - low)] = ref[low:high]
        at += high - low
    weight = weight_ref[...]
    for side, parts in enumerate(sides):
        acts = jnp.concatenate([ref[...].reshape(4 * rows, ref.shape[-1]) for ref in parts], axis=1)
        total = jnp.dot(acts, weight, preferred_element_type=WIDE)
        for kind in range(2):
            first = 2 * kind * rows
            here = slice(kind * rows, (kind + 1) * rows)
            out_refs[side][here] = total[first : first + rows]
            low = total[first + rows : first + 2 * rows].astype(LOW)
            if side:
                out_refs[3 + kind][...] = low
            else:
                out_refs[2][here] = low


def project(flip, acts, pieces):
    mine, theirs = zip(*acts)
    weights = [weight for weight, _, _ in pieces]
    spans = [(low, high) for _, low, high in pieces]
    rows, n = mine[0].shape[1], weights[0].shape[1]
    depth = sum(high - low for low, high in spans)
    return pl.pallas_call(
        functools.partial(project_kernel, len(acts), spans),
        in_specs=[pl.BlockSpec(memory_space=pltpu.SMEM)] + vmem_specs(2 * len(acts) + len(weights)),
        out_specs=vmem_specs(5),
        out_shape=[jax.ShapeDtypeStruct((rows, n), WIDE)] * 2
        + [jax.ShapeDtypeStruct((rows, n), LOW)]
        + [jax.ShapeDtypeStruct((rows // 2, n), LOW)] * 2,
        scratch_shapes=[pltpu.VMEM((depth, n), LOW)],
        compiler_params=params(),
        cost_estimate=LIGHT,
    )(flip, *mine, *theirs, *weights)


def close_kernel(keep_ref, *refs):
    got_refs, out_ref = refs[:-1], refs[-1]
    first = 0
    for got_ref in got_refs:
        here = slice(first, first + got_ref.shape[0])
        out_ref[here] = (keep_ref[here] + got_ref[...].astype(WIDE)).astype(LOW)
        first = here.stop


def close(keep, *gots):
    return pl.pallas_call(
        close_kernel,
        in_specs=vmem_specs(1 + len(gots)),
        out_specs=vmem_specs(1)[0],
        out_shape=jax.ShapeDtypeStruct(keep.shape, LOW),
        compiler_params=params(),
        cost_estimate=LIGHT,
    )(keep, *gots)


def place_kernel(where_ref, mine_ref, other_ref, *refs):
    plain_ref, dual_ref = refs[-2:]
    rows = plain_ref.shape[0]

    @pl.when(pl.program_id(0) == 0)
    def _():
        plain_ref[...] = mine_ref[:rows]
        dual_ref[...] = mine_ref[rows:]

    @pl.when(pl.program_id(0) == 1)
    def _():
        plain_ref[...] = other_ref[:rows]
        dual_ref[...] = other_ref[rows:]


def place(outs, width, where, mine, other):
    rows, n = other.shape[0] // 2, other.shape[1]
    if n % 128:
        outs = outs or [jnp.zeros((rows, width), LOW)] * 2
        for side, piece in enumerate((mine, other)):
            parts = (piece[:rows], piece[rows:])
            outs = [lax.dynamic_update_slice(out, part, (0, where[side] * n)) for out, part in zip(outs, parts)]
        return outs
    full = pl.BlockSpec((2 * rows, n), lambda i, w: (0, 0))
    block = pl.BlockSpec((rows, n), lambda i, w: (0, w[i]))
    return pl.pallas_call(
        place_kernel,
        grid_spec=pltpu.PrefetchScalarGridSpec(
            num_scalar_prefetch=1,
            grid=(2,),
            in_specs=[full] * 2 + [pl.BlockSpec(memory_space=pl.ANY)] * len(outs),
            out_specs=[block] * 2,
        ),
        out_shape=[jax.ShapeDtypeStruct((rows, width), LOW)] * 2,
        input_output_aliases={3 + at: at for at in range(len(outs))},
        compiler_params=params(),
        cost_estimate=LIGHT,
    )(where, mine, other, *outs)


def body(
    n_dp,
    n_seq,
    queries,
    key_states,
    value_states,
    query_tangent,
    key_tangent,
    value_tangent,
    query_gain,
    key_gain,
    out_weight,
):
    dp = lax.axis_index("dp")
    seq = lax.axis_index("seq")
    n_ring = n_dp // 2
    groups = n_seq // 2
    features = queries.shape[1]
    hdim = features // HEADS
    group_heads = HEADS // n_seq
    few = group_heads * 2 // 5
    chunks = [group_heads * hdim] * (groups - 1) + [(group_heads - few) * hdim, few * hdim]
    starts = [sum(chunks[:at]) for at in range(len(chunks))]
    token = jnp.zeros((1,), jnp.int32)

    def far(array):
        return lax.ppermute(array, "seq", [(i, i ^ 2) for i in range(n_seq)])

    def near(array):
        return lax.ppermute(array, "seq", [(i, i ^ 1) for i in range(n_seq)])

    def across(array):
        return lax.ppermute(array, "dp", [(i, i ^ 1) for i in range(n_dp)])

    def onward(array):
        return lax.ppermute(array, "dp", [(i, (i + 2) % n_dp) for i in range(n_dp)])

    def wait(array):
        nonlocal token
        array, token = lax.optimization_barrier((array, token))
        return array

    def after(array):
        return lax.optimization_barrier((array, token))[0]

    def turn(ring, step):
        ring[step] = wait(ring[step])
        if step + 1 < n_ring:
            ring.append(onward(ring[step]))

    depth = out_weight.shape[0]
    cut = depth * 3 // 5 // 16 * 16
    upper, lower = [out_weight[:cut]], [out_weight[cut:]]
    lower.append(onward(lower[0]))
    upper.append(onward(upper[0]))
    beside = [wait(far(upper[0]))]
    beside.append(onward(beside[0]))
    turn(lower, 1)

    core = jnp.stack([seq % 2])
    arrays = (queries, key_states, value_states, query_tangent, key_tangent, value_tangent)
    packs = [wait(array) for array in pack(core, n_seq, chunks, arrays, jnp.stack([query_gain, key_gain]))]
    query_own, *keyed_own = packs[: 1 + len(chunks)]
    query_other, *keyed_other = packs[1 + len(chunks) :]
    there = wait(near(keyed_other[0]))
    keyed = [[keyed_own[0], there, far(keyed_own[0]), far(there)]]
    for own, other in zip(keyed_own[1:], keyed_other[1:]):
        there = wait(near(other))
        keyed.append([own, there, far(jnp.concatenate([own, there]))])
    queries_both = [query_own, wait(near(query_other))]
    turn(lower, 2)

    acts, swapped = [], []

    def attention(chunk):
        keyed[chunk][-1] = wait(keyed[chunk][-1])
        acts.append(wait(attend(starts[chunk], hdim, queries_both, keyed[chunk])))
        swapped.append(across(acts[-1]))

    turn(upper, 1)
    keyed[0][2] = wait(keyed[0][2])
    turn(beside, 1)
    attention(0)
    for step in range(3, n_ring):
        turn(lower, step)
    later = [wait(jnp.concatenate(lower[step : step + 2])) for step in range(2, n_ring, 2)]
    turn(upper, 2)
    rest = [far(after(lower[0]))]
    attention(1)
    swapped[0] = wait(swapped[0])
    attention(2)
    swapped[1] = wait(swapped[1])
    turn(beside, 2)
    rest += [far(after(piece)) for piece in lower[1:2] + later]
    rest[0] = wait(rest[0])
    swapped[2] = wait(swapped[2])
    acts = list(zip(acts, swapped))
    flip = jnp.stack([seq // 2])

    keeps, sends, mine_got, mine, other = [], [], [], [], []

    def columns(step):
        own = [(upper[step], 0, cut), (lower[step], 0, depth - cut)] if step else [(out_weight, 0, depth)]
        start = step % 2 * (depth - cut) if step > 1 else 0
        got = rest[step] if step < 2 else rest[1 + step // 2]
        theirs = [(beside[step], 0, cut), (got, start, start + depth - cut)]
        keep_mine, keep_other, *low = project(after(flip), acts, own + theirs)
        keeps.append((keep_mine, keep_other))
        sends.append([near(wait(array)) for array in low[1:]])
        mine_got.append([wait(array) for array in low[:1]])

    def send(step):
        if step > 2:
            other[step - 1] = wait(other[step - 1])
        other.append(across(wait(close(keeps[step][1], *[wait(array) for array in sends[step]]))))
        mine_got[step] = [near(after(array)) for array in mine_got[step]]
        if step and not step > 2:
            other[step - 1] = wait(other[step - 1])

    def stay(step):
        mine.append(wait(close(keeps[step][0], *[wait(array) for array in mine_got[step]])))

    outs = []

    def put(step):
        pair = (dp // 2 - step) % n_ring
        where = jnp.stack([2 * pair + dp % 2, 2 * pair + 1 - dp % 2]).astype(jnp.int32) + token
        return place(outs, n_dp * out_weight.shape[1], where, mine[step], other[step])

    columns(0)
    for step in range(3, n_ring):
        turn(upper, step)
    rest[1] = wait(rest[1])
    send(0)
    columns(1)
    send(1)
    stay(0)
    for step in range(2, n_ring, 2):
        rest[1 + step // 2] = wait(rest[1 + step // 2])
        if step > 2:
            turn(beside, step)
        columns(step)
        send(step)
        stay(step - 1)
        turn(beside, step + 1)
        columns(step + 1)
        send(step + 1)
        stay(step)
    stay(n_ring - 1)
    for step in range(n_ring - 1):
        outs = [wait(out) for out in put(step)]
    other[-1] = wait(other[-1])
    return tuple(put(n_ring - 1))


def solution(mesh):
    rows = P(("dp", "seq"), None)
    return jax.shard_map(
        functools.partial(body, mesh.shape["dp"], mesh.shape["seq"]),
        mesh=mesh,
        in_specs=(rows,) * 6 + (P(), P(), P("seq", "dp")),
        out_specs=(rows, rows),
        check_vma=False,
    )
```

```python
import functools

import jax
import jax.numpy as jnp
from jax import lax
from jax.experimental import pallas as pl
from jax.experimental.pallas import tpu as pltpu
from jax.sharding import PartitionSpec as P

HEADS = 20
EPS = 1e-06
VMEM_BYTES = 10 * 1024 * 1024
ROW_STEP = 32

LOW = jnp.bfloat16
WIDE = jnp.float32
LIGHT = pl.CostEstimate(flops=1, transcendentals=0, bytes_accessed=1)


def params():
    return pltpu.CompilerParams(vmem_limit_bytes=VMEM_BYTES)


def vmem_specs(count):
    return [pl.BlockSpec(memory_space=pltpu.VMEM)] * count


def pack_kernel(n_seq, chunks, core_ref, *refs):
    query_ref, key_ref, value_ref, dquery_ref, dkey_ref, dvalue_ref, gains_ref = refs[:7]
    out_refs = refs[7:]
    n_chunks = len(chunks)
    group = query_ref.shape[-1] // n_seq

    def statistics(primal_ref, tangent_ref):
        primal = primal_ref[...].astype(WIDE)
        tangent = tangent_ref[...].astype(WIDE)
        inverse = lax.rsqrt(jnp.mean(primal * primal, axis=-1, keepdims=True) + EPS)
        across = jnp.mean(primal * tangent, axis=-1, keepdims=True)
        return inverse, inverse * inverse * inverse * across

    query_stats = statistics(query_ref, dquery_ref)
    key_stats = statistics(key_ref, dkey_ref)

    def normed(primal_ref, tangent_ref, which, stats, lanes):
        primal = primal_ref[:, lanes].astype(WIDE)
        tangent = tangent_ref[:, lanes].astype(WIDE)
        gain = gains_ref[which : which + 1, lanes]
        inverse, slope = stats
        return (primal * inverse * gain).astype(LOW), (gain * (tangent * inverse - primal * slope)).astype(LOW)

    for side in range(2):
        core = core_ref[0] if side == 0 else 1 - core_ref[0]
        queries_ref, *keyed_refs = out_refs[side * (1 + n_chunks) : (side + 1) * (1 + n_chunks)]
        for at in range(n_seq // 2):
            lanes = pl.ds(pl.multiple_of((2 * at + core) * group, 128), group)
            here = slice(at * group, (at + 1) * group)
            plain, dual = normed(query_ref, dquery_ref, 0, query_stats, lanes)
            queries_ref[0, :, here] = plain
            queries_ref[1, :, here] = dual
            four = normed(key_ref, dkey_ref, 1, key_stats, lanes)
            four += (value_ref[:, lanes], dvalue_ref[:, lanes])
            start = 0
            for keyed_ref, width in zip(keyed_refs, chunks):
                low, high = max(start, here.start), min(start + width, here.stop)
                if low < high:
                    for which, part in enumerate(four):
                        keyed_ref[which, :, low - start : high - start] = part[:, low - here.start : high - here.start]
                start += width


def pack(core, n_seq, chunks, arrays, gains):
    rows, features = arrays[0].shape
    step = min(rows, ROW_STEP)
    row_block = pl.BlockSpec((step, features), lambda i, c: (i, 0))
    gain_block = pl.BlockSpec((2, features), lambda i, c: (0, 0))
    kinds = [(2, features // 2)] + [(4, width) for width in chunks]
    kinds = kinds + kinds
    return pl.pallas_call(
        functools.partial(pack_kernel, n_seq, chunks),
        grid_spec=pltpu.PrefetchScalarGridSpec(
            num_scalar_prefetch=1,
            grid=(rows // step,),
            in_specs=[row_block] * 6 + [gain_block],
            out_specs=[pl.BlockSpec((count, step, width), lambda i, c: (0, i, 0)) for count, width in kinds],
        ),
        out_shape=[jax.ShapeDtypeStruct((count, rows, width), LOW) for count, width in kinds],
        compiler_params=params(),
        cost_estimate=LIGHT,
    )(core, *arrays, gains)


def attend_kernel(n_queries, *refs):
    query_refs, keyed_refs, out_ref = refs[:n_queries], refs[n_queries:-1], refs[-1]

    def stack(which, some_refs, kinds):
        parts = [ref[at] for ref in some_refs for at in range(which, ref.shape[0], kinds)]
        return jnp.concatenate(parts, axis=0)

    query, query_dual = (stack(which, query_refs, 2) for which in range(2))
    key, key_dual, value, value_dual = (stack(which, keyed_refs, 4) for which in range(4))
    factor = query.shape[-1] ** (-0.5)
    last = (((1,), (1,)), ((), ()))
    scores = lax.dot_general(query, key, last, preferred_element_type=WIDE) * factor
    dual_scores = (
        lax.dot_general(
            jnp.concatenate([query_dual, query], axis=1),
            jnp.concatenate([key, key_dual], axis=1),
            last,
            preferred_element_type=WIDE,
        )
        * factor
    )
    raised = jnp.exp(scores - jnp.max(scores, axis=-1, keepdims=True))
    probs = raised * (1.0 / jnp.sum(raised, axis=-1, keepdims=True))
    spread = probs * (dual_scores - jnp.sum(probs * dual_scores, axis=-1, keepdims=True))
    probs_low = probs.astype(LOW)
    spread_low = spread.astype(LOW)
    out_ref[0] = jnp.dot(probs_low, value, preferred_element_type=WIDE).astype(LOW)
    out_ref[1] = (
        jnp.dot(probs_low, value_dual, preferred_element_type=WIDE)
        + jnp.dot(spread_low, value, preferred_element_type=WIDE)
    ).astype(LOW)


def attend(start, hdim, queries, keyed):
    rows = queries[0].shape[1]
    width = keyed[0].shape[2]
    first = start // hdim
    return pl.pallas_call(
        functools.partial(attend_kernel, len(queries)),
        grid=(width // hdim,),
        in_specs=[pl.BlockSpec((2, rows, hdim), lambda h: (0, 0, first + h))] * len(queries)
        + [pl.BlockSpec((array.shape[0], rows, hdim), lambda h: (0, 0, h)) for array in keyed],
        out_specs=pl.BlockSpec((2, len(queries) * rows, hdim), lambda h: (0, 0, h)),
        out_shape=jax.ShapeDtypeStruct((2, len(queries) * rows, width), LOW),
        compiler_params=params(),
        cost_estimate=LIGHT,
    )(*queries, *keyed)


def project_kernel(n_chunks, spans, flip_ref, *refs):
    sides = refs[:n_chunks], refs[n_chunks : 2 * n_chunks]
    weight_refs, out_refs, weight_ref = refs[2 * n_chunks : -6], refs[-6:-1], refs[-1]
    rows = out_refs[0].shape[0] // 2
    depth = weight_ref.shape[0] // 2
    at = 0
    for ref, (low, high) in zip(weight_refs, spans):
        block, inside = at // depth, at % depth
        first = pl.multiple_of((block ^ flip_ref[0]) * depth + inside, 16)
        weight_ref[pl.ds(first, high - low)] = ref[low:high]
        at += high - low
    weight = weight_ref[...]
    for side, parts in enumerate(sides):
        acts = jnp.concatenate([ref[...].reshape(4 * rows, ref.shape[-1]) for ref in parts], axis=1)
        total = jnp.dot(acts, weight, preferred_element_type=WIDE)
        for kind in range(2):
            first = 2 * kind * rows
            here = slice(kind * rows, (kind + 1) * rows)
            out_refs[side][here] = total[first : first + rows]
            low = total[first + rows : first + 2 * rows].astype(LOW)
            if side:
                out_refs[3 + kind][...] = low
            else:
                out_refs[2][here] = low


def project(flip, acts, pieces):
    mine, theirs = zip(*acts)
    weights = [weight for weight, _, _ in pieces]
    spans = [(low, high) for _, low, high in pieces]
    rows, n = mine[0].shape[1], weights[0].shape[1]
    depth = sum(high - low for low, high in spans)
    return pl.pallas_call(
        functools.partial(project_kernel, len(acts), spans),
        in_specs=[pl.BlockSpec(memory_space=pltpu.SMEM)] + vmem_specs(2 * len(acts) + len(weights)),
        out_specs=vmem_specs(5),
        out_shape=[jax.ShapeDtypeStruct((rows, n), WIDE)] * 2
        + [jax.ShapeDtypeStruct((rows, n), LOW)]
        + [jax.ShapeDtypeStruct((rows // 2, n), LOW)] * 2,
        scratch_shapes=[pltpu.VMEM((depth, n), LOW)],
        compiler_params=params(),
        cost_estimate=LIGHT,
    )(flip, *mine, *theirs, *weights)


def close_kernel(keep_ref, *refs):
    got_refs, out_ref = refs[:-1], refs[-1]
    first = 0
    for got_ref in got_refs:
        here = slice(first, first + got_ref.shape[0])
        out_ref[here] = (keep_ref[here] + got_ref[...].astype(WIDE)).astype(LOW)
        first = here.stop


def close(keep, *gots):
    return pl.pallas_call(
        close_kernel,
        in_specs=vmem_specs(1 + len(gots)),
        out_specs=vmem_specs(1)[0],
        out_shape=jax.ShapeDtypeStruct(keep.shape, LOW),
        compiler_params=params(),
        cost_estimate=LIGHT,
    )(keep, *gots)


def place_kernel(where_ref, mine_ref, other_ref, *refs):
    plain_ref, dual_ref = refs[-2:]
    rows = plain_ref.shape[0]

    @pl.when(pl.program_id(0) == 0)
    def _():
        plain_ref[...] = mine_ref[:rows]
        dual_ref[...] = mine_ref[rows:]

    @pl.when(pl.program_id(0) == 1)
    def _():
        plain_ref[...] = other_ref[:rows]
        dual_ref[...] = other_ref[rows:]


def place(outs, width, where, mine, other):
    rows, n = other.shape[0] // 2, other.shape[1]
    if n % 128:
        outs = outs or [jnp.zeros((rows, width), LOW)] * 2
        for side, piece in enumerate((mine, other)):
            parts = (piece[:rows], piece[rows:])
            outs = [lax.dynamic_update_slice(out, part, (0, where[side] * n)) for out, part in zip(outs, parts)]
        return outs
    full = pl.BlockSpec((2 * rows, n), lambda i, w: (0, 0))
    block = pl.BlockSpec((rows, n), lambda i, w: (0, w[i]))
    return pl.pallas_call(
        place_kernel,
        grid_spec=pltpu.PrefetchScalarGridSpec(
            num_scalar_prefetch=1,
            grid=(2,),
            in_specs=[full] * 2 + [pl.BlockSpec(memory_space=pl.ANY)] * len(outs),
            out_specs=[block] * 2,
        ),
        out_shape=[jax.ShapeDtypeStruct((rows, width), LOW)] * 2,
        input_output_aliases={3 + at: at for at in range(len(outs))},
        compiler_params=params(),
        cost_estimate=LIGHT,
    )(where, mine, other, *outs)


def body(
    n_dp,
    n_seq,
    queries,
    key_states,
    value_states,
    query_tangent,
    key_tangent,
    value_tangent,
    query_gain,
    key_gain,
    out_weight,
):
    dp = lax.axis_index("dp")
    seq = lax.axis_index("seq")
    n_ring = n_dp // 2
    groups = n_seq // 2
    features = queries.shape[1]
    hdim = features // HEADS
    group_heads = HEADS // n_seq
    few = group_heads * 2 // 5
    chunks = [group_heads * hdim] * (groups - 1) + [(group_heads - few) * hdim, few * hdim]
    starts = [sum(chunks[:at]) for at in range(len(chunks))]
    token = jnp.zeros((1,), jnp.int32)

    def far(array):
        return lax.ppermute(array, "seq", [(i, i ^ 2) for i in range(n_seq)])

    def near(array):
        return lax.ppermute(array, "seq", [(i, i ^ 1) for i in range(n_seq)])

    def across(array):
        return lax.ppermute(array, "dp", [(i, i ^ 1) for i in range(n_dp)])

    def onward(array):
        return lax.ppermute(array, "dp", [(i, (i + 2) % n_dp) for i in range(n_dp)])

    def wait(array):
        nonlocal token
        array, token = lax.optimization_barrier((array, token))
        return array

    def after(array):
        return lax.optimization_barrier((array, token))[0]

    def turn(ring, step):
        ring[step] = wait(ring[step])
        if step + 1 < n_ring:
            ring.append(onward(ring[step]))

    depth = out_weight.shape[0]
    cut = depth * 3 // 5 // 16 * 16
    upper, lower = [out_weight[:cut]], [out_weight[cut:]]
    lower.append(onward(lower[0]))
    upper.append(onward(upper[0]))
    beside = [wait(far(upper[0]))]
    beside.append(onward(beside[0]))
    turn(lower, 1)

    core = jnp.stack([seq % 2])
    arrays = (queries, key_states, value_states, query_tangent, key_tangent, value_tangent)
    packs = [wait(array) for array in pack(core, n_seq, chunks, arrays, jnp.stack([query_gain, key_gain]))]
    query_own, *keyed_own = packs[: 1 + len(chunks)]
    query_other, *keyed_other = packs[1 + len(chunks) :]
    there = wait(near(keyed_other[0]))
    keyed = [[keyed_own[0], there, far(keyed_own[0]), far(there)]]
    for own, other in zip(keyed_own[1:], keyed_other[1:]):
        there = wait(near(other))
        keyed.append([own, there, far(jnp.concatenate([own, there]))])
    queries_both = [query_own, wait(near(query_other))]
    turn(lower, 2)

    acts, swapped = [], []

    def attention(chunk):
        keyed[chunk][-1] = wait(keyed[chunk][-1])
        acts.append(wait(attend(starts[chunk], hdim, queries_both, keyed[chunk])))
        swapped.append(across(acts[-1]))

    turn(upper, 1)
    keyed[0][2] = wait(keyed[0][2])
    turn(beside, 1)
    attention(0)
    for step in range(3, n_ring):
        turn(lower, step)
    later = [wait(jnp.concatenate(lower[step : step + 2])) for step in range(2, n_ring, 2)]
    turn(upper, 2)
    rest = [far(after(lower[0]))]
    attention(1)
    swapped[0] = wait(swapped[0])
    attention(2)
    swapped[1] = wait(swapped[1])
    turn(beside, 2)
    rest += [far(after(piece)) for piece in lower[1:2] + later]
    rest[0] = wait(rest[0])
    swapped[2] = wait(swapped[2])
    acts = list(zip(acts, swapped))
    flip = jnp.stack([seq // 2])

    keeps, sends, mine_got, mine, other = [], [], [], [], []

    def columns(step):
        own = [(upper[step], 0, cut), (lower[step], 0, depth - cut)] if step else [(out_weight, 0, depth)]
        start = step % 2 * (depth - cut) if step > 1 else 0
        got = rest[step] if step < 2 else rest[1 + step // 2]
        theirs = [(beside[step], 0, cut), (got, start, start + depth - cut)]
        keep_mine, keep_other, *low = project(after(flip), acts, own + theirs)
        keeps.append((keep_mine, keep_other))
        sends.append([near(wait(array)) for array in low[1:]])
        mine_got.append([wait(array) for array in low[:1]])

    def send(step):
        if step > 2:
            other[step - 1] = wait(other[step - 1])
        other.append(across(wait(close(keeps[step][1], *[wait(array) for array in sends[step]]))))
        mine_got[step] = [near(after(array)) for array in mine_got[step]]
        if step and not step > 2:
            other[step - 1] = wait(other[step - 1])

    def stay(step):
        mine.append(wait(close(keeps[step][0], *[wait(array) for array in mine_got[step]])))

    outs = []

    def put(step):
        pair = (dp // 2 - step) % n_ring
        where = jnp.stack([2 * pair + dp % 2, 2 * pair + 1 - dp % 2]).astype(jnp.int32) + token
        return place(outs, n_dp * out_weight.shape[1], where, mine[step], other[step])

    columns(0)
    for step in range(3, n_ring):
        turn(upper, step)
    rest[1] = wait(rest[1])
    send(0)
    columns(1)
    send(1)
    for step in range(2, n_ring, 2):
        rest[1 + step // 2] = wait(rest[1 + step // 2])
        if step > 2:
            turn(beside, step)
        turn(beside, step + 1)
        columns(step)
        send(step)
        stay(step - 2)
        stay(step - 1)
        columns(step + 1)
        send(step + 1)
    stay(n_ring - 2)
    stay(n_ring - 1)
    for step in range(n_ring - 1):
        outs = [wait(out) for out in put(step)]
    other[-1] = wait(other[-1])
    return tuple(put(n_ring - 1))


def solution(mesh):
    rows = P(("dp", "seq"), None)
    return jax.shard_map(
        functools.partial(body, mesh.shape["dp"], mesh.shape["seq"]),
        mesh=mesh,
        in_specs=(rows,) * 6 + (P(), P(), P("seq", "dp")),
        out_specs=(rows, rows),
        check_vma=False,
    )
```

```python
import functools

import jax
import jax.numpy as jnp
from jax import lax
from jax.experimental import pallas as pl
from jax.experimental.pallas import tpu as pltpu
from jax.sharding import PartitionSpec as P

HEADS = 20
EPS = 1e-06
VMEM_BYTES = 10 * 1024 * 1024
ROW_STEP = 32

LOW = jnp.bfloat16
WIDE = jnp.float32
LIGHT = pl.CostEstimate(flops=1, transcendentals=0, bytes_accessed=1)


def params():
    return pltpu.CompilerParams(vmem_limit_bytes=VMEM_BYTES)


def vmem_specs(count):
    return [pl.BlockSpec(memory_space=pltpu.VMEM)] * count


def pack_kernel(n_seq, chunks, core_ref, *refs):
    query_ref, key_ref, value_ref, dquery_ref, dkey_ref, dvalue_ref, gains_ref = refs[:7]
    out_refs = refs[7:]
    n_chunks = len(chunks)
    group = query_ref.shape[-1] // n_seq

    def statistics(primal_ref, tangent_ref):
        primal = primal_ref[...].astype(WIDE)
        tangent = tangent_ref[...].astype(WIDE)
        inverse = lax.rsqrt(jnp.mean(primal * primal, axis=-1, keepdims=True) + EPS)
        across = jnp.mean(primal * tangent, axis=-1, keepdims=True)
        return inverse, inverse * inverse * inverse * across

    query_stats = statistics(query_ref, dquery_ref)
    key_stats = statistics(key_ref, dkey_ref)

    def normed(primal_ref, tangent_ref, which, stats, lanes):
        primal = primal_ref[:, lanes].astype(WIDE)
        tangent = tangent_ref[:, lanes].astype(WIDE)
        gain = gains_ref[which : which + 1, lanes]
        inverse, slope = stats
        return (primal * inverse * gain).astype(LOW), (gain * (tangent * inverse - primal * slope)).astype(LOW)

    for side in range(2):
        core = core_ref[0] if side == 0 else 1 - core_ref[0]
        queries_ref, *keyed_refs = out_refs[side * (1 + n_chunks) : (side + 1) * (1 + n_chunks)]
        for at in range(n_seq // 2):
            lanes = pl.ds(pl.multiple_of((2 * at + core) * group, 128), group)
            here = slice(at * group, (at + 1) * group)
            plain, dual = normed(query_ref, dquery_ref, 0, query_stats, lanes)
            queries_ref[0, :, here] = plain
            queries_ref[1, :, here] = dual
            four = normed(key_ref, dkey_ref, 1, key_stats, lanes)
            four += (value_ref[:, lanes], dvalue_ref[:, lanes])
            start = 0
            for keyed_ref, width in zip(keyed_refs, chunks):
                low, high = max(start, here.start), min(start + width, here.stop)
                if low < high:
                    for which, part in enumerate(four):
                        keyed_ref[which, :, low - start : high - start] = part[:, low - here.start : high - here.start]
                start += width


def pack(core, n_seq, chunks, arrays, gains):
    rows, features = arrays[0].shape
    step = min(rows, ROW_STEP)
    row_block = pl.BlockSpec((step, features), lambda i, c: (i, 0))
    gain_block = pl.BlockSpec((2, features), lambda i, c: (0, 0))
    kinds = [(2, features // 2)] + [(4, width) for width in chunks]
    kinds = kinds + kinds
    return pl.pallas_call(
        functools.partial(pack_kernel, n_seq, chunks),
        grid_spec=pltpu.PrefetchScalarGridSpec(
            num_scalar_prefetch=1,
            grid=(rows // step,),
            in_specs=[row_block] * 6 + [gain_block],
            out_specs=[pl.BlockSpec((count, step, width), lambda i, c: (0, i, 0)) for count, width in kinds],
        ),
        out_shape=[jax.ShapeDtypeStruct((count, rows, width), LOW) for count, width in kinds],
        compiler_params=params(),
        cost_estimate=LIGHT,
    )(core, *arrays, gains)


def attend_kernel(n_queries, *refs):
    query_refs, keyed_refs, out_ref = refs[:n_queries], refs[n_queries:-1], refs[-1]

    def stack(which, some_refs, kinds):
        parts = [ref[at] for ref in some_refs for at in range(which, ref.shape[0], kinds)]
        return jnp.concatenate(parts, axis=0)

    query, query_dual = (stack(which, query_refs, 2) for which in range(2))
    key, key_dual, value, value_dual = (stack(which, keyed_refs, 4) for which in range(4))
    factor = query.shape[-1] ** (-0.5)
    last = (((1,), (1,)), ((), ()))
    scores = lax.dot_general(query, key, last, preferred_element_type=WIDE) * factor
    dual_scores = (
        lax.dot_general(
            jnp.concatenate([query_dual, query], axis=1),
            jnp.concatenate([key, key_dual], axis=1),
            last,
            preferred_element_type=WIDE,
        )
        * factor
    )
    raised = jnp.exp(scores - jnp.max(scores, axis=-1, keepdims=True))
    probs = raised * (1.0 / jnp.sum(raised, axis=-1, keepdims=True))
    spread = probs * (dual_scores - jnp.sum(probs * dual_scores, axis=-1, keepdims=True))
    probs_low = probs.astype(LOW)
    spread_low = spread.astype(LOW)
    out_ref[0] = jnp.dot(probs_low, value, preferred_element_type=WIDE).astype(LOW)
    out_ref[1] = (
        jnp.dot(probs_low, value_dual, preferred_element_type=WIDE)
        + jnp.dot(spread_low, value, preferred_element_type=WIDE)
    ).astype(LOW)


def attend(start, hdim, queries, keyed):
    rows = queries[0].shape[1]
    width = keyed[0].shape[2]
    first = start // hdim
    return pl.pallas_call(
        functools.partial(attend_kernel, len(queries)),
        grid=(width // hdim,),
        in_specs=[pl.BlockSpec((2, rows, hdim), lambda h: (0, 0, first + h))] * len(queries)
        + [pl.BlockSpec((array.shape[0], rows, hdim), lambda h: (0, 0, h)) for array in keyed],
        out_specs=pl.BlockSpec((2, len(queries) * rows, hdim), lambda h: (0, 0, h)),
        out_shape=jax.ShapeDtypeStruct((2, len(queries) * rows, width), LOW),
        compiler_params=params(),
        cost_estimate=LIGHT,
    )(*queries, *keyed)


def project_kernel(n_chunks, spans, flip_ref, *refs):
    sides = refs[:n_chunks], refs[n_chunks : 2 * n_chunks]
    weight_refs, out_refs, weight_ref = refs[2 * n_chunks : -6], refs[-6:-1], refs[-1]
    rows = out_refs[0].shape[0] // 2
    depth = weight_ref.shape[0] // 2
    at = 0
    for ref, (low, high) in zip(weight_refs, spans):
        block, inside = at // depth, at % depth
        first = pl.multiple_of((block ^ flip_ref[0]) * depth + inside, 16)
        weight_ref[pl.ds(first, high - low)] = ref[low:high]
        at += high - low
    weight = weight_ref[...]
    for side, parts in enumerate(sides):
        acts = jnp.concatenate([ref[...].reshape(4 * rows, ref.shape[-1]) for ref in parts], axis=1)
        total = jnp.dot(acts, weight, preferred_element_type=WIDE)
        for kind in range(2):
            first = 2 * kind * rows
            here = slice(kind * rows, (kind + 1) * rows)
            out_refs[side][here] = total[first : first + rows]
            low = total[first + rows : first + 2 * rows].astype(LOW)
            if side:
                out_refs[3 + kind][...] = low
            else:
                out_refs[2][here] = low


def project(flip, acts, pieces):
    mine, theirs = zip(*acts)
    weights = [weight for weight, _, _ in pieces]
    spans = [(low, high) for _, low, high in pieces]
    rows, n = mine[0].shape[1], weights[0].shape[1]
    depth = sum(high - low for low, high in spans)
    return pl.pallas_call(
        functools.partial(project_kernel, len(acts), spans),
        in_specs=[pl.BlockSpec(memory_space=pltpu.SMEM)] + vmem_specs(2 * len(acts) + len(weights)),
        out_specs=vmem_specs(5),
        out_shape=[jax.ShapeDtypeStruct((rows, n), WIDE)] * 2
        + [jax.ShapeDtypeStruct((rows, n), LOW)]
        + [jax.ShapeDtypeStruct((rows // 2, n), LOW)] * 2,
        scratch_shapes=[pltpu.VMEM((depth, n), LOW)],
        compiler_params=params(),
        cost_estimate=LIGHT,
    )(flip, *mine, *theirs, *weights)


def close_kernel(keep_ref, *refs):
    got_refs, out_ref = refs[:-1], refs[-1]
    first = 0
    for got_ref in got_refs:
        here = slice(first, first + got_ref.shape[0])
        out_ref[here] = (keep_ref[here] + got_ref[...].astype(WIDE)).astype(LOW)
        first = here.stop


def close(keep, *gots):
    return pl.pallas_call(
        close_kernel,
        in_specs=vmem_specs(1 + len(gots)),
        out_specs=vmem_specs(1)[0],
        out_shape=jax.ShapeDtypeStruct(keep.shape, LOW),
        compiler_params=params(),
        cost_estimate=LIGHT,
    )(keep, *gots)


def place_kernel(where_ref, mine_ref, other_ref, *refs):
    plain_ref, dual_ref = refs[-2:]
    rows = plain_ref.shape[0]

    @pl.when(pl.program_id(0) == 0)
    def _():
        plain_ref[...] = mine_ref[:rows]
        dual_ref[...] = mine_ref[rows:]

    @pl.when(pl.program_id(0) == 1)
    def _():
        plain_ref[...] = other_ref[:rows]
        dual_ref[...] = other_ref[rows:]


def place(outs, width, where, mine, other):
    rows, n = other.shape[0] // 2, other.shape[1]
    if n % 128:
        outs = outs or [jnp.zeros((rows, width), LOW)] * 2
        for side, piece in enumerate((mine, other)):
            parts = (piece[:rows], piece[rows:])
            outs = [lax.dynamic_update_slice(out, part, (0, where[side] * n)) for out, part in zip(outs, parts)]
        return outs
    full = pl.BlockSpec((2 * rows, n), lambda i, w: (0, 0))
    block = pl.BlockSpec((rows, n), lambda i, w: (0, w[i]))
    return pl.pallas_call(
        place_kernel,
        grid_spec=pltpu.PrefetchScalarGridSpec(
            num_scalar_prefetch=1,
            grid=(2,),
            in_specs=[full] * 2 + [pl.BlockSpec(memory_space=pl.ANY)] * len(outs),
            out_specs=[block] * 2,
        ),
        out_shape=[jax.ShapeDtypeStruct((rows, width), LOW)] * 2,
        input_output_aliases={3 + at: at for at in range(len(outs))},
        compiler_params=params(),
        cost_estimate=LIGHT,
    )(where, mine, other, *outs)


def body(
    n_dp,
    n_seq,
    queries,
    key_states,
    value_states,
    query_tangent,
    key_tangent,
    value_tangent,
    query_gain,
    key_gain,
    out_weight,
):
    dp = lax.axis_index("dp")
    seq = lax.axis_index("seq")
    n_ring = n_dp // 2
    groups = n_seq // 2
    features = queries.shape[1]
    hdim = features // HEADS
    group_heads = HEADS // n_seq
    few = group_heads * 2 // 5
    chunks = [group_heads * hdim] * (groups - 1) + [(group_heads - few) * hdim, few * hdim]
    starts = [sum(chunks[:at]) for at in range(len(chunks))]
    token = jnp.zeros((1,), jnp.int32)

    def far(array):
        return lax.ppermute(array, "seq", [(i, i ^ 2) for i in range(n_seq)])

    def near(array):
        return lax.ppermute(array, "seq", [(i, i ^ 1) for i in range(n_seq)])

    def across(array):
        return lax.ppermute(array, "dp", [(i, i ^ 1) for i in range(n_dp)])

    def onward(array):
        return lax.ppermute(array, "dp", [(i, (i + 2) % n_dp) for i in range(n_dp)])

    def wait(array):
        nonlocal token
        array, token = lax.optimization_barrier((array, token))
        return array

    def after(array):
        return lax.optimization_barrier((array, token))[0]

    def turn(ring, step):
        ring[step] = wait(ring[step])
        if step + 1 < n_ring:
            ring.append(onward(ring[step]))

    depth = out_weight.shape[0]
    cut = depth * 3 // 5 // 16 * 16
    upper, lower = [out_weight[:cut]], [out_weight[cut:]]
    lower.append(onward(lower[0]))
    upper.append(onward(upper[0]))
    beside = [wait(far(upper[0]))]
    beside.append(onward(beside[0]))
    turn(lower, 1)

    core = jnp.stack([seq % 2])
    arrays = (queries, key_states, value_states, query_tangent, key_tangent, value_tangent)
    packs = [wait(array) for array in pack(core, n_seq, chunks, arrays, jnp.stack([query_gain, key_gain]))]
    query_own, *keyed_own = packs[: 1 + len(chunks)]
    query_other, *keyed_other = packs[1 + len(chunks) :]
    there = wait(near(keyed_other[0]))
    keyed = [[keyed_own[0], there, far(keyed_own[0]), far(there)]]
    for own, other in zip(keyed_own[1:], keyed_other[1:]):
        there = wait(near(other))
        keyed.append([own, there, far(jnp.concatenate([own, there]))])
    queries_both = [query_own, wait(near(query_other))]
    turn(lower, 2)

    acts, swapped = [], []

    def attention(chunk):
        keyed[chunk][-1] = wait(keyed[chunk][-1])
        acts.append(wait(attend(starts[chunk], hdim, queries_both, keyed[chunk])))
        swapped.append(across(acts[-1]))

    turn(upper, 1)
    keyed[0][2] = wait(keyed[0][2])
    turn(beside, 1)
    attention(0)
    for step in range(3, n_ring):
        turn(lower, step)
    later = [wait(jnp.concatenate(lower[step : step + 2])) for step in range(2, n_ring, 2)]
    turn(upper, 2)
    rest = [far(after(lower[0]))]
    attention(1)
    swapped[0] = wait(swapped[0])
    attention(2)
    swapped[1] = wait(swapped[1])
    turn(beside, 2)
    rest += [far(after(piece)) for piece in lower[1:2] + later]
    rest[0] = wait(rest[0])
    swapped[2] = wait(swapped[2])
    acts = list(zip(acts, swapped))
    turned = jnp.stack([seq // 2])

    keeps, sends, mine_got, mine, other = [], [], [], [], []

    def columns(step, flip=None):
        own = [(upper[step], 0, cut), (lower[step], 0, depth - cut)] if step else [(out_weight, 0, depth)]
        start = step % 2 * (depth - cut) if step > 1 else 0
        got = rest[step] if step < 2 else rest[1 + step // 2]
        theirs = [(beside[step], 0, cut), (got, start, start + depth - cut)]
        keep_mine, keep_other, *low = project(after(turned) if flip is None else flip, acts, own + theirs)
        keeps.append((keep_mine, keep_other))
        sends.append([near(wait(array)) for array in low[1:]])
        mine_got.append([wait(array) for array in low[:1]])

    def send(step):
        if step > 2:
            other[step - 1] = wait(other[step - 1])
        other.append(across(wait(close(keeps[step][1], *[wait(array) for array in sends[step]]))))
        mine_got[step] = [near(after(array)) for array in mine_got[step]]
        if step and not step > 2:
            other[step - 1] = wait(other[step - 1])

    def stay(step):
        mine.append(wait(close(keeps[step][0], *[wait(array) for array in mine_got[step]])))

    outs = []

    def put(step):
        pair = (dp // 2 - step) % n_ring
        where = jnp.stack([2 * pair + dp % 2, 2 * pair + 1 - dp % 2]).astype(jnp.int32) + token
        return place(outs, n_dp * out_weight.shape[1], where, mine[step], other[step])

    columns(0)
    for step in range(3, n_ring):
        turn(upper, step)
    rest[1] = wait(rest[1])
    send(0)
    columns(1)
    send(1)
    for step in range(2, n_ring, 2):
        rest[1 + step // 2] = wait(rest[1 + step // 2])
        if step > 2:
            turn(beside, step)
        flip = after(turned)
        turn(beside, step + 1)
        columns(step, flip)
        send(step)
        stay(step - 2)
        stay(step - 1)
        columns(step + 1)
        send(step + 1)
    stay(n_ring - 2)
    stay(n_ring - 1)
    for step in range(n_ring - 1):
        outs = [wait(out) for out in put(step)]
    other[-1] = wait(other[-1])
    return tuple(put(n_ring - 1))


def solution(mesh):
    rows = P(("dp", "seq"), None)
    return jax.shard_map(
        functools.partial(body, mesh.shape["dp"], mesh.shape["seq"]),
        mesh=mesh,
        in_specs=(rows,) * 6 + (P(), P(), P("seq", "dp")),
        out_specs=(rows, rows),
        check_vma=False,
    )
```

```python
import functools

import jax
import jax.numpy as jnp
from jax import lax
from jax.experimental import pallas as pl
from jax.experimental.pallas import tpu as pltpu
from jax.sharding import PartitionSpec as P

HEADS = 20
EPS = 1e-06
VMEM_BYTES = 10 * 1024 * 1024
ROW_STEP = 32

LOW = jnp.bfloat16
WIDE = jnp.float32
LIGHT = pl.CostEstimate(flops=1, transcendentals=0, bytes_accessed=1)


def params():
    return pltpu.CompilerParams(vmem_limit_bytes=VMEM_BYTES)


def vmem_specs(count):
    return [pl.BlockSpec(memory_space=pltpu.VMEM)] * count


def pack_kernel(n_seq, chunks, core_ref, *refs):
    query_ref, key_ref, value_ref, dquery_ref, dkey_ref, dvalue_ref, gains_ref = refs[:7]
    out_refs = refs[7:]
    n_chunks = len(chunks)
    group = query_ref.shape[-1] // n_seq

    def statistics(primal_ref, tangent_ref):
        primal = primal_ref[...].astype(WIDE)
        tangent = tangent_ref[...].astype(WIDE)
        inverse = lax.rsqrt(jnp.mean(primal * primal, axis=-1, keepdims=True) + EPS)
        across = jnp.mean(primal * tangent, axis=-1, keepdims=True)
        return inverse, inverse * inverse * inverse * across

    query_stats = statistics(query_ref, dquery_ref)
    key_stats = statistics(key_ref, dkey_ref)

    def normed(primal_ref, tangent_ref, which, stats, lanes):
        primal = primal_ref[:, lanes].astype(WIDE)
        tangent = tangent_ref[:, lanes].astype(WIDE)
        gain = gains_ref[which : which + 1, lanes]
        inverse, slope = stats
        return (primal * inverse * gain).astype(LOW), (gain * (tangent * inverse - primal * slope)).astype(LOW)

    for side in range(2):
        core = core_ref[0] if side == 0 else 1 - core_ref[0]
        queries_ref, *keyed_refs = out_refs[side * (1 + n_chunks) : (side + 1) * (1 + n_chunks)]
        for at in range(n_seq // 2):
            lanes = pl.ds(pl.multiple_of((2 * at + core) * group, 128), group)
            here = slice(at * group, (at + 1) * group)
            plain, dual = normed(query_ref, dquery_ref, 0, query_stats, lanes)
            queries_ref[0, :, here] = plain
            queries_ref[1, :, here] = dual
            four = normed(key_ref, dkey_ref, 1, key_stats, lanes)
            four += (value_ref[:, lanes], dvalue_ref[:, lanes])
            start = 0
            for keyed_ref, width in zip(keyed_refs, chunks):
                low, high = max(start, here.start), min(start + width, here.stop)
                if low < high:
                    for which, part in enumerate(four):
                        keyed_ref[which, :, low - start : high - start] = part[:, low - here.start : high - here.start]
                start += width


def pack(core, n_seq, chunks, arrays, gains):
    rows, features = arrays[0].shape
    step = min(rows, ROW_STEP)
    row_block = pl.BlockSpec((step, features), lambda i, c: (i, 0))
    gain_block = pl.BlockSpec((2, features), lambda i, c: (0, 0))
    kinds = [(2, features // 2)] + [(4, width) for width in chunks]
    kinds = kinds + kinds
    return pl.pallas_call(
        functools.partial(pack_kernel, n_seq, chunks),
        grid_spec=pltpu.PrefetchScalarGridSpec(
            num_scalar_prefetch=1,
            grid=(rows // step,),
            in_specs=[row_block] * 6 + [gain_block],
            out_specs=[pl.BlockSpec((count, step, width), lambda i, c: (0, i, 0)) for count, width in kinds],
        ),
        out_shape=[jax.ShapeDtypeStruct((count, rows, width), LOW) for count, width in kinds],
        compiler_params=params(),
        cost_estimate=LIGHT,
    )(core, *arrays, gains)


def attend_kernel(n_queries, *refs):
    query_refs, keyed_refs, out_ref = refs[:n_queries], refs[n_queries:-1], refs[-1]

    def stack(which, some_refs, kinds):
        parts = [ref[at] for ref in some_refs for at in range(which, ref.shape[0], kinds)]
        return jnp.concatenate(parts, axis=0)

    query, query_dual = (stack(which, query_refs, 2) for which in range(2))
    key, key_dual, value, value_dual = (stack(which, keyed_refs, 4) for which in range(4))
    factor = query.shape[-1] ** (-0.5)
    last = (((1,), (1,)), ((), ()))
    scores = lax.dot_general(query, key, last, preferred_element_type=WIDE) * factor
    dual_scores = (
        lax.dot_general(
            jnp.concatenate([query_dual, query], axis=1),
            jnp.concatenate([key, key_dual], axis=1),
            last,
            preferred_element_type=WIDE,
        )
        * factor
    )
    raised = jnp.exp(scores - jnp.max(scores, axis=-1, keepdims=True))
    probs = raised * (1.0 / jnp.sum(raised, axis=-1, keepdims=True))
    spread = probs * (dual_scores - jnp.sum(probs * dual_scores, axis=-1, keepdims=True))
    probs_low = probs.astype(LOW)
    spread_low = spread.astype(LOW)
    out_ref[0] = jnp.dot(probs_low, value, preferred_element_type=WIDE).astype(LOW)
    out_ref[1] = (
        jnp.dot(probs_low, value_dual, preferred_element_type=WIDE)
        + jnp.dot(spread_low, value, preferred_element_type=WIDE)
    ).astype(LOW)


def attend(start, hdim, queries, keyed):
    rows = queries[0].shape[1]
    width = keyed[0].shape[2]
    first = start // hdim
    return pl.pallas_call(
        functools.partial(attend_kernel, len(queries)),
        grid=(width // hdim,),
        in_specs=[pl.BlockSpec((2, rows, hdim), lambda h: (0, 0, first + h))] * len(queries)
        + [pl.BlockSpec((array.shape[0], rows, hdim), lambda h: (0, 0, h)) for array in keyed],
        out_specs=pl.BlockSpec((2, len(queries) * rows, hdim), lambda h: (0, 0, h)),
        out_shape=jax.ShapeDtypeStruct((2, len(queries) * rows, width), LOW),
        compiler_params=params(),
        cost_estimate=LIGHT,
    )(*queries, *keyed)


def project_kernel(n_chunks, spans, flip_ref, *refs):
    sides = refs[:n_chunks], refs[n_chunks : 2 * n_chunks]
    weight_refs, out_refs, weight_ref = refs[2 * n_chunks : -6], refs[-6:-1], refs[-1]
    rows = out_refs[0].shape[0] // 2
    depth = weight_ref.shape[0] // 2
    at = 0
    for ref, (low, high) in zip(weight_refs, spans):
        block, inside = at // depth, at % depth
        first = pl.multiple_of((block ^ flip_ref[0]) * depth + inside, 16)
        weight_ref[pl.ds(first, high - low)] = ref[low:high]
        at += high - low
    weight = weight_ref[...]
    for side, parts in enumerate(sides):
        acts = jnp.concatenate([ref[...].reshape(4 * rows, ref.shape[-1]) for ref in parts], axis=1)
        total = jnp.dot(acts, weight, preferred_element_type=WIDE)
        for kind in range(2):
            first = 2 * kind * rows
            here = slice(kind * rows, (kind + 1) * rows)
            out_refs[side][here] = total[first : first + rows]
            low = total[first + rows : first + 2 * rows].astype(LOW)
            if side:
                out_refs[3 + kind][...] = low
            else:
                out_refs[2][here] = low


def project(flip, acts, pieces):
    mine, theirs = zip(*acts)
    weights = [weight for weight, _, _ in pieces]
    spans = [(low, high) for _, low, high in pieces]
    rows, n = mine[0].shape[1], weights[0].shape[1]
    depth = sum(high - low for low, high in spans)
    return pl.pallas_call(
        functools.partial(project_kernel, len(acts), spans),
        in_specs=[pl.BlockSpec(memory_space=pltpu.SMEM)] + vmem_specs(2 * len(acts) + len(weights)),
        out_specs=vmem_specs(5),
        out_shape=[jax.ShapeDtypeStruct((rows, n), WIDE)] * 2
        + [jax.ShapeDtypeStruct((rows, n), LOW)]
        + [jax.ShapeDtypeStruct((rows // 2, n), LOW)] * 2,
        scratch_shapes=[pltpu.VMEM((depth, n), LOW)],
        compiler_params=params(),
        cost_estimate=LIGHT,
    )(flip, *mine, *theirs, *weights)


def close_kernel(keep_ref, *refs):
    got_refs, out_ref = refs[:-1], refs[-1]
    first = 0
    for got_ref in got_refs:
        here = slice(first, first + got_ref.shape[0])
        out_ref[here] = (keep_ref[here] + got_ref[...].astype(WIDE)).astype(LOW)
        first = here.stop


def close(keep, *gots):
    return pl.pallas_call(
        close_kernel,
        in_specs=vmem_specs(1 + len(gots)),
        out_specs=vmem_specs(1)[0],
        out_shape=jax.ShapeDtypeStruct(keep.shape, LOW),
        compiler_params=params(),
        cost_estimate=LIGHT,
    )(keep, *gots)


def place_kernel(where_ref, mine_ref, other_ref, *refs):
    plain_ref, dual_ref = refs[-2:]
    rows = plain_ref.shape[0]

    @pl.when(pl.program_id(0) == 0)
    def _():
        plain_ref[...] = mine_ref[:rows]
        dual_ref[...] = mine_ref[rows:]

    @pl.when(pl.program_id(0) == 1)
    def _():
        plain_ref[...] = other_ref[:rows]
        dual_ref[...] = other_ref[rows:]


def place(outs, width, where, mine, other):
    rows, n = other.shape[0] // 2, other.shape[1]
    if n % 128:
        outs = outs or [jnp.zeros((rows, width), LOW)] * 2
        for side, piece in enumerate((mine, other)):
            parts = (piece[:rows], piece[rows:])
            outs = [lax.dynamic_update_slice(out, part, (0, where[side] * n)) for out, part in zip(outs, parts)]
        return outs
    full = pl.BlockSpec((2 * rows, n), lambda i, w: (0, 0))
    block = pl.BlockSpec((rows, n), lambda i, w: (0, w[i]))
    return pl.pallas_call(
        place_kernel,
        grid_spec=pltpu.PrefetchScalarGridSpec(
            num_scalar_prefetch=1,
            grid=(2,),
            in_specs=[full] * 2 + [pl.BlockSpec(memory_space=pl.ANY)] * len(outs),
            out_specs=[block] * 2,
        ),
        out_shape=[jax.ShapeDtypeStruct((rows, width), LOW)] * 2,
        input_output_aliases={3 + at: at for at in range(len(outs))},
        compiler_params=params(),
        cost_estimate=LIGHT,
    )(where, mine, other, *outs)


def body(
    n_dp,
    n_seq,
    queries,
    key_states,
    value_states,
    query_tangent,
    key_tangent,
    value_tangent,
    query_gain,
    key_gain,
    out_weight,
):
    dp = lax.axis_index("dp")
    seq = lax.axis_index("seq")
    n_ring = n_dp // 2
    groups = n_seq // 2
    features = queries.shape[1]
    hdim = features // HEADS
    group_heads = HEADS // n_seq
    few = group_heads * 2 // 5
    chunks = [group_heads * hdim] * (groups - 1) + [(group_heads - few) * hdim, few * hdim]
    starts = [sum(chunks[:at]) for at in range(len(chunks))]
    token = jnp.zeros((1,), jnp.int32)

    def far(array):
        return lax.ppermute(array, "seq", [(i, i ^ 2) for i in range(n_seq)])

    def near(array):
        return lax.ppermute(array, "seq", [(i, i ^ 1) for i in range(n_seq)])

    def across(array):
        return lax.ppermute(array, "dp", [(i, i ^ 1) for i in range(n_dp)])

    def onward(array):
        return lax.ppermute(array, "dp", [(i, (i + 2) % n_dp) for i in range(n_dp)])

    def wait(array):
        nonlocal token
        array, token = lax.optimization_barrier((array, token))
        return array

    def after(array):
        return lax.optimization_barrier((array, token))[0]

    def turn(ring, step):
        ring[step] = wait(ring[step])
        if step + 1 < n_ring:
            ring.append(onward(ring[step]))

    depth = out_weight.shape[0]
    cut = depth * 3 // 5 // 16 * 16
    upper, lower = [out_weight[:cut]], [out_weight[cut:]]
    lower.append(onward(lower[0]))
    upper.append(onward(upper[0]))
    beside = [wait(far(upper[0]))]
    beside.append(onward(beside[0]))
    turn(lower, 1)

    core = jnp.stack([seq % 2])
    arrays = (queries, key_states, value_states, query_tangent, key_tangent, value_tangent)
    packs = [wait(array) for array in pack(core, n_seq, chunks, arrays, jnp.stack([query_gain, key_gain]))]
    query_own, *keyed_own = packs[: 1 + len(chunks)]
    query_other, *keyed_other = packs[1 + len(chunks) :]
    there = wait(near(keyed_other[0]))
    keyed = [[keyed_own[0], there, far(keyed_own[0]), far(there)]]
    for own, other in zip(keyed_own[1:], keyed_other[1:]):
        there = wait(near(other))
        keyed.append([own, there, far(jnp.concatenate([own, there]))])
    queries_both = [query_own, wait(near(query_other))]
    turn(lower, 2)

    acts, swapped = [], []

    def attention(chunk):
        keyed[chunk][-1] = wait(keyed[chunk][-1])
        acts.append(wait(attend(starts[chunk], hdim, queries_both, keyed[chunk])))
        swapped.append(across(acts[-1]))

    turn(upper, 1)
    keyed[0][2] = wait(keyed[0][2])
    turn(beside, 1)
    attention(0)
    for step in range(3, n_ring):
        turn(lower, step)
    later = [wait(jnp.concatenate(lower[step : step + 2])) for step in range(2, n_ring, 2)]
    turn(upper, 2)
    rest = [far(after(lower[0]))]
    attention(1)
    swapped[0] = wait(swapped[0])
    attention(2)
    swapped[1] = wait(swapped[1])
    turn(beside, 2)
    rest += [far(after(piece)) for piece in lower[1:2] + later]
    rest[0] = wait(rest[0])
    swapped[2] = wait(swapped[2])
    acts = list(zip(acts, swapped))
    turned = jnp.stack([seq // 2])

    keeps, sends, mine_got, mine, other = [], [], [], [], []

    def columns(step, flip=None):
        own = [(upper[step], 0, cut), (lower[step], 0, depth - cut)] if step else [(out_weight, 0, depth)]
        start = step % 2 * (depth - cut) if step > 1 else 0
        got = rest[step] if step < 2 else rest[1 + step // 2]
        theirs = [(beside[step], 0, cut), (got, start, start + depth - cut)]
        keep_mine, keep_other, *low = project(after(turned) if flip is None else flip, acts, own + theirs)
        keeps.append((keep_mine, keep_other))
        sends.append([near(wait(array)) for array in low[1:]])
        mine_got.append([wait(array) for array in low[:1]])

    def send(step):
        closed = wait(close(keeps[step][1], *[wait(array) for array in sends[step]]))
        if step > 2:
            other[step - 1] = wait(other[step - 1])
        other.append(across(after(closed)))
        mine_got[step] = [near(after(array)) for array in mine_got[step]]
        if step and not step > 2:
            other[step - 1] = wait(other[step - 1])

    def stay(step):
        mine.append(wait(close(keeps[step][0], *[wait(array) for array in mine_got[step]])))

    outs = []

    def put(step):
        pair = (dp // 2 - step) % n_ring
        where = jnp.stack([2 * pair + dp % 2, 2 * pair + 1 - dp % 2]).astype(jnp.int32) + token
        return place(outs, n_dp * out_weight.shape[1], where, mine[step], other[step])

    columns(0)
    for step in range(3, n_ring):
        turn(upper, step)
    rest[1] = wait(rest[1])
    send(0)
    columns(1)
    send(1)
    for step in range(2, n_ring, 2):
        rest[1 + step // 2] = wait(rest[1 + step // 2])
        if step > 2:
            turn(beside, step)
        flip = after(turned)
        turn(beside, step + 1)
        columns(step, flip)
        send(step)
        stay(step - 2)
        stay(step - 1)
        columns(step + 1)
        send(step + 1)
    stay(n_ring - 2)
    stay(n_ring - 1)
    for step in range(n_ring - 1):
        outs = [wait(out) for out in put(step)]
    other[-1] = wait(other[-1])
    return tuple(put(n_ring - 1))


def solution(mesh):
    rows = P(("dp", "seq"), None)
    return jax.shard_map(
        functools.partial(body, mesh.shape["dp"], mesh.shape["seq"]),
        mesh=mesh,
        in_specs=(rows,) * 6 + (P(), P(), P("seq", "dp")),
        out_specs=(rows, rows),
        check_vma=False,
    )
```

```python
import functools

import jax
import jax.numpy as jnp
from jax import lax
from jax.experimental import pallas as pl
from jax.experimental.pallas import tpu as pltpu
from jax.sharding import PartitionSpec as P

HEADS = 20
EPS = 1e-06
VMEM_BYTES = 10 * 1024 * 1024
ROW_STEP = 32

LOW = jnp.bfloat16
WIDE = jnp.float32
LIGHT = pl.CostEstimate(flops=1, transcendentals=0, bytes_accessed=1)


def params():
    return pltpu.CompilerParams(vmem_limit_bytes=VMEM_BYTES)


def vmem_specs(count):
    return [pl.BlockSpec(memory_space=pltpu.VMEM)] * count


def pack_kernel(n_seq, chunks, core_ref, *refs):
    query_ref, key_ref, value_ref, dquery_ref, dkey_ref, dvalue_ref, gains_ref = refs[:7]
    out_refs = refs[7:]
    n_chunks = len(chunks)
    group = query_ref.shape[-1] // n_seq

    def statistics(primal_ref, tangent_ref):
        primal = primal_ref[...].astype(WIDE)
        tangent = tangent_ref[...].astype(WIDE)
        inverse = lax.rsqrt(jnp.mean(primal * primal, axis=-1, keepdims=True) + EPS)
        across = jnp.mean(primal * tangent, axis=-1, keepdims=True)
        return inverse, inverse * inverse * inverse * across

    query_stats = statistics(query_ref, dquery_ref)
    key_stats = statistics(key_ref, dkey_ref)

    def normed(primal_ref, tangent_ref, which, stats, lanes):
        primal = primal_ref[:, lanes].astype(WIDE)
        tangent = tangent_ref[:, lanes].astype(WIDE)
        gain = gains_ref[which : which + 1, lanes]
        inverse, slope = stats
        return (primal * inverse * gain).astype(LOW), (gain * (tangent * inverse - primal * slope)).astype(LOW)

    for side in range(2):
        core = core_ref[0] if side == 0 else 1 - core_ref[0]
        queries_ref, *keyed_refs = out_refs[side * (1 + n_chunks) : (side + 1) * (1 + n_chunks)]
        for at in range(n_seq // 2):
            lanes = pl.ds(pl.multiple_of((2 * at + core) * group, 128), group)
            here = slice(at * group, (at + 1) * group)
            plain, dual = normed(query_ref, dquery_ref, 0, query_stats, lanes)
            queries_ref[0, :, here] = plain
            queries_ref[1, :, here] = dual
            four = normed(key_ref, dkey_ref, 1, key_stats, lanes)
            four += (value_ref[:, lanes], dvalue_ref[:, lanes])
            start = 0
            for keyed_ref, width in zip(keyed_refs, chunks):
                low, high = max(start, here.start), min(start + width, here.stop)
                if low < high:
                    for which, part in enumerate(four):
                        keyed_ref[which, :, low - start : high - start] = part[:, low - here.start : high - here.start]
                start += width


def pack(core, n_seq, chunks, arrays, gains):
    rows, features = arrays[0].shape
    step = min(rows, ROW_STEP)
    row_block = pl.BlockSpec((step, features), lambda i, c: (i, 0))
    gain_block = pl.BlockSpec((2, features), lambda i, c: (0, 0))
    kinds = [(2, features // 2)] + [(4, width) for width in chunks]
    kinds = kinds + kinds
    return pl.pallas_call(
        functools.partial(pack_kernel, n_seq, chunks),
        grid_spec=pltpu.PrefetchScalarGridSpec(
            num_scalar_prefetch=1,
            grid=(rows // step,),
            in_specs=[row_block] * 6 + [gain_block],
            out_specs=[pl.BlockSpec((count, step, width), lambda i, c: (0, i, 0)) for count, width in kinds],
        ),
        out_shape=[jax.ShapeDtypeStruct((count, rows, width), LOW) for count, width in kinds],
        compiler_params=params(),
        cost_estimate=LIGHT,
    )(core, *arrays, gains)


def attend_kernel(n_queries, *refs):
    query_refs, keyed_refs, out_ref = refs[:n_queries], refs[n_queries:-1], refs[-1]

    def stack(which, some_refs, kinds):
        parts = [ref[at] for ref in some_refs for at in range(which, ref.shape[0], kinds)]
        return jnp.concatenate(parts, axis=0)

    query, query_dual = (stack(which, query_refs, 2) for which in range(2))
    key, key_dual, value, value_dual = (stack(which, keyed_refs, 4) for which in range(4))
    factor = query.shape[-1] ** (-0.5)
    last = (((1,), (1,)), ((), ()))
    scores = lax.dot_general(query, key, last, preferred_element_type=WIDE) * factor
    dual_scores = (
        lax.dot_general(
            jnp.concatenate([query_dual, query], axis=1),
            jnp.concatenate([key, key_dual], axis=1),
            last,
            preferred_element_type=WIDE,
        )
        * factor
    )
    raised = jnp.exp(scores - jnp.max(scores, axis=-1, keepdims=True))
    probs = raised * (1.0 / jnp.sum(raised, axis=-1, keepdims=True))
    spread = probs * (dual_scores - jnp.sum(probs * dual_scores, axis=-1, keepdims=True))
    probs_low = probs.astype(LOW)
    spread_low = spread.astype(LOW)
    out_ref[0] = jnp.dot(probs_low, value, preferred_element_type=WIDE).astype(LOW)
    out_ref[1] = (
        jnp.dot(probs_low, value_dual, preferred_element_type=WIDE)
        + jnp.dot(spread_low, value, preferred_element_type=WIDE)
    ).astype(LOW)


def attend(start, hdim, queries, keyed):
    rows = queries[0].shape[1]
    width = keyed[0].shape[2]
    first = start // hdim
    return pl.pallas_call(
        functools.partial(attend_kernel, len(queries)),
        grid=(width // hdim,),
        in_specs=[pl.BlockSpec((2, rows, hdim), lambda h: (0, 0, first + h))] * len(queries)
        + [pl.BlockSpec((array.shape[0], rows, hdim), lambda h: (0, 0, h)) for array in keyed],
        out_specs=pl.BlockSpec((2, len(queries) * rows, hdim), lambda h: (0, 0, h)),
        out_shape=jax.ShapeDtypeStruct((2, len(queries) * rows, width), LOW),
        compiler_params=params(),
        cost_estimate=LIGHT,
    )(*queries, *keyed)


def project_kernel(n_chunks, spans, flip_ref, *refs):
    sides = refs[:n_chunks], refs[n_chunks : 2 * n_chunks]
    weight_refs, out_refs, weight_ref = refs[2 * n_chunks : -6], refs[-6:-1], refs[-1]
    rows = out_refs[0].shape[0] // 2
    depth = weight_ref.shape[0] // 2
    at = 0
    for ref, (low, high) in zip(weight_refs, spans):
        block, inside = at // depth, at % depth
        first = pl.multiple_of((block ^ flip_ref[0]) * depth + inside, 16)
        weight_ref[pl.ds(first, high - low)] = ref[low:high]
        at += high - low
    weight = weight_ref[...]
    for side, parts in enumerate(sides):
        acts = jnp.concatenate([ref[...].reshape(4 * rows, ref.shape[-1]) for ref in parts], axis=1)
        total = jnp.dot(acts, weight, preferred_element_type=WIDE)
        for kind in range(2):
            first = 2 * kind * rows
            here = slice(kind * rows, (kind + 1) * rows)
            out_refs[side][here] = total[first : first + rows]
            low = total[first + rows : first + 2 * rows].astype(LOW)
            if side:
                out_refs[3 + kind][...] = low
            else:
                out_refs[2][here] = low


def project(flip, acts, pieces):
    mine, theirs = zip(*acts)
    weights = [weight for weight, _, _ in pieces]
    spans = [(low, high) for _, low, high in pieces]
    rows, n = mine[0].shape[1], weights[0].shape[1]
    depth = sum(high - low for low, high in spans)
    return pl.pallas_call(
        functools.partial(project_kernel, len(acts), spans),
        in_specs=[pl.BlockSpec(memory_space=pltpu.SMEM)] + vmem_specs(2 * len(acts) + len(weights)),
        out_specs=vmem_specs(5),
        out_shape=[jax.ShapeDtypeStruct((rows, n), WIDE)] * 2
        + [jax.ShapeDtypeStruct((rows, n), LOW)]
        + [jax.ShapeDtypeStruct((rows // 2, n), LOW)] * 2,
        scratch_shapes=[pltpu.VMEM((depth, n), LOW)],
        compiler_params=params(),
        cost_estimate=LIGHT,
    )(flip, *mine, *theirs, *weights)


def close_kernel(keep_ref, *refs):
    got_refs, out_ref = refs[:-1], refs[-1]
    first = 0
    for got_ref in got_refs:
        here = slice(first, first + got_ref.shape[0])
        out_ref[here] = (keep_ref[here] + got_ref[...].astype(WIDE)).astype(LOW)
        first = here.stop


def close(keep, *gots):
    return pl.pallas_call(
        close_kernel,
        in_specs=vmem_specs(1 + len(gots)),
        out_specs=vmem_specs(1)[0],
        out_shape=jax.ShapeDtypeStruct(keep.shape, LOW),
        compiler_params=params(),
        cost_estimate=LIGHT,
    )(keep, *gots)


def place_kernel(where_ref, mine_ref, other_ref, *refs):
    plain_ref, dual_ref = refs[-2:]
    rows = plain_ref.shape[0]

    @pl.when(pl.program_id(0) == 0)
    def _():
        plain_ref[...] = mine_ref[:rows]
        dual_ref[...] = mine_ref[rows:]

    @pl.when(pl.program_id(0) == 1)
    def _():
        plain_ref[...] = other_ref[:rows]
        dual_ref[...] = other_ref[rows:]


def place(outs, width, where, mine, other):
    rows, n = other.shape[0] // 2, other.shape[1]
    if n % 128:
        outs = outs or [jnp.zeros((rows, width), LOW)] * 2
        for side, piece in enumerate((mine, other)):
            parts = (piece[:rows], piece[rows:])
            outs = [lax.dynamic_update_slice(out, part, (0, where[side] * n)) for out, part in zip(outs, parts)]
        return outs
    full = pl.BlockSpec((2 * rows, n), lambda i, w: (0, 0))
    block = pl.BlockSpec((rows, n), lambda i, w: (0, w[i]))
    return pl.pallas_call(
        place_kernel,
        grid_spec=pltpu.PrefetchScalarGridSpec(
            num_scalar_prefetch=1,
            grid=(2,),
            in_specs=[full] * 2 + [pl.BlockSpec(memory_space=pl.ANY)] * len(outs),
            out_specs=[block] * 2,
        ),
        out_shape=[jax.ShapeDtypeStruct((rows, width), LOW)] * 2,
        input_output_aliases={3 + at: at for at in range(len(outs))},
        compiler_params=params(),
        cost_estimate=LIGHT,
    )(where, mine, other, *outs)


def body(
    n_dp,
    n_seq,
    queries,
    key_states,
    value_states,
    query_tangent,
    key_tangent,
    value_tangent,
    query_gain,
    key_gain,
    out_weight,
):
    dp = lax.axis_index("dp")
    seq = lax.axis_index("seq")
    n_ring = n_dp // 2
    groups = n_seq // 2
    features = queries.shape[1]
    hdim = features // HEADS
    group_heads = HEADS // n_seq
    few = group_heads * 2 // 5
    chunks = [group_heads * hdim] * (groups - 1) + [(group_heads - few) * hdim, few * hdim]
    starts = [sum(chunks[:at]) for at in range(len(chunks))]
    token = jnp.zeros((1,), jnp.int32)

    def far(array):
        return lax.ppermute(array, "seq", [(i, i ^ 2) for i in range(n_seq)])

    def near(array):
        return lax.ppermute(array, "seq", [(i, i ^ 1) for i in range(n_seq)])

    def across(array):
        return lax.ppermute(array, "dp", [(i, i ^ 1) for i in range(n_dp)])

    def onward(array):
        return lax.ppermute(array, "dp", [(i, (i + 2) % n_dp) for i in range(n_dp)])

    def wait(array):
        nonlocal token
        array, token = lax.optimization_barrier((array, token))
        return array

    def after(array):
        return lax.optimization_barrier((array, token))[0]

    def turn(ring, step):
        ring[step] = wait(ring[step])
        if step + 1 < n_ring:
            ring.append(onward(ring[step]))

    depth = out_weight.shape[0]
    cut = depth * 13 // 20 // 16 * 16
    upper, lower = [out_weight[:cut]], [out_weight[cut:]]
    lower.append(onward(lower[0]))
    upper.append(onward(upper[0]))
    beside = [wait(far(upper[0]))]
    beside.append(onward(beside[0]))
    turn(lower, 1)

    core = jnp.stack([seq % 2])
    arrays = (queries, key_states, value_states, query_tangent, key_tangent, value_tangent)
    packs = [wait(array) for array in pack(core, n_seq, chunks, arrays, jnp.stack([query_gain, key_gain]))]
    query_own, *keyed_own = packs[: 1 + len(chunks)]
    query_other, *keyed_other = packs[1 + len(chunks) :]
    there = wait(near(keyed_other[0]))
    keyed = [[keyed_own[0], there, far(keyed_own[0]), far(there)]]
    for own, other in zip(keyed_own[1:], keyed_other[1:]):
        there = wait(near(other))
        keyed.append([own, there, far(jnp.concatenate([own, there]))])
    queries_both = [query_own, wait(near(query_other))]
    turn(lower, 2)

    acts, swapped = [], []

    def attention(chunk):
        keyed[chunk][-1] = wait(keyed[chunk][-1])
        acts.append(wait(attend(starts[chunk], hdim, queries_both, keyed[chunk])))
        swapped.append(across(acts[-1]))

    turn(upper, 1)
    keyed[0][2] = wait(keyed[0][2])
    turn(beside, 1)
    attention(0)
    for step in range(3, n_ring):
        turn(lower, step)
    later = [wait(jnp.concatenate(lower[step : step + 2])) for step in range(2, n_ring, 2)]
    turn(upper, 2)
    rest = [far(after(lower[0]))]
    attention(1)
    swapped[0] = wait(swapped[0])
    attention(2)
    swapped[1] = wait(swapped[1])
    turn(beside, 2)
    rest += [far(after(piece)) for piece in lower[1:2] + later]
    rest[0] = wait(rest[0])
    swapped[2] = wait(swapped[2])
    acts = list(zip(acts, swapped))
    turned = jnp.stack([seq // 2])

    keeps, sends, mine_got, mine, other = [], [], [], [], []

    def columns(step, flip=None):
        own = [(upper[step], 0, cut), (lower[step], 0, depth - cut)] if step else [(out_weight, 0, depth)]
        start = step % 2 * (depth - cut) if step > 1 else 0
        got = rest[step] if step < 2 else rest[1 + step // 2]
        theirs = [(beside[step], 0, cut), (got, start, start + depth - cut)]
        keep_mine, keep_other, *low = project(after(turned) if flip is None else flip, acts, own + theirs)
        keeps.append((keep_mine, keep_other))
        sends.append([near(wait(array)) for array in low[1:]])
        mine_got.append([wait(array) for array in low[:1]])

    def send(step):
        closed = wait(close(keeps[step][1], *[wait(array) for array in sends[step]]))
        if step > 2:
            other[step - 1] = wait(other[step - 1])
        other.append(across(after(closed)))
        mine_got[step] = [near(after(array)) for array in mine_got[step]]
        if step and not step > 2:
            other[step - 1] = wait(other[step - 1])

    def stay(step):
        mine.append(wait(close(keeps[step][0], *[wait(array) for array in mine_got[step]])))

    outs = []

    def put(step):
        pair = (dp // 2 - step) % n_ring
        where = jnp.stack([2 * pair + dp % 2, 2 * pair + 1 - dp % 2]).astype(jnp.int32) + token
        return place(outs, n_dp * out_weight.shape[1], where, mine[step], other[step])

    columns(0)
    for step in range(3, n_ring):
        turn(upper, step)
    rest[1] = wait(rest[1])
    send(0)
    columns(1)
    send(1)
    for step in range(2, n_ring, 2):
        rest[1 + step // 2] = wait(rest[1 + step // 2])
        if step > 2:
            turn(beside, step)
        flip = after(turned)
        turn(beside, step + 1)
        columns(step, flip)
        send(step)
        stay(step - 2)
        stay(step - 1)
        columns(step + 1)
        send(step + 1)
    stay(n_ring - 2)
    stay(n_ring - 1)
    for step in range(n_ring - 1):
        outs = [wait(out) for out in put(step)]
    other[-1] = wait(other[-1])
    return tuple(put(n_ring - 1))


def solution(mesh):
    rows = P(("dp", "seq"), None)
    return jax.shard_map(
        functools.partial(body, mesh.shape["dp"], mesh.shape["seq"]),
        mesh=mesh,
        in_specs=(rows,) * 6 + (P(), P(), P("seq", "dp")),
        out_specs=(rows, rows),
        check_vma=False,
    )
```
